32 devices in a mesh: dp: 8 (over z, x), mp: 4 (over y, core).
Axes of the slice: x: 2, y: 2, z: 4, core: 2. Of those that a mesh axis runs over, the one named last changes fastest.
Arguments:
- tokens: bfloat16 [8, 512, 2048], P('dp', 'mp'), may hold values from -6 to 6
- norm_gains: float32 [3, 2048], replicated, may hold values from 0.25 to 1.75
- w_query: bfloat16 [2048, 2048], P(None, 'mp'), may hold values from -0.125 to 0.125
- w_key: bfloat16 [2048, 2048], P(None, 'mp'), may hold values from -0.125 to 0.125
- w_value: bfloat16 [2048, 2048], P(None, 'mp'), may hold values from -0.125 to 0.125
- w_out: bfloat16 [2048, 2048], P('mp'), may hold values from -0.75 to 0.75
- c_query: bfloat16 [2048, 2048], P(None, 'mp'), may hold values from -0.125 to 0.125
- c_key: bfloat16 [2048, 2048], P(None, 'mp'), may hold values from -0.125 to 0.125
- c_value: bfloat16 [2048, 2048], P(None, 'mp'), may hold values from -0.125 to 0.125
- c_out: bfloat16 [2048, 2048], P('mp'), may hold values from -1.5 to 1.5
- patch_proj: bfloat16 [1664, 2048], replicated, may hold values from -0.15625 to 0.15625
- w_gate: bfloat16 [2048, 5120], P(None, 'mp'), may hold values from -0.125 to 0.125
- w_up: bfloat16 [2048, 5120], P(None, 'mp'), may hold values from -0.125 to 0.125
- w_down: bfloat16 [5120, 2048], P('mp'), may hold values from -0.078125 to 0.078125
- patches: bfloat16 [32, 256, 1664], P('dp'), may hold values from -6 to 6
- segment_ids: int32 [8, 512], P('dp'), may hold values from 0 to 3, as said below
- image_index: int32 [8, 4], P('dp'), may hold values from 0 to 3
- cotangent: bfloat16 [8, 512, 2048], P('dp', 'mp'), may hold values from -6 to 6
Outputs:
- output: bfloat16 [8, 512, 2048], P('dp', 'mp')
- tokens_grad: float32 [8, 512, 2048], P('dp', 'mp')
- norm_gains_grad: float32 [3, 2048], P(None, ('dp', 'mp'))
- w_query_grad: float32 [2048, 2048], P('dp', 'mp')
- w_key_grad: float32 [2048, 2048], P('dp', 'mp')
- w_value_grad: float32 [2048, 2048], P('dp', 'mp')
- w_out_grad: float32 [2048, 2048], P('mp', 'dp')
- c_query_grad: float32 [2048, 2048], P('dp', 'mp')
- c_key_grad: float32 [2048, 2048], P('dp', 'mp')
- c_value_grad: float32 [2048, 2048], P('dp', 'mp')
- c_out_grad: float32 [2048, 2048], P('mp', 'dp')
- patch_proj_grad: float32 [1664, 2048], P(None, ('dp', 'mp'))
- w_gate_grad: float32 [2048, 5120], P('dp', 'mp')
- w_up_grad: float32 [2048, 5120], P('dp', 'mp')
- w_down_grad: float32 [5120, 2048], P('mp', 'dp')
The draws below stay inside these ranges and needn't reach their ends.
Inputs may be any that keep to these rules, and one draw needn't show every extreme that they name: `segment_ids`: within each packed row the ids run from 0 to 3 without falling, and every id is present. `image_index`: rows held at index g of dp read the images g * 4 to g * 4 + 3.
All inputs are finite; a program needn't handle non-finite values.
Results may differ from the reference program's by a relative error of at most 0.033.
Values may be sent and summed in bfloat16 or wider, within the bound.
A program may use at most 256 MiB of HBM per device.

```python
import jax
import jax.numpy as jnp
from jax import lax

D = 2048
HEADS = 16
HEAD_DIM = 128
FF = 5120
VIT = 1664
PATCHES = 256
SEQ = 512
SEGS = 4
IMG_DEV = 4
ROWS_DEV = 1
ROWS = 8
IMAGES = 32
N_DP = 8


def draw_segment_ids(key, part):
    key = jax.random.fold_in(key, 7)
    first_key, second_key = jax.random.split(key)
    long_index = jax.random.randint(first_key, (ROWS, 1), 0, SEGS)
    short_len = jax.random.randint(second_key, (ROWS, SEGS), 1, SEQ // (4 * SEGS) + 1)
    slot_ids = jnp.arange(SEGS)[None, :]
    short_len = jnp.where(slot_ids == long_index, 0, short_len)
    lengths = jnp.where(slot_ids == long_index, SEQ - jnp.sum(short_len, axis=1, keepdims=True), short_len)
    seg_ends = jnp.cumsum(lengths, axis=1)
    positions = jnp.arange(SEQ)
    return jnp.sum((positions[None, :, None] >= seg_ends[:, None, :]).astype(jnp.int32), axis=-1).astype(jnp.int32)


def set_ends(entries, stream_key, smallest, top_value):
    shape = entries.shape
    index_at = [jax.random.randint(jax.random.fold_in(stream_key, axis), (), 0, shape[axis]) for axis in range(len(shape))]
    entries = entries.at[tuple(index_at)].set(smallest)
    longest = shape.index(max(shape))
    index_at[longest] = (index_at[longest] + 1) % shape[longest]
    return entries.at[tuple(index_at)].set(top_value)


def raised(array, rng, source, target, parts, factor):
    owner, partner = [(jnp.arange(array.shape[position]) // (array.shape[position] // parts)).reshape([-1 if axis == position else 1 for axis in range(array.ndim)]) for position in (source, target)]
    chosen = jax.random.permutation(rng, parts)[partner]
    strong = (owner == chosen) | (owner == (partner + parts // 2) % parts)
    return jnp.where(strong, factor * array, array)


def level_of(own_key, shape, cuts, least, largest):
    factor_of = 1.0
    for dim, shards_of in cuts:
        heights = jax.random.uniform(jax.random.fold_in(jax.random.fold_in(own_key, 6), dim), (shards_of,), jnp.float32, least / len(cuts), largest / len(cuts))
        factor_of = factor_of * jnp.repeat(jnp.exp(heights), shape[dim] // shards_of).reshape((-1,) + (1,) * (len(shape) - 1 - dim))
    return factor_of


def gaussian(stream_key, extent, scale, reach, cuts=(), kind=jnp.bfloat16):
    values = scale * jax.random.normal(stream_key, extent, jnp.float32)
    if cuts:
        values = values * level_of(stream_key, extent, cuts, -0.22, 0.18)
    return jnp.clip(values, -reach, reach).astype(kind)


def bell_draw_with(rng, extent, deviation, limit, shards, heavy, held_as=jnp.bfloat16):
    values = deviation * jax.random.normal(rng, extent, jnp.float32)
    if shards:
        values = values * level_of(rng, extent, shards, -0.22, 0.18)
    return jnp.clip(raised(values, jax.random.fold_in(rng, 3), *heavy), -limit, limit).astype(held_as)


def setup_inputs(seed: int = 0) -> dict:
    keys = jax.random.split(jax.random.key(seed), 19)
    tokens = bell_draw_with(keys[0], (ROWS, SEQ, D), 1.0, 6.0, ((0, 8), (1, 4)), (0, 2, 8, 2.0))
    norm_gains = jnp.clip(1.0 + 0.15 * jax.random.normal(keys[1], (3, D), jnp.float32), 0.25, 1.75)
    w_query = gaussian(keys[2], (D, D), D ** -0.5, 0.125, ((1, 4),))
    w_key = gaussian(keys[3], (D, D), D ** -0.5, 0.125, ((1, 4),))
    w_value = gaussian(keys[4], (D, D), D ** -0.5, 0.125, ((1, 4),))
    w_out = gaussian(keys[5], (D, D), (D // 32) ** -0.5, 0.75, ((0, 4),))
    c_query = gaussian(keys[6], (D, D), D ** -0.5, 0.125, ((1, 4),))
    c_key = gaussian(keys[7], (D, D), D ** -0.5, 0.125, ((1, 4),))
    c_value = gaussian(keys[8], (D, D), D ** -0.5, 0.125, ((1, 4),))
    c_out = gaussian(keys[9], (D, D), (D // 128) ** -0.5, 1.5, ((0, 4),))
    patch_proj = gaussian(keys[10], (VIT, D), VIT ** -0.5, 0.15625)
    w_gate = gaussian(keys[11], (D, FF), D ** -0.5, 0.125, ((1, 4),))
    w_up = gaussian(keys[12], (D, FF), D ** -0.5, 0.125, ((1, 4),))
    w_down = gaussian(keys[13], (FF, D), FF ** -0.5, 0.078125, ((0, 4),))
    patches = gaussian(keys[14], (IMAGES, PATCHES, VIT), 1.0, 6.0, ((0, 8),))
    segment_ids = draw_segment_ids(jax.random.fold_in(keys[18], 71), 0)
    image_index = set_ends(jax.random.randint(keys[16], (ROWS, SEGS), 0, IMG_DEV), jax.random.fold_in(keys[16], 1), 0, IMG_DEV - 1).astype(jnp.int32)
    cotangent = bell_draw_with(keys[17], (ROWS, SEQ, D), 1.0, 6.0, ((0, 8), (1, 4)), (0, 2, 8, 2.0))
    return dict(tokens=tokens, norm_gains=norm_gains, w_query=w_query, w_key=w_key, w_value=w_value, w_out=w_out, c_query=c_query, c_key=c_key, c_value=c_value, c_out=c_out, patch_proj=patch_proj, w_gate=w_gate, w_up=w_up, w_down=w_down, patches=patches, segment_ids=segment_ids, image_index=image_index, cotangent=cotangent)


EPSILON = 1e-06
HIGH = lax.Precision.HIGHEST

@jax.custom_vjp
def low(v):
    return lax.optimization_barrier(v.astype(jnp.bfloat16)).astype(jnp.float32)

@jax.custom_vjp
def low_back(v):
    return v

def low_keep(v):
    return (low(v), None)

def low_pass(kept, grad):
    return (grad,)

def back_keep(v):
    return (v, None)

def back_low(kept, grad):
    return (low(grad),)
low.defvjp(low_keep, low_pass)
low_back.defvjp(back_keep, back_low)

def both_ways(value):
    return low_back(low(value))

def product(left, right):
    return jnp.einsum('...d,de->...e', left, right, precision=HIGH)

def rms_norm(rows_in, gain):
    return rows_in * lax.rsqrt(lax.optimization_barrier(jnp.mean(rows_in * rows_in, axis=-1, keepdims=True)) + EPSILON) * gain

def attend(queries, key_rows, value_rows, allowed):
    score_scale = HEAD_DIM ** (-0.5)
    scores = jnp.einsum('shd,thd->hst', queries, key_rows, precision=HIGH) * score_scale
    scores = low_back(jnp.where(allowed[None], scores, -1000000000.0))
    weights = jax.nn.softmax(scores, axis=-1)
    return jnp.einsum('hst,thd->shd', low(weights), value_rows, precision=HIGH)

def forward(tokens, norm_gains, w_query, w_key, w_value, w_out, c_query, c_key, c_value, c_out, patch_proj, w_gate, w_up, w_down, patches, segment_ids, token_image):
    rows_all = tokens.shape[0]
    length = tokens.shape[1]

    def heads_view(arr):
        return arr.reshape(arr.shape[:-1] + (HEADS, HEAD_DIM))

    def flat_view(arr):
        return arr.reshape(rows_all, length, HEADS * HEAD_DIM)
    positions = jnp.arange(length, dtype=jnp.int32)

    def self_row(row_parts):
        queries_row, keys_row, values_row, segment_row = row_parts
        allowed = (segment_row[:, None] == segment_row[None, :]) & (positions[None, :] <= positions[:, None])
        return attend(queries_row, keys_row, values_row, allowed)
    normed = low(rms_norm(tokens, norm_gains[0]))
    queries = both_ways(product(normed, w_query))
    key_rows = both_ways(product(normed, w_key))
    value_rows = both_ways(product(normed, w_value))
    self_mixed = lax.map(jax.checkpoint(self_row), (heads_view(queries), heads_view(key_rows), heads_view(value_rows), segment_ids))
    self_mixed = both_ways(flat_view(self_mixed))
    after_self = tokens + low_back(product(self_mixed, w_out))
    normed = low(rms_norm(after_self, norm_gains[1]))
    cross_queries = both_ways(product(normed, c_query))
    projected = both_ways(product(patches, patch_proj))
    cross_keys = both_ways(product(projected, c_key)).reshape(N_DP, IMG_DEV * PATCHES, HEADS, HEAD_DIM)
    cross_values = both_ways(product(projected, c_value)).reshape(N_DP, IMG_DEV * PATCHES, HEADS, HEAD_DIM)
    patch_image = jnp.arange(IMG_DEV * PATCHES, dtype=jnp.int32) // PATCHES
    group_index = jnp.arange(rows_all, dtype=jnp.int32) // ROWS_DEV

    def cross_row(row_parts):
        queries_row, image_row, group_row = row_parts
        keys_here = lax.dynamic_index_in_dim(cross_keys, group_row, 0, keepdims=False)
        values_here = lax.dynamic_index_in_dim(cross_values, group_row, 0, keepdims=False)
        allowed = image_row[:, None] == patch_image[None, :]
        return attend(queries_row, keys_here, values_here, allowed)
    cross_mixed = lax.map(jax.checkpoint(cross_row), (heads_view(cross_queries), token_image, group_index))
    cross_mixed = both_ways(flat_view(cross_mixed))
    after_cross = after_self + low_back(product(cross_mixed, c_out))
    normed = low(rms_norm(after_cross, norm_gains[2]))
    gate_pre = low_back(product(normed, w_gate))
    up_pre = low_back(product(normed, w_up))
    hidden = low(jax.nn.gelu(gate_pre, approximate=True) * up_pre)
    return after_cross + low_back(product(hidden, w_down))

def reference(tokens, norm_gains, w_query, w_key, w_value, w_out, c_query, c_key, c_value, c_out, patch_proj, w_gate, w_up, w_down, patches, segment_ids, image_index, cotangent):
    seg_slots = jnp.arange(SEGS, dtype=jnp.int32)
    token_image = lax.optimization_barrier(jnp.sum(jnp.where(segment_ids[:, :, None] == seg_slots, image_index[:, None, :], 0), axis=-1)).astype(jnp.int32)
    patches_wide = patches.astype(jnp.float32)

    def run_layer(tokens_wide, gains_wide, *matrices):
        return forward(tokens_wide, gains_wide, *matrices, patches_wide, segment_ids, token_image)
    matrices = [m.astype(jnp.float32) for m in (w_query, w_key, w_value, w_out, c_query, c_key, c_value, c_out, patch_proj, w_gate, w_up, w_down)]
    result, pullback = jax.vjp(run_layer, tokens.astype(jnp.float32), norm_gains, *matrices)
    grads = pullback(cotangent.astype(jnp.float32))
    return (result.astype(jnp.bfloat16), grads[0], grads[1], grads[2], grads[3], grads[4], grads[5], grads[6], grads[7], grads[8], grads[9], grads[10], grads[11], grads[12], grads[13])
```

```python
import jax
import jax.numpy as jnp
from jax import lax
from jax.sharding import PartitionSpec as P

HEAD_DIM = 128
SEGS = 4


EPSILON = 1e-06


def rms_norm(rows_in, gain):
    return rows_in * lax.rsqrt(jnp.mean(rows_in * rows_in, axis=-1, keepdims=True) + EPSILON) * gain


def matmul(left, right):
    return jnp.dot(left, right, preferred_element_type=jnp.float32)


def attend_block(queries, key_rows, value_rows, allowed):
    score_scale = queries.shape[-1] ** (-0.5)
    scores = (
        jnp.einsum("shd,thd->hst", queries, key_rows, preferred_element_type=jnp.float32)
        * score_scale
    )
    scores = jnp.where(allowed[None], scores, -1000000000.0)
    row_max = jnp.max(scores, axis=-1, keepdims=True)
    exponent = jnp.exp(scores - row_max)
    row_total = jnp.sum(exponent, axis=-1, keepdims=True)
    weights = (exponent / row_total).astype(jnp.bfloat16)
    attended = jnp.einsum("hst,thd->shd", weights, value_rows, preferred_element_type=jnp.float32)
    return (attended.astype(jnp.bfloat16), (row_max + jnp.log(row_total))[..., 0])


def attend_back(queries, key_rows, value_rows, allowed, log_total, grad_out):
    score_scale = queries.shape[-1] ** (-0.5)
    scores = (
        jnp.einsum("shd,thd->hst", queries, key_rows, preferred_element_type=jnp.float32)
        * score_scale
    )
    scores = jnp.where(allowed[None], scores, -1000000000.0)
    weights = jnp.exp(scores - log_total[..., None])
    grad_weights = jnp.einsum(
        "shd,thd->hst", grad_out, value_rows, preferred_element_type=jnp.float32
    )
    inner_sum = jnp.sum(weights * grad_weights, axis=-1, keepdims=True)
    grad_scores = (weights * (grad_weights - inner_sum)).astype(jnp.bfloat16)
    grad_query = (
        jnp.einsum("hst,thd->shd", grad_scores, key_rows, preferred_element_type=jnp.float32)
        * score_scale
    )
    grad_key = (
        jnp.einsum("hst,shd->thd", grad_scores, queries, preferred_element_type=jnp.float32)
        * score_scale
    )
    grad_value = jnp.einsum(
        "hst,shd->thd", weights.astype(jnp.bfloat16), grad_out, preferred_element_type=jnp.float32
    )
    return (grad_query, grad_key, grad_value)


def gated_unit(gate_arg, up_arg):
    return jax.nn.gelu(gate_arg, approximate=True) * up_arg


def shards(
    tokens,
    norm_gains,
    w_query,
    w_key,
    w_value,
    w_out,
    c_query,
    c_key,
    c_value,
    c_out,
    patch_proj,
    w_gate,
    w_up,
    w_down,
    patches,
    segment_ids,
    image_index,
    cotangent,
):
    rows_here = segment_ids.shape[0]
    length = segment_ids.shape[1]
    local_heads = w_query.shape[1] // HEAD_DIM
    patch_rows = patches.shape[0] * patches.shape[1]
    positions = jnp.arange(length, dtype=jnp.int32)
    causal = positions[None, :] <= positions[:, None]
    seg_slots = jnp.arange(SEGS, dtype=jnp.int32)
    token_image = jnp.sum(
        jnp.where(segment_ids[:, :, None] == seg_slots, image_index[:, None, :], 0), axis=-1
    )
    patch_image = jnp.arange(patch_rows, dtype=jnp.int32) // patches.shape[1]

    def heads_view(arr):
        return arr.reshape(arr.shape[:-1] + (local_heads, HEAD_DIM))

    def flat_rows(arr):
        return arr.reshape(rows_here, length, local_heads * HEAD_DIM)

    def widen_rows(local_rows):
        return lax.all_gather(local_rows, "mp", axis=1, tiled=True)

    def narrow(partial_sum):
        return lax.psum_scatter(
            partial_sum.astype(jnp.bfloat16), "mp", scatter_dimension=1, tiled=True
        ).astype(jnp.float32)

    def gather_grad(grad_local):
        return lax.all_gather(grad_local.astype(jnp.bfloat16), "mp", axis=1, tiled=True)

    def sum_grad(partial_sum):
        return lax.psum_scatter(
            partial_sum.astype(jnp.bfloat16), "mp", scatter_dimension=1, tiled=True
        ).astype(jnp.float32)

    def self_allowed(segment_row):
        return (segment_row[:, None] == segment_row[None, :]) & causal

    def self_forward(row_parts):
        queries_row, keys_row, values_row, segment_row = row_parts
        return attend_block(queries_row, keys_row, values_row, self_allowed(segment_row))

    def self_backward(row_parts):
        queries_row, keys_row, values_row, segment_row, log_row, grad_row = row_parts
        return attend_back(
            queries_row, keys_row, values_row, self_allowed(segment_row), log_row, grad_row
        )

    residual = tokens.astype(jnp.float32)
    normed_one_local = rms_norm(residual, norm_gains[0]).astype(jnp.bfloat16)
    normed_one = widen_rows(normed_one_local)
    queries = matmul(normed_one, w_query).astype(jnp.bfloat16)
    key_rows = matmul(normed_one, w_key).astype(jnp.bfloat16)
    value_rows = matmul(normed_one, w_value).astype(jnp.bfloat16)
    self_mixed, self_log = lax.map(
        self_forward,
        (heads_view(queries), heads_view(key_rows), heads_view(value_rows), segment_ids),
    )
    self_mixed = flat_rows(self_mixed)
    after_self = residual + narrow(matmul(self_mixed, w_out))
    normed_two_local = rms_norm(after_self, norm_gains[1]).astype(jnp.bfloat16)
    normed_two = widen_rows(normed_two_local)
    cross_queries = matmul(normed_two, c_query).astype(jnp.bfloat16)
    patch_flat = patches.reshape(patch_rows, patches.shape[2])
    projected = matmul(patch_flat, patch_proj).astype(jnp.bfloat16)
    cross_keys = matmul(projected, c_key).astype(jnp.bfloat16)
    cross_values = matmul(projected, c_value).astype(jnp.bfloat16)

    def cross_allowed(image_row):
        return image_row[:, None] == patch_image[None, :]

    def cross_forward(row_parts):
        queries_row, image_row = row_parts
        return attend_block(
            queries_row, heads_view(cross_keys), heads_view(cross_values), cross_allowed(image_row)
        )

    def cross_backward(row_parts):
        queries_row, image_row, log_row, grad_row = row_parts
        return attend_back(
            queries_row,
            heads_view(cross_keys),
            heads_view(cross_values),
            cross_allowed(image_row),
            log_row,
            grad_row,
        )

    cross_mixed, cross_log = lax.map(cross_forward, (heads_view(cross_queries), token_image))
    cross_mixed = flat_rows(cross_mixed)
    after_cross = after_self + narrow(matmul(cross_mixed, c_out))
    normed_three_local = rms_norm(after_cross, norm_gains[2]).astype(jnp.bfloat16)
    normed_three = widen_rows(normed_three_local)
    gate_pre = matmul(normed_three, w_gate)
    up_pre = matmul(normed_three, w_up)
    hidden = gated_unit(gate_pre, up_pre).astype(jnp.bfloat16)
    output = (after_cross + narrow(matmul(hidden, w_down))).astype(jnp.bfloat16)
    grad_rows = cotangent.astype(jnp.float32)
    normed_full = normed_three
    grad_branch = gather_grad(grad_rows)
    grad_hidden = jnp.einsum("rsd,fd->rsf", grad_branch, w_down, preferred_element_type=jnp.float32)
    unused, gate_pull = jax.vjp(gated_unit, gate_pre, up_pre)
    grad_gate, grad_up = gate_pull(grad_hidden)
    grad_gate = grad_gate.astype(jnp.bfloat16)
    grad_up = grad_up.astype(jnp.bfloat16)
    grad_w_down = jnp.einsum("rsf,rsd->fd", hidden, grad_branch, preferred_element_type=jnp.float32)
    grad_w_gate = jnp.einsum(
        "rsd,rsf->df", normed_full, grad_gate, preferred_element_type=jnp.float32
    )
    grad_w_up = jnp.einsum("rsd,rsf->df", normed_full, grad_up, preferred_element_type=jnp.float32)
    grad_normed = sum_grad(
        jnp.einsum("rsf,df->rsd", grad_gate, w_gate, preferred_element_type=jnp.float32)
        + jnp.einsum("rsf,df->rsd", grad_up, w_up, preferred_element_type=jnp.float32)
    )
    unused, norm_pull = jax.vjp(rms_norm, after_cross, norm_gains[2])
    grad_input, grad_gain_three = norm_pull(grad_normed)
    grad_rows = grad_rows + grad_input
    normed_full = normed_two
    grad_branch = gather_grad(grad_rows)
    grad_attended = jnp.einsum(
        "rsd,ed->rse", grad_branch, c_out, preferred_element_type=jnp.float32
    ).astype(jnp.bfloat16)
    grad_c_out = jnp.einsum(
        "rse,rsd->ed", cross_mixed, grad_branch, preferred_element_type=jnp.float32
    )
    grad_cq, grad_ck, grad_cv = lax.map(
        cross_backward,
        (heads_view(cross_queries), token_image, cross_log, heads_view(grad_attended)),
    )
    grad_cq = flat_rows(grad_cq).astype(jnp.bfloat16)
    grad_ck = jnp.sum(grad_ck, axis=0).reshape(patch_rows, -1).astype(jnp.bfloat16)
    grad_cv = jnp.sum(grad_cv, axis=0).reshape(patch_rows, -1).astype(jnp.bfloat16)
    grad_c_query = jnp.einsum(
        "rsd,rse->de", normed_full, grad_cq, preferred_element_type=jnp.float32
    )
    grad_c_key = jnp.einsum("pd,pe->de", projected, grad_ck, preferred_element_type=jnp.float32)
    grad_c_value = jnp.einsum("pd,pe->de", projected, grad_cv, preferred_element_type=jnp.float32)
    projected_part = jnp.einsum(
        "pe,de->pd", grad_ck, c_key, preferred_element_type=jnp.float32
    ) + jnp.einsum("pe,de->pd", grad_cv, c_value, preferred_element_type=jnp.float32)
    grad_projected = lax.psum_scatter(
        projected_part.astype(jnp.bfloat16), "mp", scatter_dimension=0, tiled=True
    )
    share_rows = grad_projected.shape[0]
    patch_share = lax.dynamic_slice_in_dim(
        patch_flat, lax.axis_index("mp") * share_rows, share_rows, 0
    )
    grad_patch_proj = jnp.einsum(
        "pv,pd->vd", patch_share, grad_projected, preferred_element_type=jnp.float32
    )
    grad_normed = sum_grad(
        jnp.einsum("rse,de->rsd", grad_cq, c_query, preferred_element_type=jnp.float32)
    )
    unused, norm_pull = jax.vjp(rms_norm, after_self, norm_gains[1])
    grad_input, grad_gain_two = norm_pull(grad_normed)
    grad_rows = grad_rows + grad_input
    normed_full = normed_one
    grad_branch = gather_grad(grad_rows)
    grad_attended = jnp.einsum(
        "rsd,ed->rse", grad_branch, w_out, preferred_element_type=jnp.float32
    ).astype(jnp.bfloat16)
    grad_w_out = jnp.einsum(
        "rse,rsd->ed", self_mixed, grad_branch, preferred_element_type=jnp.float32
    )
    grad_sq, grad_sk, grad_sv = lax.map(
        self_backward,
        (
            heads_view(queries),
            heads_view(key_rows),
            heads_view(value_rows),
            segment_ids,
            self_log,
            heads_view(grad_attended),
        ),
    )
    grad_sq = flat_rows(grad_sq).astype(jnp.bfloat16)
    grad_sk = flat_rows(grad_sk).astype(jnp.bfloat16)
    grad_sv = flat_rows(grad_sv).astype(jnp.bfloat16)
    grad_w_query = jnp.einsum(
        "rsd,rse->de", normed_full, grad_sq, preferred_element_type=jnp.float32
    )
    grad_w_key = jnp.einsum("rsd,rse->de", normed_full, grad_sk, preferred_element_type=jnp.float32)
    grad_w_value = jnp.einsum(
        "rsd,rse->de", normed_full, grad_sv, preferred_element_type=jnp.float32
    )
    grad_normed = sum_grad(
        jnp.einsum("rse,de->rsd", grad_sq, w_query, preferred_element_type=jnp.float32)
        + jnp.einsum("rse,de->rsd", grad_sk, w_key, preferred_element_type=jnp.float32)
        + jnp.einsum("rse,de->rsd", grad_sv, w_value, preferred_element_type=jnp.float32)
    )
    unused, norm_pull = jax.vjp(rms_norm, residual, norm_gains[0])
    grad_input, grad_gain_one = norm_pull(grad_normed)
    grad_rows = grad_rows + grad_input
    gain_terms = jnp.stack([grad_gain_one, grad_gain_two, grad_gain_three])
    def sum_rows(partial, axes, dim):
        return lax.psum_scatter(
            partial.astype(jnp.bfloat16), axes, scatter_dimension=dim, tiled=True
        ).astype(jnp.float32)

    gain_total = lax.psum_scatter(gain_terms, ("dp", "mp"), scatter_dimension=1, tiled=True)
    patch_total = sum_rows(grad_patch_proj, ("dp", "mp"), 1)
    sum_query = sum_rows(grad_w_query, "dp", 0)
    sum_key = sum_rows(grad_w_key, "dp", 0)
    sum_value = sum_rows(grad_w_value, "dp", 0)
    sum_out = sum_rows(grad_w_out, "dp", 1)
    sum_cquery = sum_rows(grad_c_query, "dp", 0)
    sum_ckey = sum_rows(grad_c_key, "dp", 0)
    sum_cvalue = sum_rows(grad_c_value, "dp", 0)
    sum_cout = sum_rows(grad_c_out, "dp", 1)
    sum_gate = sum_rows(grad_w_gate, "dp", 0)
    sum_up = sum_rows(grad_w_up, "dp", 0)
    sum_down = sum_rows(grad_w_down, "dp", 1)
    return (
        output,
        grad_rows,
        gain_total,
        sum_query,
        sum_key,
        sum_value,
        sum_out,
        sum_cquery,
        sum_ckey,
        sum_cvalue,
        sum_cout,
        patch_total,
        sum_gate,
        sum_up,
        sum_down,
    )


def solution(mesh):
    return jax.shard_map(
        shards,
        mesh=mesh,
        in_specs=(
            P("dp", "mp", None),
            P(),
            P(None, "mp"),
            P(None, "mp"),
            P(None, "mp"),
            P("mp", None),
            P(None, "mp"),
            P(None, "mp"),
            P(None, "mp"),
            P("mp", None),
            P(),
            P(None, "mp"),
            P(None, "mp"),
            P("mp", None),
            P("dp", None, None),
            P("dp", None),
            P("dp", None),
            P("dp", "mp", None),
        ),
        out_specs=(
            P("dp", "mp", None),
            P("dp", "mp", None),
            P(None, ("dp", "mp")),
            P("dp", "mp"),
            P("dp", "mp"),
            P("dp", "mp"),
            P("mp", "dp"),
            P("dp", "mp"),
            P("dp", "mp"),
            P("dp", "mp"),
            P("mp", "dp"),
            P(None, ("dp", "mp")),
            P("dp", "mp"),
            P("dp", "mp"),
            P("mp", "dp"),
        ),
        check_vma=False,
    )
```

```python
import jax
import jax.numpy as jnp
from jax import lax
from jax.sharding import PartitionSpec as P

HEAD_DIM = 128
SEGS = 4
EPSILON = 1e-06
MASKED = -1000000000.0
F32 = jnp.float32
BF16 = jnp.bfloat16


def matmul(left, right):
    return jnp.dot(left, right, preferred_element_type=F32)


def product(spec, left, right):
    return jnp.einsum(spec, left, right, preferred_element_type=F32)


def rows_dot(left, right):
    return lax.dot_general(left, right, (((0,), (0,)), ((), ())), preferred_element_type=F32)


def cols_dot(left, right):
    return lax.dot_general(left, right, (((1,), (1,)), ((), ())), preferred_element_type=F32)


def tie(value, after):
    return lax.optimization_barrier((value, after))[0]


def inverse_rms(rows):
    return lax.rsqrt(jnp.mean(rows * rows, axis=-1, keepdims=True) + EPSILON)


def norm_rows(rows, gain):
    return (rows * inverse_rms(rows) * gain).astype(BF16)


def norm_back(rows, gain, grad):
    inv = inverse_rms(rows)
    weighted = gain * grad
    inner = jnp.mean(rows * weighted, axis=-1, keepdims=True)
    grad_rows = inv * weighted - rows * (inv * inv * inv) * inner
    return grad_rows, jnp.sum(grad * rows * inv, axis=0)


def plain_scores(queries, keys, allowed):
    scores = product("shd,thd->hst", queries, keys) * (HEAD_DIM ** (-0.5))
    return jnp.where(allowed[None], scores, MASKED)


def by_head(arr):
    return arr.reshape(arr.shape[0], -1, HEAD_DIM)


def flat_heads(arr):
    return arr.reshape(arr.shape[0], -1).astype(BF16)


def plain_attend(queries, keys, values, allowed):
    scores = plain_scores(by_head(queries), by_head(keys), allowed)
    top = jnp.max(scores, axis=-1, keepdims=True)
    exponent = jnp.exp(scores - top)
    total = jnp.sum(exponent, axis=-1, keepdims=True)
    weights = (exponent / total).astype(BF16)
    return flat_heads(product("hst,thd->shd", weights, by_head(values))), top + jnp.log(total)


def plain_back(queries, keys, values, allowed, log_total, grad_out):
    queries, keys, values, grad_out = [by_head(v) for v in (queries, keys, values, grad_out)]
    weights = jnp.exp(plain_scores(queries, keys, allowed) - log_total)
    grad_weights = product("shd,thd->hst", grad_out, values)
    inner = jnp.sum(weights * grad_weights, axis=-1, keepdims=True)
    grad_scores = (weights * (grad_weights - inner)).astype(BF16)
    scale = HEAD_DIM ** (-0.5)
    grad_queries = product("hst,thd->shd", grad_scores, keys) * scale
    grad_keys = product("hst,shd->thd", grad_scores, queries) * scale
    grad_values = product("hst,shd->thd", weights.astype(BF16), grad_out)
    return [flat_heads(v) for v in (grad_queries, grad_keys, grad_values)]


def gated_unit(gate_arg, up_arg):
    return jax.nn.gelu(gate_arg, approximate=True) * up_arg


def layer(n_dp, n_mp):
    lanes = n_dp // 2
    paired = n_dp == 8

    def swap(value, axis, size, bit):
        return lax.ppermute(value, axis, [(i, i ^ bit) for i in range(size)])

    def core(value):
        return swap(value, "mp", n_mp, 1)

    def chip(value):
        return swap(value, "mp", n_mp, 2)

    def beside(value):
        return swap(value, "dp", n_dp, 1)

    def gather(mine):
        far = chip(mine)
        return jnp.concatenate([mine, far, core(mine), core(far)], axis=0)

    def scatter_rows(partial):
        step = partial.shape[0] // 4
        block = [partial[k * step : (k + 1) * step] for k in range(4)]
        far = (block[1].astype(F32) + core(block[3]).astype(F32)).astype(BF16)
        far_in = chip(far)
        return block[0].astype(F32) + core(block[2]).astype(F32) + far_in.astype(F32)

    def line_place():
        z = lax.axis_index("dp") // 2
        number = lambda value: jnp.asarray(value).astype(jnp.int32)
        return lax.axis_index("dp") % 2, number(z >= 2), number((z == 1) | (z == 2))

    def outer_swap(value):
        return swap(value, "dp", n_dp, 2)

    def inner_swap(value):
        pairs = []
        for d in range(n_dp):
            for m in range(n_mp):
                inner = d // 2 in (1, 2)
                to = (d ^ 6) * n_mp + m if inner else d * n_mp + (m ^ 1)
                pairs.append((d * n_mp + m, to))
        return lax.ppermute(value, ("dp", "mp"), pairs)

    def line_steps(near, far):
        inner = line_place()[2]
        incoming = outer_swap(far)
        yield
        sums = (far.astype(F32) + incoming.astype(F32)).astype(BF16)
        crossed = inner_swap(sums)
        yield
        mine = jnp.where(
                inner == 1,
                (near[:1].astype(F32) + crossed[1:].astype(F32)).astype(BF16),
                near[1:],
            )
        last = outer_swap(mine)
        yield
        total = jnp.where(inner == 1, near[1], near[0]).astype(F32) + last[0].astype(F32)
        return total + jnp.where(inner == 1, crossed[0].astype(F32), 0.0)

    def split_columns(value):
        if not paired:
            return (value,)
        x = lax.axis_index("dp") % 2
        half, width = value.shape[0] // 2, value.shape[1] // n_dp
        wanted = jnp.concatenate(
            [
                jnp.where(
                    x == 0,
                    value[:half, (2 * z + 1) * width : (2 * z + 2) * width],
                    value[:half, 2 * z * width : (2 * z + 1) * width],
                )
                for z in range(lanes)
            ],
            axis=1,
        )
        low = beside(wanted)
        return value, low, core(low)

    def weight_grad(split, grad, rows_first, grad_far=None):
        if paired:
            if grad_far is None:
                grad_far = beside(grad)
            grads = grad if grad.ndim == 3 else grad[None]
            grads_far = grad_far if grad.ndim == 3 else grad_far[None]
            x, flip, inner = line_place()
            own, low, high = split
            half = low.shape[0]
            width = own.shape[1] // 8
            own = jnp.concatenate(
                [
                    jnp.where(
                        x == 0,
                        own[:, 2 * z * width : (2 * z + 1) * width],
                        own[:, (2 * z + 1) * width : (2 * z + 2) * width],
                    )
                    for z in range(4)
                ],
                axis=1,
            )
            part = (
                product("td,nte->dne", own, grads)
                + product("td,nte->dne", low, grads_far[:, :half])
                + product("td,nte->dne", high, grads_far[:, half:])
            ).astype(BF16)
            part = part.reshape(4, width, grads.shape[0], grads.shape[2]).transpose(0, 2, 1, 3)
            near = jnp.where(flip == 1, jnp.stack([part[3], part[2]]), part[:2])
            far = jnp.where(flip == 1, jnp.stack([part[1], part[0]]), part[2:])
            total = yield from line_steps(near, far)
        else:
            grads = grad if grad.ndim == 3 else grad[None]
            partial = product("td,nte->dne", split[0], grads).astype(BF16)
            total = lax.psum_scatter(partial, "dp", scatter_dimension=0, tiled=True)
            total = total.astype(F32).transpose(1, 0, 2)
        return [total[n] if rows_first else total[n].T for n in range(total.shape[0])]

    results = {}

    def advance(name, work):
        try:
            next(work)
        except StopIteration as stop:
            results[name] = stop.value
            return False
        return True

    def total_sum(value):
        for bit in (1, 2):
            value = value + swap(value, "mp", n_mp, bit)
        if not paired:
            return lax.psum(value, "dp")
        for bit in (1, 2, 4):
            value = value + swap(value, "dp", n_dp, bit)
        return value

    def shards(
        tokens, norm_gains, w_query, w_key, w_value, w_out, c_query, c_key, c_value, c_out,
        patch_proj, w_gate, w_up, w_down, patches, segment_ids, image_index, cotangent,
    ):
        length = segment_ids.shape[1]
        model = tokens.shape[2]
        patch_rows = patches.shape[0] * patches.shape[1]
        m = lax.axis_index("mp")
        order = [m, m ^ 2, m ^ 1, m ^ 3]

        def blocks(arr, axis=0):
            step = arr.shape[axis] // 4
            return jnp.concatenate(
                [lax.dynamic_slice_in_dim(arr, k * step, step, axis) for k in order], axis=axis
            )

        places = blocks(jnp.arange(length, dtype=jnp.int32))
        segment_row = blocks(segment_ids[0])
        slots = jnp.arange(SEGS, dtype=jnp.int32)
        token_image = jnp.sum(
            jnp.where(segment_row[:, None] == slots, image_index[0][None, :], 0), axis=-1
        )
        patch_image = blocks(jnp.arange(patch_rows, dtype=jnp.int32) // patches.shape[1])

        residual = tokens[0].astype(F32)
        normed_one = gather(norm_rows(residual, norm_gains[0]))
        patch_own = blocks(patches.reshape(patch_rows, patches.shape[2]))
        projected = gather(matmul(patch_own[: patch_rows // 4], patch_proj).astype(BF16))
        cross_keys = matmul(projected, c_key).astype(BF16)
        cross_values = matmul(projected, c_value).astype(BF16)
        grad_three = gather(cotangent[0])
        grad_hidden = product("sd,fd->sf", grad_three, w_down)
        queries = matmul(normed_one, w_query).astype(BF16)
        key_rows = matmul(normed_one, w_key).astype(BF16)
        value_rows = matmul(normed_one, w_value).astype(BF16)
        self_allowed = (segment_row[:, None] == segment_row[None, :]) & (
            places[None, :] <= places[:, None]
        )
        cross_allowed = token_image[:, None] == patch_image[None, :]
        self_mixed, self_log = plain_attend(queries, key_rows, value_rows, self_allowed)
        after_self = residual + scatter_rows(matmul(self_mixed, w_out).astype(BF16))
        normed_two = gather(norm_rows(after_self, norm_gains[1]))
        cross_queries = matmul(normed_two, c_query).astype(BF16)
        cross_mixed, cross_log = plain_attend(
            cross_queries, cross_keys, cross_values, cross_allowed
        )
        after_cross = after_self + scatter_rows(matmul(cross_mixed, c_out).astype(BF16))
        normed_three = gather(norm_rows(after_cross, norm_gains[2]))
        gate_pre, up_pre = matmul(normed_three, w_gate), matmul(normed_three, w_up)
        hidden, pull = jax.vjp(gated_unit, gate_pre, up_pre)
        hidden = hidden.astype(BF16)
        grad_gate, grad_up = [g.astype(BF16) for g in pull(grad_hidden)]
        results.clear()
        running = []

        def begin(name, *args):
            running.append((name, weight_grad(*args)))
            turn()

        def turn():
            for item in running[:2]:
                if not advance(*item):
                    running.remove(item)

        split_three = split_columns(normed_three)
        if paired:
            hidden_far = beside(hidden)
            gate_far = beside(tie(grad_gate, hidden_far))
            up_far = beside(tie(grad_up, gate_far))
        else:
            hidden_far = gate_far = up_far = None
        grad_normed = scatter_rows(
            (
                product("sf,df->sd", grad_gate, w_gate) + product("sf,df->sd", grad_up, w_up)
            ).astype(BF16)
        )
        begin("down", split_columns(grad_three), hidden, False, hidden_far)
        grad_input, gain_three = norm_back(after_cross, norm_gains[2], grad_normed)
        grad_rows = cotangent[0].astype(F32) + grad_input
        begin("gate", split_three, grad_gate, True, gate_far)

        grad_two = gather(grad_rows.astype(BF16))
        turn()
        grad_mixed = product("sd,ed->se", grad_two, c_out).astype(BF16)
        begin("up", split_three, grad_up, True, up_far)
        grad_cq, grad_ck, grad_cv = plain_back(
            cross_queries, cross_keys, cross_values, cross_allowed, cross_log, grad_mixed
        )
        grad_ckv = jnp.stack([grad_ck, grad_cv])
        output = after_cross + scatter_rows(matmul(hidden, w_down).astype(BF16))
        turn()
        grad_normed = scatter_rows(product("se,de->sd", grad_cq, c_query).astype(BF16))
        grad_input, gain_two = norm_back(after_self, norm_gains[1], grad_normed)
        grad_rows = grad_rows + grad_input
        begin("c_out", split_columns(grad_two), cross_mixed, False)
        begin("c_query", split_columns(normed_two), grad_cq, True)
        begin("c_pair", split_columns(projected), grad_ckv, True)

        grad_one = gather(grad_rows.astype(BF16))
        grad_mixed = product("sd,ed->se", grad_one, w_out).astype(BF16)
        grad_self = jnp.stack(
            plain_back(queries, key_rows, value_rows, self_allowed, self_log, grad_mixed)
        )
        grad_normed = scatter_rows(
            (
                product("se,de->sd", grad_self[0], w_query)
                + product("se,de->sd", grad_self[1], w_key)
                + product("se,de->sd", grad_self[2], w_value)
            ).astype(BF16)
        )
        grad_input, gain_one = norm_back(residual, norm_gains[0], grad_normed)
        grad_rows = grad_rows + grad_input
        gain_total = total_sum(jnp.stack([gain_one, gain_two, gain_three]))
        share = model // (n_dp * n_mp)
        gain_total = lax.dynamic_slice_in_dim(
            gain_total, (lax.axis_index("dp") * n_mp + m) * share, share, 1
        )
        begin("w_out", split_columns(grad_one), self_mixed, False)
        begin("w_qkv", split_columns(normed_one), grad_self, True)

        width = model // (n_dp * n_mp)

        def projected_block(k):
            def rows_of(weight):
                cut = weight.reshape(n_dp, n_mp, width, weight.shape[1])
                return lax.dynamic_index_in_dim(cut, k, 1, keepdims=False).reshape(
                    n_dp * width, weight.shape[1]
                )

            return (
                cols_dot(grad_ckv[0], rows_of(c_key)) + cols_dot(grad_ckv[1], rows_of(c_value))
            ).astype(BF16)

        def swap_blocks(value, size):
            starts = [size * (k ^ 1) for k in range(value.shape[0] // size)]
            return jnp.concatenate([value[at : at + size] for at in starts], axis=0)

        block = [projected_block(k) for k in order]
        half, quarter = patch_rows // 2, patch_rows // 4
        far = block[1].astype(F32) + swap_blocks(core(block[3]), half).astype(F32)
        near = block[0].astype(F32) + swap_blocks(core(block[2]), half).astype(F32)
        grad_projected = near + swap_blocks(chip(far.astype(BF16)), quarter).astype(F32)
        patch_partial = rows_dot(grad_projected.astype(BF16), patch_own).astype(BF16)

        def patch_sum():
            if not paired:
                return lax.psum_scatter(
                    patch_partial, "dp", scatter_dimension=0, tiled=True
                ).astype(F32)
            x = lax.axis_index("dp") % 2
            parts = patch_partial.reshape(lanes, 2, width, patches.shape[2])
            sent = beside(lax.dynamic_index_in_dim(parts, 1 - x, 1, keepdims=False))
            kept = lax.dynamic_index_in_dim(parts, x, 1, keepdims=False)
            summed = (kept.astype(F32) + sent.astype(F32)).astype(BF16)[:, None]
            flip = line_place()[1] == 1
            near, far = (
                jnp.where(flip, jnp.stack([summed[3 - a], summed[3 - b]]), summed[a : b + 1])
                for a, b in ((0, 1), (2, 3))
            )
            total = yield from line_steps(near, far)
            return total[0]

        running.append(("patch", patch_sum()))
        while running:
            turn()
        [sum_down], [sum_gate], [sum_up] = results["down"], results["gate"], results["up"]
        [sum_cout], [sum_cquery], [sum_out] = results["c_out"], results["c_query"], results["w_out"]
        sum_ckey, sum_cvalue = results["c_pair"]
        sum_query, sum_key, sum_value = results["w_qkv"]
        patch_total = results["patch"].T
        return (
            output.astype(BF16)[None], grad_rows[None], gain_total,
            sum_query, sum_key, sum_value, sum_out,
            sum_cquery, sum_ckey, sum_cvalue, sum_cout,
            patch_total, sum_gate, sum_up, sum_down,
        )

    return shards


def solution(mesh):
    columns, rows = P(None, "mp"), P("mp", None)
    return jax.shard_map(
        layer(mesh.shape["dp"], mesh.shape["mp"]),
        mesh=mesh,
        in_specs=(
            P("dp", "mp", None), P(), columns, columns, columns, rows, columns, columns, columns,
            rows, P(), columns, columns, rows, P("dp", None, None), P("dp", None), P("dp", None),
            P("dp", "mp", None),
        ),
        out_specs=(
            P("dp", "mp", None), P("dp", "mp", None), P(None, ("dp", "mp")),
            P("dp", "mp"), P("dp", "mp"), P("dp", "mp"), P("mp", "dp"),
            P("dp", "mp"), P("dp", "mp"), P("dp", "mp"), P("mp", "dp"),
            P(None, ("dp", "mp")), P("dp", "mp"), P("dp", "mp"), P("mp", "dp"),
        ),
        check_vma=False,
    )
```

```python
import functools

import jax
import jax.numpy as jnp
from jax import lax
from jax.experimental import pallas as pl
from jax.experimental.pallas import tpu as pltpu
from jax.sharding import PartitionSpec as P

HEAD_DIM = 128
SEGS = 4
EPSILON = 1e-06
MASKED = -1000000000.0
F32 = jnp.float32
BF16 = jnp.bfloat16


def matmul(left, right):
    return jnp.dot(left, right, preferred_element_type=F32)


def product(spec, left, right):
    return jnp.einsum(spec, left, right, preferred_element_type=F32)


def rows_dot(left, right):
    return lax.dot_general(left, right, (((0,), (0,)), ((), ())), preferred_element_type=F32)


def cols_dot(left, right):
    return lax.dot_general(left, right, (((1,), (1,)), ((), ())), preferred_element_type=F32)


def tie(value, after):
    return lax.optimization_barrier((value, after))[0]


def inverse_rms(rows):
    return lax.rsqrt(jnp.mean(rows * rows, axis=-1, keepdims=True) + EPSILON)


def norm_rows(rows, gain):
    return (rows * inverse_rms(rows) * gain).astype(BF16)


def norm_back(rows, gain, grad):
    inv = inverse_rms(rows)
    weighted = gain * grad
    inner = jnp.mean(rows * weighted, axis=-1, keepdims=True)
    grad_rows = inv * weighted - rows * (inv * inv * inv) * inner
    return grad_rows, jnp.sum(grad * rows * inv, axis=0)


def plain_scores(queries, keys, allowed):
    scores = product("shd,thd->hst", queries, keys) * (HEAD_DIM ** (-0.5))
    return jnp.where(allowed[None], scores, MASKED)


def by_head(arr):
    return arr.reshape(arr.shape[0], -1, HEAD_DIM)


def flat_heads(arr):
    return arr.reshape(arr.shape[0], -1).astype(BF16)


def plain_attend(queries, keys, values, allowed):
    scores = plain_scores(by_head(queries), by_head(keys), allowed)
    top = jnp.max(scores, axis=-1, keepdims=True)
    exponent = jnp.exp(scores - top)
    total = jnp.sum(exponent, axis=-1, keepdims=True)
    weights = (exponent / total).astype(BF16)
    return flat_heads(product("hst,thd->shd", weights, by_head(values))), top + jnp.log(total)


def plain_back(queries, keys, values, allowed, log_total, grad_out):
    queries, keys, values, grad_out = [by_head(v) for v in (queries, keys, values, grad_out)]
    weights = jnp.exp(plain_scores(queries, keys, allowed) - log_total)
    grad_weights = product("shd,thd->hst", grad_out, values)
    inner = jnp.sum(weights * grad_weights, axis=-1, keepdims=True)
    grad_scores = (weights * (grad_weights - inner)).astype(BF16)
    scale = HEAD_DIM ** (-0.5)
    grad_queries = product("hst,thd->shd", grad_scores, keys) * scale
    grad_keys = product("hst,shd->thd", grad_scores, queries) * scale
    grad_values = product("hst,shd->thd", weights.astype(BF16), grad_out)
    return [flat_heads(v) for v in (grad_queries, grad_keys, grad_values)]


VMEM_LIMIT = 20 * 2**20
ANY = pl.BlockSpec(memory_space=pl.ANY)


def params(grid_rank):
    return pltpu.CompilerParams(
        dimension_semantics=("arbitrary",) * grid_rank, vmem_limit_bytes=VMEM_LIMIT
    )


def cost(flops, size):
    return pl.CostEstimate(flops=flops, bytes_accessed=size, transcendentals=0)


def assemble_kernel(*refs):
    *blocks, out_ref = refs
    step = blocks[0].shape[0]
    for k, block in enumerate(blocks):
        out_ref[k * step : (k + 1) * step] = block[...]


def assemble(blocks):
    step, width = blocks[0].shape
    columns = 512
    return pl.pallas_call(
        assemble_kernel,
        grid=(width // columns,),
        in_specs=[pl.BlockSpec((step, columns), lambda j: (0, j))] * len(blocks),
        out_specs=pl.BlockSpec((len(blocks) * step, columns), lambda j: (0, j)),
        out_shape=jax.ShapeDtypeStruct((len(blocks) * step, width), blocks[0].dtype),
        compiler_params=params(1),
        cost_estimate=cost(0, 4 * len(blocks) * step * width),
    )(*blocks)


def copy_kernel(at_ref, in_ref, out_ref):
    out_ref[...] = in_ref[...]


def pick_rows(at, arr, step):
    count, width = at.shape[0], arr.shape[1]
    return pl.pallas_call(
        copy_kernel,
        grid_spec=pltpu.PrefetchScalarGridSpec(
            num_scalar_prefetch=1,
            grid=(count,),
            in_specs=[pl.BlockSpec((step, width), lambda k, at: (at[k], 0))],
            out_specs=pl.BlockSpec((step, width), lambda k, at: (k, 0)),
        ),
        out_shape=jax.ShapeDtypeStruct((count * step, width), arr.dtype),
        compiler_params=params(1),
        cost_estimate=cost(0, 4 * count * step * width),
    )(at, arr)


def pick_columns(at, arr, rows, width):
    count = at.shape[0]
    return pl.pallas_call(
        copy_kernel,
        grid_spec=pltpu.PrefetchScalarGridSpec(
            num_scalar_prefetch=1,
            grid=(count,),
            in_specs=[pl.BlockSpec((rows, width), lambda k, at: (0, at[k]))],
            out_specs=pl.BlockSpec((rows, width), lambda k, at: (0, k)),
        ),
        out_shape=jax.ShapeDtypeStruct((rows, count * width), arr.dtype),
        compiler_params=params(1),
        cost_estimate=cost(0, 4 * count * rows * width),
    )(at, arr)


def add_kernel(left_ref, right_ref, out_ref):
    out_ref[...] = (left_ref[...].astype(F32) + right_ref[...].astype(F32)).astype(BF16)


def add_swapped(left, right, size):
    width = left.shape[1]
    block = pl.BlockSpec((size, width), lambda k: (k, 0))
    return pl.pallas_call(
        add_kernel,
        grid=(left.shape[0] // size,),
        in_specs=[block, pl.BlockSpec((size, width), lambda k: (k + 1 - 2 * (k % 2), 0))],
        out_specs=block,
        out_shape=jax.ShapeDtypeStruct(left.shape, BF16),
        compiler_params=params(1),
        cost_estimate=cost(left.size, 6 * left.size),
    )(left, right)


def pair_kernel(at_ref, a_ref, lo_ref, hi_ref, g_ref, far_ref, *rest):
    half = lo_ref.shape[0]
    total = rows_dot(a_ref[...], g_ref[...])
    total += rows_dot(lo_ref[...], far_ref[:half])
    total += rows_dot(hi_ref[...], far_ref[half:])
    rest[-1][0] = total.astype(BF16)


def pair_grad(at, own, low, high, grad, grad_far, after):
    length, units = grad.shape
    width = own.shape[1] // 8
    whole = pl.BlockSpec((length, units), lambda k, at: (0, 0))
    side = pl.BlockSpec((length // 2, width), lambda k, at: (0, k))
    return pl.pallas_call(
        pair_kernel,
        grid_spec=pltpu.PrefetchScalarGridSpec(
            num_scalar_prefetch=1,
            grid=(4,),
            in_specs=[
                pl.BlockSpec((length, width), lambda k, at: (0, at[k])), side, side, whole, whole,
            ] + [ANY] * len(after),
            out_specs=pl.BlockSpec((1, width, units), lambda k, at: (k, 0, 0)),
        ),
        out_shape=jax.ShapeDtypeStruct((4, width, units), BF16),
        compiler_params=params(1),
        cost_estimate=cost(
            16 * length * width * units, 2 * units * (2 * length + 4 * width) + 16 * length * width
        ),
    )(at, own, low, high, grad, grad_far, *after)


def merge_kernel(in_ref, part_ref, out_ref):
    keep = jnp.where(pl.program_id(0) > 0, in_ref[...].astype(F32), 0.0)
    out_ref[...] = (part_ref[...].astype(F32) + keep).astype(BF16)


def merge(part, incoming):
    block = (1,) + part.shape[1:]
    return pl.pallas_call(
        merge_kernel,
        grid=(4,),
        in_specs=[
            pl.BlockSpec(block, lambda k: (jnp.maximum(k - 1, 0), 0, 0)),
            pl.BlockSpec(block, lambda k: (k, 0, 0)),
        ],
        out_specs=pl.BlockSpec(block, lambda k: (k, 0, 0)),
        out_shape=jax.ShapeDtypeStruct(part.shape, BF16),
        compiler_params=params(1),
        cost_estimate=cost(part.size, 6 * part.size),
    )(incoming, part)


def cross_kernel(at_ref, part_ref, in_ref, out_ref):
    keep = jnp.where(at_ref[0] == 1, in_ref[...].astype(F32), 0.0)
    out_ref[...] = (part_ref[...].astype(F32) + keep).astype(BF16)


def cross_add(inner, part, crossed):
    block = (1,) + part.shape[1:]
    return pl.pallas_call(
        cross_kernel,
        grid_spec=pltpu.PrefetchScalarGridSpec(
            num_scalar_prefetch=1,
            grid=(2,),
            in_specs=[
                pl.BlockSpec(block, lambda k, at: (k, 0, 0)),
                pl.BlockSpec(block, lambda k, at: (1 - k, 0, 0)),
            ],
            out_specs=pl.BlockSpec(block, lambda k, at: (k, 0, 0)),
        ),
        out_shape=jax.ShapeDtypeStruct((2,) + part.shape[1:], BF16),
        compiler_params=params(1),
        cost_estimate=cost(crossed.size, 6 * crossed.size),
    )(inner, part, crossed)


def add_rows(target, *sources):
    step = 32

    def body(i, carry):
        rows = pl.ds(pl.multiple_of(i * step, step), step)
        total = sources[0][rows].astype(F32)
        for source in sources[1:]:
            total = total + source[rows].astype(F32)
        target[rows] = total.astype(target.dtype)
        return carry

    lax.fori_loop(0, target.shape[0] // step, body, 0)


def line_kernel(ready, count, *refs):
    parts, outs, refs = refs[:count], refs[count : 2 * count], refs[2 * count :]
    late = range(ready, count)
    from_outer = dict(zip(late, refs[: count - ready]))
    refs = refs[count - ready :]
    from_inner = dict(zip(late, refs[: count - ready]))
    refs = refs[count - ready :]
    last, refs = refs[:count], refs[count:]
    send_out, got_out, send_in, got_in, send_last, got_last = refs
    dp, mp = lax.axis_index("dp"), lax.axis_index("mp")
    z, x = dp // 2, dp % 2
    beside = ((z + 1 - 2 * (z % 2)) * 2 + x, mp)
    across = ((3 - z) * 2 + x, mp)
    inner = (z == 1) | (z == 2)
    outer = (z == 0) | (z == 3)
    where = pl.DeviceIdType.MESH
    barrier = pltpu.get_barrier_semaphore()
    pl.semaphore_signal(barrier, inc=1, device_id=beside, device_id_type=where)

    def copy(source, target, sent, got, device):
        return pltpu.make_async_remote_copy(
            src_ref=source, dst_ref=target, send_sem=sent, recv_sem=got,
            device_id=device, device_id_type=where,
        )

    def copy_out(g):
        return copy(
            parts[g].at[pl.ds(1, 3)], from_outer[g], send_out.at[g], got_out.at[g], beside
        )

    def copy_in(g):
        return copy(
            from_outer[g].at[pl.ds(1, 2)], from_inner[g], send_in.at[g], got_in.at[g], across
        )

    def copy_last(g):
        source = parts[g].at[0] if g < ready else from_inner[g].at[1]
        return copy(source, last[g], send_last.at[g], got_last.at[g], beside)

    @pl.when(outer)
    def _():
        pl.semaphore_wait(barrier, 1)
        for g in late:
            copy_out(g).start()
        for g in range(count):
            copy_last(g).wait_recv()
            add_rows(outs[g], parts[g].at[0], last[g])
        for g in late:
            copy_out(g).wait_send()

    @pl.when(inner)
    def _():
        pl.semaphore_signal(barrier, inc=1, device_id=across, device_id_type=where)
        pl.semaphore_wait(barrier, 2)
        for g in range(ready):
            copy_last(g).start()

        def finish(g):
            copy_in(g).wait_recv()
            add_rows(outs[g], parts[g].at[1], from_outer[g].at[0], from_inner[g].at[0])
            add_rows(from_inner[g].at[1], parts[g].at[0], from_inner[g].at[1])
            copy_last(g).start()

        for g in range(ready):
            add_rows(outs[g], parts[g].at[1])
        for g in late:
            copy_out(g).wait_recv()
            for k in (1, 2):
                add_rows(from_outer[g].at[k], parts[g].at[k + 1], from_outer[g].at[k])
            copy_in(g).start()
            if g > ready:
                finish(g - 1)
        finish(count - 1)
        for g in late:
            copy_in(g).wait_send()
        for g in range(count):
            copy_last(g).wait_send()


def line_sums(ready_parts, late_parts):
    parts = list(ready_parts) + list(late_parts)
    ready, count = len(ready_parts), len(parts)
    vmem = pl.BlockSpec(memory_space=pltpu.VMEM)
    blocks = lambda size, arr: pltpu.VMEM((size,) + arr.shape[1:], BF16)
    size = sum(p.size for p in parts)
    return pl.pallas_call(
        functools.partial(line_kernel, ready, count),
        in_specs=[vmem] * count,
        out_specs=[vmem] * count,
        out_shape=[jax.ShapeDtypeStruct(p.shape[1:], F32) for p in parts],
        scratch_shapes=[blocks(3, p) for p in late_parts]
        + [blocks(2, p) for p in late_parts]
        + [pltpu.VMEM(p.shape[1:], BF16) for p in parts]
        + [pltpu.SemaphoreType.DMA((count,))] * 6,
        compiler_params=pltpu.CompilerParams(
            collective_id=0, has_side_effects=True, vmem_limit_bytes=56 * 2**20
        ),
        cost_estimate=cost(4 * size, 20 * size),
    )(*parts)


def gated_unit(gate_arg, up_arg):
    return jax.nn.gelu(gate_arg, approximate=True) * up_arg


def layer(n_dp, n_mp):
    lanes = n_dp // 2
    paired = n_dp == 8

    def swap(value, axis, size, bit):
        return lax.ppermute(value, axis, [(i, i ^ bit) for i in range(size)])

    def core(value):
        return swap(value, "mp", n_mp, 1)

    def chip(value):
        return swap(value, "mp", n_mp, 2)

    def beside(value):
        return swap(value, "dp", n_dp, 1)

    def gather(mine):
        far = chip(mine)
        return assemble([mine, far, core(mine), core(far)])

    def gather_after(mine, after):
        return gather(tie(mine, after))

    def scatter_rows(partial):
        step = partial.shape[0] // 4
        block = [partial[k * step : (k + 1) * step] for k in range(4)]
        far = (block[1].astype(F32) + core(block[3]).astype(F32)).astype(BF16)
        far_in = chip(far)
        return block[0].astype(F32) + core(block[2]).astype(F32) + far_in.astype(F32)

    def line_place():
        z = lax.axis_index("dp") // 2
        number = lambda value: jnp.asarray(value).astype(jnp.int32)
        return lax.axis_index("dp") % 2, number(z >= 2), number((z == 1) | (z == 2))

    def outer_swap(value):
        return swap(value, "dp", n_dp, 2)

    def inner_swap(value):
        pairs = []
        for d in range(n_dp):
            for m in range(n_mp):
                inner = d // 2 in (1, 2)
                to = (d ^ 6) * n_mp + m if inner else d * n_mp + (m ^ 1)
                pairs.append((d * n_mp + m, to))
        return lax.ppermute(value, ("dp", "mp"), pairs)

    def lane_columns(parity):
        flip = line_place()[1]
        k = jnp.arange(4, dtype=jnp.int32)
        return 2 * (k + flip * (3 - 2 * k)) + parity

    def split_columns(value):
        if not paired:
            return (value,)
        x = line_place()[0]
        wanted = pick_columns(
            lane_columns(1 - x), value, value.shape[0] // 2, value.shape[1] // n_dp
        )
        low = beside(wanted)
        return value, low, core(low)

    def shards(
        tokens, norm_gains, w_query, w_key, w_value, w_out, c_query, c_key, c_value, c_out,
        patch_proj, w_gate, w_up, w_down, patches, segment_ids, image_index, cotangent,
    ):
        length = segment_ids.shape[1]
        model = tokens.shape[2]
        patch_rows = patches.shape[0] * patches.shape[1]
        m = lax.axis_index("mp")
        order = [m, m ^ 2, m ^ 1, m ^ 3]

        def blocks(arr, axis=0):
            step = arr.shape[axis] // 4
            return jnp.concatenate(
                [lax.dynamic_slice_in_dim(arr, k * step, step, axis) for k in order], axis=axis
            )

        places = blocks(jnp.arange(length, dtype=jnp.int32))
        segment_row = blocks(segment_ids[0])
        slots = jnp.arange(SEGS, dtype=jnp.int32)
        token_image = jnp.sum(
            jnp.where(segment_row[:, None] == slots, image_index[0][None, :], 0), axis=-1
        )
        patch_image = blocks(jnp.arange(patch_rows, dtype=jnp.int32) // patches.shape[1])

        residual = tokens[0].astype(F32)
        normed_one_mine = norm_rows(residual, norm_gains[0])
        normed_one = gather(normed_one_mine)
        patch_own = pick_rows(
            jnp.stack(order).astype(jnp.int32), patches.reshape(patch_rows, patches.shape[2]), patch_rows // 4
        )
        patch_mine = tie(patch_own[: patch_rows // 4], normed_one_mine)
        projected = gather(matmul(patch_mine, patch_proj).astype(BF16))
        queries = matmul(normed_one, w_query).astype(BF16)
        key_rows = matmul(normed_one, w_key).astype(BF16)
        value_rows = matmul(normed_one, w_value).astype(BF16)
        self_allowed = (segment_row[:, None] == segment_row[None, :]) & (
            places[None, :] <= places[:, None]
        )
        cross_allowed = token_image[:, None] == patch_image[None, :]
        self_mixed, self_log = plain_attend(queries, key_rows, value_rows, self_allowed)
        after_self = residual + scatter_rows(matmul(self_mixed, w_out).astype(BF16))
        split_one = split_columns(normed_one)
        cross_keys = matmul(projected, c_key).astype(BF16)
        cross_values = matmul(projected, c_value).astype(BF16)
        normed_two = gather(norm_rows(after_self, norm_gains[1]))
        grad_three = gather_after(cotangent[0], normed_two)
        cross_queries = matmul(normed_two, c_query).astype(BF16)
        cross_mixed, cross_log = plain_attend(
            cross_queries, cross_keys, cross_values, cross_allowed
        )
        split_patch = split_columns(projected)
        cross_mixed = tie(cross_mixed, split_one)
        after_cross = after_self + scatter_rows(matmul(cross_mixed, c_out).astype(BF16))
        split_two = split_columns(normed_two)
        split_cotangent = split_columns(grad_three)
        grad_hidden = tie(product("sd,fd->sf", grad_three, w_down), ())
        normed_three = gather(norm_rows(after_cross, norm_gains[2]))
        normed_three = tie(normed_three, (grad_hidden, split_patch))
        gate_pre, up_pre = matmul(normed_three, w_gate), matmul(normed_three, w_up)
        hidden, pull = jax.vjp(gated_unit, gate_pre, up_pre)
        hidden = hidden.astype(BF16)
        grad_gate, grad_up = [g.astype(BF16) for g in pull(grad_hidden)]

        results, turned = {}, {}

        def line(name, split, grad, grad_far, rows_first, after=()):
            turned[name] = not rows_first
            if not paired:
                partial = product("td,te->de", split[0], grad).astype(BF16)
                total = lax.psum_scatter(partial, "dp", scatter_dimension=0, tiled=True)
                results[name] = total.astype(F32)
                return ()
            results[name] = pair_grad(
                lane_columns(line_place()[0]), *split, grad, grad_far, after
            )
            return (results[name],)

        def line_early(name):
            if paired:
                part = results[name]
                part = merge(part, outer_swap(part[1:]))
                inner = line_place()[2]
                results[name] = cross_add(inner.reshape(1), part, inner_swap(part[2:]))

        far_of = beside if paired else (lambda value: value)
        hidden_far, gate_far, up_far = far_of(hidden), far_of(grad_gate), far_of(grad_up)
        split_three = split_columns(normed_three)
        grad_normed = scatter_rows(
            (
                product("sf,df->sd", grad_gate, w_gate) + product("sf,df->sd", grad_up, w_up)
            ).astype(BF16)
        )
        grad_input, gain_three = norm_back(after_cross, norm_gains[2], grad_normed)
        grad_rows = cotangent[0].astype(F32) + grad_input
        grad_two = gather(grad_rows.astype(BF16))
        sent = line("down", split_cotangent, hidden, hidden_far, False)
        line_early("down")

        grad_two = tie(grad_two, sent)
        grad_mixed = product("sd,ed->se", grad_two, c_out).astype(BF16)
        mixed_far = far_of(cross_mixed)
        grad_cq, grad_ck, grad_cv = plain_back(
            cross_queries, cross_keys, cross_values, cross_allowed, cross_log, grad_mixed
        )
        sent = line("gate", split_three, grad_gate, gate_far, True, sent)
        line_early("gate")
        grad_cq = tie(grad_cq, sent)
        grad_normed = scatter_rows(product("se,de->sd", grad_cq, c_query).astype(BF16))
        grad_input, gain_two = norm_back(after_self, norm_gains[1], grad_normed)
        grad_rows = grad_rows + grad_input
        cq_far, ck_far, cv_far = far_of(grad_cq), far_of(grad_ck), far_of(grad_cv)
        split_grad_two = split_columns(grad_two)
        grad_one = gather(grad_rows.astype(BF16))
        sent = line("up", split_three, grad_up, up_far, True, sent)
        line_early("up")

        grad_one = tie(grad_one, sent)
        grad_mixed = product("sd,ed->se", grad_one, w_out).astype(BF16)
        grad_sq, grad_sk, grad_sv = plain_back(
            queries, key_rows, value_rows, self_allowed, self_log, grad_mixed
        )
        sent = line("c_out", split_grad_two, cross_mixed, mixed_far, False, sent)
        sent = line("c_query", split_two, grad_cq, cq_far, True, sent)
        grad_sq, grad_sk, grad_sv = tie((grad_sq, grad_sk, grad_sv), sent)
        grad_normed = scatter_rows(
            (
                product("se,de->sd", grad_sq, w_query)
                + product("se,de->sd", grad_sk, w_key)
                + product("se,de->sd", grad_sv, w_value)
            ).astype(BF16)
        )
        grad_input, gain_one = norm_back(residual, norm_gains[0], grad_normed)
        grad_rows = grad_rows + grad_input
        sent = line("c_key", split_patch, grad_ck, ck_far, True, sent)
        sent = line("c_value", split_patch, grad_cv, cv_far, True, sent)
        self_far = far_of(self_mixed)
        sq_far, sk_far, sv_far = far_of(grad_sq), far_of(grad_sk), far_of(grad_sv)
        output = after_cross + scatter_rows(matmul(tie(hidden, sent), w_down).astype(BF16))
        sent = line("w_out", split_columns(grad_one), self_mixed, self_far, False, sent)
        sent = line("w_query", split_one, grad_sq, sq_far, True, sent)
        sent = line("w_key", split_one, grad_sk, sk_far, True, sent)
        sent = line("w_value", split_one, grad_sv, sv_far, True, sent)

        width = model // (n_dp * n_mp)

        def projected_block(k):
            def rows_of(weight):
                cut = weight.reshape(n_dp, n_mp, width, weight.shape[1])
                return lax.dynamic_index_in_dim(cut, k, 1, keepdims=False).reshape(
                    n_dp * width, weight.shape[1]
                )

            return (cols_dot(grad_ck, rows_of(c_key)) + cols_dot(grad_cv, rows_of(c_value))).astype(
                BF16
            )

        block = [projected_block(k) for k in order]
        half, quarter = patch_rows // 2, patch_rows // 4
        far = add_swapped(block[1], core(block[3]), half)
        near = add_swapped(block[0], core(block[2]), half)
        grad_projected = add_swapped(near, chip(far), quarter)
        patch_partial = rows_dot(grad_projected, patch_own).astype(BF16)
        if paired:
            x, flip, unused = line_place()
            parts = patch_partial.reshape(4, 2, width, patches.shape[2])
            sent = beside(lax.dynamic_index_in_dim(parts, 1 - x, 1, keepdims=False))
            kept = lax.dynamic_index_in_dim(parts, x, 1, keepdims=False)
            summed = kept.astype(F32) + sent.astype(F32)
            results["patch"] = jnp.where(flip == 1, summed[::-1], summed).astype(BF16)
            early = ["down", "gate", "up"]
            late = ["c_out", "c_query", "c_key", "c_value", "w_out", "w_query", "w_key", "w_value"]
            late.append("patch")
            sums = line_sums([results[n] for n in early], [results[n] for n in late])
            results.update(zip(early + late, sums))
        else:
            results["patch"] = lax.psum_scatter(
                patch_partial, "dp", scatter_dimension=0, tiled=True
            ).astype(F32)
        turned["patch"] = True
        results = {n: v.T if turned[n] else v for n, v in results.items()}
        patch_total = results["patch"]
        gain_total = lax.psum_scatter(
            jnp.stack([gain_one, gain_two, gain_three]),
            ("dp", "mp"), scatter_dimension=1, tiled=True,
        )
        sum_query, sum_key, sum_value = results["w_query"], results["w_key"], results["w_value"]
        sum_cquery, sum_ckey, sum_cvalue = results["c_query"], results["c_key"], results["c_value"]
        sum_out, sum_cout, sum_down = results["w_out"], results["c_out"], results["down"]
        sum_gate, sum_up = results["gate"], results["up"]
        return (
            output.astype(BF16)[None], grad_rows[None], gain_total,
            sum_query, sum_key, sum_value, sum_out,
            sum_cquery, sum_ckey, sum_cvalue, sum_cout,
            patch_total, sum_gate, sum_up, sum_down,
        )

    return shards


def solution(mesh):
    columns, rows = P(None, "mp"), P("mp", None)
    return jax.shard_map(
        layer(mesh.shape["dp"], mesh.shape["mp"]),
        mesh=mesh,
        in_specs=(
            P("dp", "mp", None), P(), columns, columns, columns, rows, columns, columns, columns,
            rows, P(), columns, columns, rows, P("dp", None, None), P("dp", None), P("dp", None),
            P("dp", "mp", None),
        ),
        out_specs=(
            P("dp", "mp", None), P("dp", "mp", None), P(None, ("dp", "mp")),
            P("dp", "mp"), P("dp", "mp"), P("dp", "mp"), P("mp", "dp"),
            P("dp", "mp"), P("dp", "mp"), P("dp", "mp"), P("mp", "dp"),
            P(None, ("dp", "mp")), P("dp", "mp"), P("dp", "mp"), P("mp", "dp"),
        ),
        check_vma=False,
    )
```

```python
import functools

import jax
import jax.numpy as jnp
from jax import lax
from jax.experimental import pallas as pl
from jax.experimental.pallas import tpu as pltpu
from jax.sharding import PartitionSpec as P

HEAD_DIM = 128
SEGS = 4
EPSILON = 1e-06
MASKED = -1000000000.0
F32 = jnp.float32
BF16 = jnp.bfloat16


def matmul(left, right):
    return jnp.dot(left, right, preferred_element_type=F32)


def product(spec, left, right):
    return jnp.einsum(spec, left, right, preferred_element_type=F32)


def rows_dot(left, right):
    return lax.dot_general(left, right, (((0,), (0,)), ((), ())), preferred_element_type=F32)


def cols_dot(left, right):
    return lax.dot_general(left, right, (((1,), (1,)), ((), ())), preferred_element_type=F32)


def tie(value, after):
    return lax.optimization_barrier((value, after))[0]


def inverse_rms(rows):
    return lax.rsqrt(jnp.mean(rows * rows, axis=-1, keepdims=True) + EPSILON)


def norm_rows(rows, gain):
    return (rows * inverse_rms(rows) * gain).astype(BF16)


def norm_back(rows, gain, grad):
    inv = inverse_rms(rows)
    weighted = gain * grad
    inner = jnp.mean(rows * weighted, axis=-1, keepdims=True)
    grad_rows = inv * weighted - rows * (inv * inv * inv) * inner
    return grad_rows, jnp.sum(grad * rows * inv, axis=0)


VMEM_LIMIT = 20 * 2**20
ANY = pl.BlockSpec(memory_space=pl.ANY)


def params(grid_rank):
    return pltpu.CompilerParams(
        dimension_semantics=("arbitrary",) * grid_rank, vmem_limit_bytes=VMEM_LIMIT
    )


def cost(flops, size):
    return pl.CostEstimate(flops=flops, bytes_accessed=size, transcendentals=0)


def masked_scores(q_ref, k_ref, row_ref, col_ref, causal):
    scores = cols_dot(q_ref[...], k_ref[...]) * (HEAD_DIM ** (-0.5))
    allowed = row_ref[:, 0:1] == col_ref[0:1, :]
    if causal:
        allowed = allowed & (col_ref[1:2, :] <= row_ref[:, 1:2])
    return jnp.where(allowed, scores, MASKED)


def attend_kernel(causal, q_ref, k_ref, v_ref, row_ref, col_ref, out_ref):
    scores = masked_scores(q_ref, k_ref, row_ref, col_ref, causal)
    exponent = jnp.exp(scores - jnp.max(scores, axis=-1, keepdims=True))
    total = jnp.sum(exponent, axis=-1, keepdims=True)
    weights = (exponent * (1.0 / total)).astype(BF16)
    out_ref[...] = matmul(weights, v_ref[...]).astype(BF16)


def attend(queries, keys, values, rows, cols, causal):
    length, width = queries.shape
    spots = keys.shape[0]
    head = lambda size: pl.BlockSpec((size, HEAD_DIM), lambda h: (0, h))
    whole = lambda arr: pl.BlockSpec(arr.shape, lambda h: (0, 0))
    return pl.pallas_call(
        functools.partial(attend_kernel, causal),
        grid=(width // HEAD_DIM,),
        in_specs=[head(length), head(spots), head(spots), whole(rows), whole(cols)],
        out_specs=head(length),
        out_shape=jax.ShapeDtypeStruct((length, width), BF16),
        compiler_params=params(1),
        cost_estimate=pl.CostEstimate(
            flops=4 * length * spots * width,
            bytes_accessed=4 * (length + spots) * width,
            transcendentals=length * spots * width // HEAD_DIM,
        ),
    )(queries, keys, values, rows, cols)


def attend_back_kernel(causal, q_ref, k_ref, v_ref, row_ref, col_ref, do_ref, dq_ref, dk_ref, dv_ref):
    scale = HEAD_DIM ** (-0.5)
    scores = masked_scores(q_ref, k_ref, row_ref, col_ref, causal)
    exponent = jnp.exp(scores - jnp.max(scores, axis=-1, keepdims=True))
    weights = exponent * (1.0 / jnp.sum(exponent, axis=-1, keepdims=True))
    grad_weights = cols_dot(do_ref[...], v_ref[...])
    inner = jnp.sum(weights * grad_weights, axis=-1, keepdims=True)
    grad_scores = (weights * (grad_weights - inner)).astype(BF16)
    dq_ref[...] = (matmul(grad_scores, k_ref[...]) * scale).astype(BF16)
    dk_ref[...] = (rows_dot(grad_scores, q_ref[...]) * scale).astype(BF16)
    dv_ref[...] = rows_dot(weights.astype(BF16), do_ref[...]).astype(BF16)


def self_back_kernel(q_ref, k_ref, v_ref, row_ref, col_ref, do_ref, *outs):
    attend_back_kernel(
        True, q_ref, k_ref, v_ref, row_ref, col_ref, do_ref,
        *outs,
    )


def cross_back_kernel(q_ref, k_ref, v_ref, row_ref, col_ref, do_ref, *outs):
    attend_back_kernel(
        False, q_ref, k_ref, v_ref, row_ref, col_ref, do_ref,
        *outs,
    )


def attend_back(queries, keys, values, rows, cols, grad_out, causal):
    length, width = queries.shape
    spots = keys.shape[0]
    head = lambda size: pl.BlockSpec((size, HEAD_DIM), lambda h: (0, h))
    whole = lambda arr: pl.BlockSpec(arr.shape, lambda h: (0, 0))
    sizes = (length, spots, spots)
    out_specs = tuple(head(size) for size in sizes)
    out_shape = tuple(jax.ShapeDtypeStruct((size, width), BF16) for size in sizes)
    return pl.pallas_call(
        self_back_kernel if causal else cross_back_kernel,
        grid=(width // HEAD_DIM,),
        in_specs=[
            head(length), head(spots), head(spots), whole(rows), whole(cols), head(length),
        ],
        out_specs=out_specs,
        out_shape=out_shape,
        compiler_params=params(1),
        cost_estimate=pl.CostEstimate(
            flops=10 * length * spots * width,
            bytes_accessed=8 * (length + spots) * width,
            transcendentals=length * spots * width // HEAD_DIM,
        ),
    )(queries, keys, values, rows, cols, grad_out)


def assemble_kernel(*refs):
    *blocks, out_ref = refs
    step = blocks[0].shape[0]
    for k, block in enumerate(blocks):
        out_ref[k * step : (k + 1) * step] = block[...]


def assemble(blocks):
    step, width = blocks[0].shape
    columns = 512
    return pl.pallas_call(
        assemble_kernel,
        grid=(width // columns,),
        in_specs=[pl.BlockSpec((step, columns), lambda j: (0, j))] * len(blocks),
        out_specs=pl.BlockSpec((len(blocks) * step, columns), lambda j: (0, j)),
        out_shape=jax.ShapeDtypeStruct((len(blocks) * step, width), blocks[0].dtype),
        compiler_params=params(1),
        cost_estimate=cost(0, 4 * len(blocks) * step * width),
    )(*blocks)


def copy_kernel(at_ref, in_ref, out_ref):
    out_ref[...] = in_ref[...]


def pick_rows(at, arr, step):
    count, width = at.shape[0], arr.shape[1]
    return pl.pallas_call(
        copy_kernel,
        grid_spec=pltpu.PrefetchScalarGridSpec(
            num_scalar_prefetch=1,
            grid=(count,),
            in_specs=[pl.BlockSpec((step, width), lambda k, at: (at[k], 0))],
            out_specs=pl.BlockSpec((step, width), lambda k, at: (k, 0)),
        ),
        out_shape=jax.ShapeDtypeStruct((count * step, width), arr.dtype),
        compiler_params=params(1),
        cost_estimate=cost(0, 4 * count * step * width),
    )(at, arr)


def pick_columns(at, arr, rows, width):
    count = at.shape[0]
    return pl.pallas_call(
        copy_kernel,
        grid_spec=pltpu.PrefetchScalarGridSpec(
            num_scalar_prefetch=1,
            grid=(count,),
            in_specs=[pl.BlockSpec((rows, width), lambda k, at: (0, at[k]))],
            out_specs=pl.BlockSpec((rows, width), lambda k, at: (0, k)),
        ),
        out_shape=jax.ShapeDtypeStruct((rows, count * width), arr.dtype),
        compiler_params=params(1),
        cost_estimate=cost(0, 4 * count * rows * width),
    )(at, arr)


def pair_kernel(at_ref, a_ref, lo_ref, hi_ref, g_ref, far_ref, *rest):
    half = lo_ref.shape[0]
    total = rows_dot(a_ref[...], g_ref[...])
    total += rows_dot(lo_ref[...], far_ref[:half])
    total += rows_dot(hi_ref[...], far_ref[half:])
    first_ref, rest_ref = rest[-2:]

    @pl.when(pl.program_id(0) == 0)
    def _():
        first_ref[0] = total.astype(BF16)

    @pl.when(pl.program_id(0) > 0)
    def _():
        rest_ref[0] = total.astype(BF16)


def pair_grad(at, own, low, high, grad, grad_far, after):
    length, units = grad.shape
    width = own.shape[1] // 8
    whole = pl.BlockSpec((length, units), lambda k, at: (0, 0))
    side = pl.BlockSpec((length // 2, width), lambda k, at: (0, k))
    return pl.pallas_call(
        pair_kernel,
        grid_spec=pltpu.PrefetchScalarGridSpec(
            num_scalar_prefetch=1,
            grid=(4,),
            in_specs=[
                pl.BlockSpec((length, width), lambda k, at: (0, at[k])), side, side, whole, whole,
            ] + [ANY] * len(after),
            out_specs=(
                pl.BlockSpec((1, width, units), lambda k, at: (0, 0, 0)),
                pl.BlockSpec((1, width, units), lambda k, at: (jnp.maximum(k - 1, 0), 0, 0)),
            ),
        ),
        out_shape=tuple(jax.ShapeDtypeStruct((n, width, units), BF16) for n in (1, 3)),
        compiler_params=params(1),
        cost_estimate=cost(
            16 * length * width * units, 2 * units * (2 * length + 4 * width) + 16 * length * width
        ),
    )(at, own, low, high, grad, grad_far, *after)


def merge_kernel(left_ref, right_ref, *rest):
    rest[-1][...] = (left_ref[...].astype(F32) + right_ref[...].astype(F32)).astype(BF16)


def merge(left, right, after):
    spec = pl.BlockSpec((1,) + left.shape[1:], lambda k: (k, 0, 0))
    return pl.pallas_call(
        merge_kernel,
        grid=(left.shape[0],),
        in_specs=[spec, spec] + [ANY] * len(after),
        out_specs=spec,
        out_shape=jax.ShapeDtypeStruct(left.shape, BF16),
        compiler_params=params(1),
        cost_estimate=cost(left.size, 6 * left.size),
    )(left, right, *after)


def cross_kernel(at_ref, first_ref, rest_ref, in_ref, out_ref):
    part = jnp.where(pl.program_id(0) == 0, first_ref[...], rest_ref[...]).astype(F32)
    keep = jnp.where(at_ref[0] == 1, in_ref[...].astype(F32), 0.0)
    out_ref[...] = (part + keep).astype(BF16)


def cross_add(inner, first, rest, crossed):
    block = (1,) + rest.shape[1:]
    here = pl.BlockSpec(block, lambda k, at: (0, 0, 0))
    return pl.pallas_call(
        cross_kernel,
        grid_spec=pltpu.PrefetchScalarGridSpec(
            num_scalar_prefetch=1,
            grid=(2,),
            in_specs=[here, here, pl.BlockSpec(block, lambda k, at: (1 - k, 0, 0))],
            out_specs=pl.BlockSpec(block, lambda k, at: (k, 0, 0)),
        ),
        out_shape=jax.ShapeDtypeStruct((2,) + rest.shape[1:], BF16),
        compiler_params=params(1),
        cost_estimate=cost(crossed.size, 6 * crossed.size),
    )(inner, first, rest, crossed)


def add_rows(target, *sources):
    step = 32

    def body(i, carry):
        rows = pl.ds(pl.multiple_of(i * step, step), step)
        total = sources[0][rows].astype(F32)
        for source in sources[1:]:
            total = total + source[rows].astype(F32)
        target[rows] = total.astype(target.dtype)
        return carry

    lax.fori_loop(0, target.shape[0] // step, body, 0)


def line_kernel(ready, merged, count, pairs, *refs):
    refs = list(refs)
    take = lambda size: [refs.pop(0) for unused in range(size)]
    total = count + pairs
    first = take(count)
    rest = dict(zip(range(ready, count), take(count - ready)))
    grads, [own, low, high] = take(pairs), take(3)
    outs = take(total)
    late = range(ready + merged, total)
    open_ends = range(ready, total)
    first += take(pairs)
    rest.update(zip(range(count, total), take(pairs)))
    far = take(pairs)
    from_outer = dict(zip(late, take(len(late))))
    from_inner = dict(zip(open_ends, take(len(open_ends))))
    last = take(total)
    send_out, got_out, send_in, got_in, send_last, got_last, send_x, got_x = refs
    dp, mp = lax.axis_index("dp"), lax.axis_index("mp")
    z, x = dp // 2, dp % 2
    beside = ((z + 1 - 2 * (z % 2)) * 2 + x, mp)
    across = ((3 - z) * 2 + x, mp)
    partner = (z * 2 + 1 - x, mp)
    flip = z // 2
    inner = (z == 1) | (z == 2)
    outer = (z == 0) | (z == 3)
    mesh_id = pl.DeviceIdType.MESH
    barrier = pltpu.get_barrier_semaphore()
    for device in (beside, partner):
        pl.semaphore_signal(barrier, inc=1, device_id=device, device_id_type=mesh_id)

    def copy(source, target, sent, got, device):
        return pltpu.make_async_remote_copy(
            src_ref=source, dst_ref=target, send_sem=sent, recv_sem=got,
            device_id=device, device_id_type=mesh_id,
        )

    def copy_out(g):
        return copy(rest[g], from_outer[g], send_out.at[g], got_out.at[g], beside)

    def copy_in(g):
        source = (from_outer if g in late else rest)[g].at[pl.ds(1, 2)]
        return copy(source, from_inner[g], send_in.at[g], got_in.at[g], across)

    def copy_last(g):
        source = first[g].at[0] if g < ready else from_inner[g].at[1]
        return copy(source, last[g], send_last.at[g], got_last.at[g], beside)

    def copy_grad(p):
        return copy(grads[p], far[p], send_x.at[p], got_x.at[p], partner)

    def multiply(p):
        copy_grad(p).wait_recv()
        half, width = low.shape[0], first[count + p].shape[1]

        def body(k, carry):
            lane = k + flip * (3 - 2 * k)
            at = pl.ds(pl.multiple_of((2 * lane + x) * width, width), width)
            side = pl.ds(pl.multiple_of(k * width, width), width)
            value = rows_dot(own[:, at], grads[p][...])
            value += rows_dot(low[:, side], far[p][:half])
            value += rows_dot(high[:, side], far[p][half:])

            @pl.when(k == 0)
            def _():
                first[count + p][0] = value.astype(BF16)

            @pl.when(k > 0)
            def _():
                rest[count + p][jnp.maximum(k - 1, 0)] = value.astype(BF16)

            return carry

        lax.fori_loop(0, 4, body, 0)

    large = [g for g in late if g < count and first[g].shape[1] >= 256]
    small = [g for g in late if g < count and first[g].shape[1] < 256]
    sequence = large + list(range(count, total)) + small

    @pl.when(outer)
    def _():
        pl.semaphore_wait(barrier, 2)
        for p in range(pairs):
            copy_grad(p).start()
        for g in sequence:
            if g >= count:
                multiply(g - count)
            copy_out(g).start()
        for g in list(range(ready + merged)) + sequence:
            copy_last(g).wait_recv()
            add_rows(outs[g], first[g].at[0], last[g])
        for g in late:
            copy_out(g).wait_send()

    @pl.when(inner)
    def _():
        pl.semaphore_signal(barrier, inc=1, device_id=across, device_id_type=mesh_id)
        pl.semaphore_wait(barrier, 3)
        for p in range(pairs):
            copy_grad(p).start()
        for g in range(ready):
            copy_last(g).start()
        for g in range(ready, ready + merged):
            copy_in(g).start()

        def begin(g):
            copy_out(g).wait_recv()
            for k in (1, 2):
                add_rows(from_outer[g].at[k], rest[g].at[k], from_outer[g].at[k])
            copy_in(g).start()

        def finish(g):
            copy_in(g).wait_recv()
            add_rows(from_inner[g].at[1], first[g].at[0], from_inner[g].at[1])
            copy_last(g).start()
            near = [from_outer[g].at[0]] if g in late else []
            add_rows(outs[g], rest[g].at[0], from_inner[g].at[0], *near)

        for g in range(ready):
            add_rows(outs[g], first[g].at[1])
        waiting = list(range(ready, ready + merged))
        for g in sequence:
            if g >= count:
                multiply(g - count)
            begin(g)
            waiting.append(g)
            if len(waiting) > 1:
                finish(waiting.pop(0))
        for g in waiting:
            finish(g)
        for g in open_ends:
            copy_in(g).wait_send()
        for g in range(total):
            copy_last(g).wait_send()

    for p in range(pairs):
        copy_grad(p).wait_send()


def line_sums(ready_parts, merged_parts, late_parts, grads, own, low, high):
    open_parts = list(merged_parts) + list(late_parts)
    parts = list(ready_parts) + [first for first, unused in open_parts]
    rests = [rest for unused, rest in open_parts]
    ready, merged, count, pairs = len(ready_parts), len(merged_parts), len(parts), len(grads)
    width = own.shape[1] // 8
    shapes = [p.shape[1:] for p in parts] + [(width, g.shape[1]) for g in grads]
    total, late = count + pairs, shapes[ready + merged :]
    assert ready + merged <= count and merged <= 1
    vmem = pl.BlockSpec(memory_space=pltpu.VMEM)
    sizes = [r * k for r, k in shapes]
    return pl.pallas_call(
        functools.partial(line_kernel, ready, merged, count, pairs),
        in_specs=[vmem] * (count + len(rests) + pairs + 3),
        out_specs=[vmem] * total,
        out_shape=[jax.ShapeDtypeStruct(shape, F32) for shape in shapes],
        scratch_shapes=[pltpu.VMEM((n,) + shape, BF16) for n in (1, 3) for shape in shapes[count:]]
        + [pltpu.VMEM(g.shape, BF16) for g in grads]
        + [pltpu.VMEM((3,) + shape, BF16) for shape in late]
        + [pltpu.VMEM((2,) + shape, BF16) for shape in shapes[ready:]]
        + [pltpu.VMEM(shape, BF16) for shape in shapes]
        + [pltpu.SemaphoreType.DMA((total,))] * 6
        + [pltpu.SemaphoreType.DMA((pairs,))] * 2,
        compiler_params=pltpu.CompilerParams(
            collective_id=0, has_side_effects=True, vmem_limit_bytes=56 * 2**20
        ),
        cost_estimate=cost(4 * sum(sizes), 40 * sum(sizes)),
    )(*parts, *rests, *grads, own, low, high)


CHUNKS = 4


def boundary_kernel(mode, jobs, plain, partial, rows, kept, gain, *refs):
    refs = list(refs)
    take = lambda size: [refs.pop(0) for unused in range(size)]
    wanted = take(jobs)
    [sums] = take(1) if mode != "first" else [None]
    [gathered] = take(1) if mode not in ("last", "sum") else [None]
    [gain_out] = take(1) if mode in ("backward", "last") else [None]
    [kept_out] = take(1) if mode == "sum" else [None]
    low_out, high_out = take(jobs), take(0 if plain else jobs)
    from_core, far_sum, from_chip, whole = take(4)
    low, high = take(jobs), take(0 if plain else jobs)
    sends, gots = take(2)
    if jobs:
        send_jobs, got_jobs = take(2)
    if mode == "sum":
        running, others, send_kept, got_kept = take(4)
    dp, mp = lax.axis_index("dp"), lax.axis_index("mp")
    core = (dp, mp + 1 - 2 * (mp % 2))
    chip = (dp, (mp + 2) % 4)
    mesh_id = pl.DeviceIdType.MESH
    step = rows.shape[0]
    size = step // CHUNKS
    barrier = pltpu.get_barrier_semaphore()
    beside = (dp + 1 - 2 * (dp % 2), mp)
    near = (core, chip, beside) if jobs or mode == "sum" else (core, chip)
    for device in near:
        pl.semaphore_signal(barrier, inc=1, device_id=device, device_id_type=mesh_id)
    pl.semaphore_wait(barrier, len(near))

    def job(hop, k):
        source, target = ((wanted, low), (low, high))[hop]
        return pltpu.make_async_remote_copy(
            src_ref=source[k], dst_ref=target[k], send_sem=send_jobs.at[hop, k],
            recv_sem=got_jobs.at[hop, k], device_id=(beside, core)[hop], device_id_type=mesh_id,
        )

    for k in range(jobs):
        job(0, k).start()

    def copy(kind, c, source, target, device):
        return pltpu.make_async_remote_copy(
            src_ref=source, dst_ref=target, send_sem=sends.at[kind, c], recv_sem=gots.at[kind, c],
            device_id=device, device_id_type=mesh_id,
        )

    def part(block, c):
        return pl.ds(block * step + c * size, size)

    def core_sum(block, c):
        return copy(
            block, c, partial.at[part(2 + block, c)], from_core.at[part(block, c)], core
        )

    def chip_sum(c):
        return copy(2, c, far_sum.at[part(0, c)], from_chip.at[part(0, c)], chip)

    def chip_row(c):
        return copy(3, c, whole.at[part(0, c)], whole.at[part(1, c)], chip)

    def core_row(block, c):
        return copy(
            4 + block, c, whole.at[part(block, c)], whole.at[part(2 + block, c)], core
        )

    every = range(CHUNKS)
    wide = lambda value: value.astype(F32)
    if mode != "first":
        for block in (1, 0):
            for c in every:
                core_sum(block, c).start()
        for c in every:
            core_sum(1, c).wait_recv()
            total = wide(partial[part(1, c)]) + wide(from_core[part(1, c)])
            far_sum[part(0, c)] = total.astype(BF16)
            chip_sum(c).start()
    if gain_out is not None:
        gain_out[...] = jnp.zeros_like(gain_out)
    for c in every:
        here = part(0, c)
        if mode == "first":
            value = wide(rows[here])
        else:
            core_sum(0, c).wait_recv()
            chip_sum(c).wait_recv()
            total = wide(partial[here]) + wide(from_core[here]) + wide(from_chip[here])
            if mode in ("forward", "sum"):
                value = wide(rows[here]) + total
                sums[here] = value
            else:
                old = kept[here]
                inv = inverse_rms(old)
                weighted = gain[...] * total
                inner = jnp.mean(old * weighted, axis=-1, keepdims=True)
                value = wide(rows[here]) + inv * weighted - old * (inv * inv * inv) * inner
                gain_out[...] += jnp.sum(total * old * inv, axis=0, keepdims=True)
                sums[here] = value
        if gathered is not None:
            if mode != "backward":
                value = value * inverse_rms(value) * gain[...]
            whole[here] = value.astype(BF16)
            chip_row(c).start()
            core_row(0, c).start()
    if gathered is not None:
        for c in every:
            chip_row(c).wait_recv()
            core_row(1, c).start()
        for c in every:
            for block in range(2):
                core_row(block, c).wait_recv()
        gathered[...] = whole[...]
    if mode == "sum":
        running[...] = kept[...]
        hops = []
        for k, device in enumerate((core, chip, beside)):
            hop = pltpu.make_async_remote_copy(
                src_ref=running, dst_ref=others.at[k], send_sem=send_kept.at[k],
                recv_sem=got_kept.at[k], device_id=device, device_id_type=mesh_id,
            )
            hop.start()
            hop.wait()
            running[...] = running[...] + others[k]
        kept_out[...] = running[...]
    for k in range(jobs):
        job(0, k).wait_recv()
        if not plain:
            job(1, k).start()
        low_out[k][...] = low[k][...]
    for k in range(jobs):
        job(0, k).wait_send()
        if not plain:
            job(1, k).wait_recv()
            high_out[k][...] = high[k][...]
            job(1, k).wait_send()
    for c in every:
        if mode != "first":
            core_sum(0, c).wait_send()
            core_sum(1, c).wait_send()
            chip_sum(c).wait_send()
        if gathered is not None:
            chip_row(c).wait_send()
            core_row(0, c).wait_send()
            core_row(1, c).wait_send()


def boundary(mode, number, partial, rows, kept, gain, wanted=(), plain=False):
    step, width = rows.shape
    vmem = pl.BlockSpec(memory_space=pltpu.VMEM)
    shapes = []
    if mode != "first":
        shapes.append(jax.ShapeDtypeStruct((step, width), F32))
    if mode not in ("last", "sum"):
        shapes.append(jax.ShapeDtypeStruct((4 * step, width), BF16))
    if mode in ("backward", "last"):
        shapes.append(jax.ShapeDtypeStruct((1, width), F32))
    if mode == "sum":
        shapes.append(jax.ShapeDtypeStruct(kept.shape, F32))
    jobs = len(wanted)
    hops = 1 if plain else 2
    shapes += [jax.ShapeDtypeStruct(w.shape, BF16) for w in wanted] * hops
    scratch = [pltpu.VMEM(w.shape, BF16) for w in wanted] * hops
    outs = pl.pallas_call(
        functools.partial(boundary_kernel, mode, jobs, plain),
        in_specs=[vmem] * (4 + jobs),
        out_specs=[vmem] * len(shapes),
        out_shape=shapes,
        scratch_shapes=[
            pltpu.VMEM((2 * step, width), BF16),
            pltpu.VMEM((step, width), BF16),
            pltpu.VMEM((step, width), BF16),
            pltpu.VMEM((4 * step, width), BF16),
        ]
        + scratch
        + [pltpu.SemaphoreType.DMA((6, CHUNKS))] * 2
        + ([pltpu.SemaphoreType.DMA((2, jobs))] * 2 if jobs else [])
        + (
            [pltpu.VMEM(kept.shape, F32), pltpu.VMEM((3,) + kept.shape, F32)]
            + [pltpu.SemaphoreType.DMA((3,))] * 2
            if mode == "sum"
            else []
        ),
        compiler_params=pltpu.CompilerParams(
            collective_id=number, has_side_effects=True, vmem_limit_bytes=2 * VMEM_LIMIT
        ),
        cost_estimate=cost(10 * step * width, 60 * 2**20),
    )(partial, rows, kept, gain, *wanted)
    if not jobs or plain:
        return outs
    halves = list(zip(outs[-2 * jobs : -jobs], outs[-jobs:]))
    return list(outs[: -2 * jobs]) + halves


def gated_unit(gate_arg, up_arg):
    return jax.nn.gelu(gate_arg, approximate=True) * up_arg


def layer(n_dp, n_mp):
    lanes = n_dp // 2
    paired = n_dp == 8

    def swap(value, axis, size, bit):
        return lax.ppermute(value, axis, [(i, i ^ bit) for i in range(size)])

    def core(value):
        return swap(value, "mp", n_mp, 1)

    def chip(value):
        return swap(value, "mp", n_mp, 2)

    def beside(value):
        return swap(value, "dp", n_dp, 1)

    def gather(mine):
        far = chip(mine)
        return assemble([mine, far, core(mine), core(far)])

    def gather_after(mine, after):
        return gather(tie(mine, after))

    def scatter_rows(partial):
        step = partial.shape[0] // 4
        block = [partial[k * step : (k + 1) * step] for k in range(4)]
        far = (block[1].astype(F32) + core(block[3]).astype(F32)).astype(BF16)
        far_in = chip(far)
        return block[0].astype(F32) + core(block[2]).astype(F32) + far_in.astype(F32)

    def line_place():
        z = lax.axis_index("dp") // 2
        number = lambda value: jnp.asarray(value).astype(jnp.int32)
        return lax.axis_index("dp") % 2, number(z >= 2), number((z == 1) | (z == 2))

    def outer_swap(value):
        return swap(value, "dp", n_dp, 2)

    def inner_swap(value):
        pairs = []
        for d in range(n_dp):
            for m in range(n_mp):
                inner = d // 2 in (1, 2)
                to = (d ^ 6) * n_mp + m if inner else d * n_mp + (m ^ 1)
                pairs.append((d * n_mp + m, to))
        return lax.ppermute(value, ("dp", "mp"), pairs)

    def lane_columns(parity):
        flip = line_place()[1]
        k = jnp.arange(4, dtype=jnp.int32)
        return 2 * (k + flip * (3 - 2 * k)) + parity

    def wanted_of(value, half=None):
        rows = value.shape[0] // 2
        if half is not None:
            value = pick_rows(jnp.stack([half]).astype(jnp.int32), value, rows)
        x = line_place()[0]
        return pick_columns(lane_columns(1 - x), value, rows, value.shape[1] // n_dp)

    def shards(
        tokens, norm_gains, w_query, w_key, w_value, w_out, c_query, c_key, c_value, c_out,
        patch_proj, w_gate, w_up, w_down, patches, segment_ids, image_index, cotangent,
    ):
        length = segment_ids.shape[1]
        model = tokens.shape[2]
        patch_rows = patches.shape[0] * patches.shape[1]
        m = lax.axis_index("mp")
        order = [m, m ^ 2, m ^ 1, m ^ 3]

        def blocks(arr, axis=0):
            step = arr.shape[axis] // 4
            return jnp.concatenate(
                [lax.dynamic_slice_in_dim(arr, k * step, step, axis) for k in order], axis=axis
            )

        places = blocks(jnp.arange(length, dtype=jnp.int32))
        segment_row = blocks(segment_ids[0])
        slots = jnp.arange(SEGS, dtype=jnp.int32)
        token_image = jnp.sum(
            jnp.where(segment_row[:, None] == slots, image_index[0][None, :], 0), axis=-1
        )
        patch_image = jnp.arange(patch_rows, dtype=jnp.int32) // patches.shape[1]

        far_of = beside if paired else (lambda value: value)
        core_bit = m % 2

        def exchange(*values):
            return [wanted_of(*value) for value in values] if paired else []

        def split(value, halves):
            return (value, *halves) if paired else (value,)

        def split_now(value):
            if not paired:
                return (value,)
            wanted = wanted_of(value)
            low = beside(wanted)
            return value, low, core(low)

        self_rows = jnp.stack([segment_row, places], axis=1)
        self_cols = self_rows.T
        cross_rows, cross_cols = token_image[:, None], patch_image[None, :]
        residual = tokens[0].astype(F32)
        gain_rows = [norm_gains[k : k + 1] for k in range(3)]
        nothing = jnp.zeros((16, 128), BF16)
        none = [None] * 4
        [normed_one] = boundary("first", 1, nothing, tokens[0], nothing, gain_rows[0])
        patch_own = patches.reshape(patch_rows, patches.shape[2])
        projected = matmul(patch_own, patch_proj).astype(BF16)
        queries = matmul(normed_one, w_query).astype(BF16)
        key_rows = matmul(normed_one, w_key).astype(BF16)
        value_rows = matmul(normed_one, w_value).astype(BF16)
        self_mixed = attend(queries, key_rows, value_rows, self_rows, self_cols, True)
        self_far = far_of(self_mixed)
        grad_three = gather_after(cotangent[0], normed_one)
        split_one = split_now(normed_one)
        self_mixed = tie(self_mixed, (grad_three, split_one))
        partial = matmul(self_mixed, w_out).astype(BF16)
        after_self, normed_two, *halves = boundary(
            "forward", 2, partial, tokens[0], nothing, gain_rows[1], exchange((projected, core_bit), (grad_three,))
        )
        patch_low, patch_high = halves[0] if paired else (None, None)
        [split_cotangent] = map(split, (grad_three,), halves[1:] or none)
        normed_two = tie(normed_two, self_far)
        cross_keys = matmul(projected, c_key).astype(BF16)
        cross_values = matmul(projected, c_value).astype(BF16)
        cross_queries = matmul(normed_two, c_query).astype(BF16)
        cross_mixed = attend(
            cross_queries, cross_keys, cross_values, cross_rows, cross_cols, False
        )
        mixed_far = far_of(cross_mixed)
        partial = matmul(cross_mixed, c_out).astype(BF16)
        after_cross, normed_three, *halves = boundary(
            "forward", 3, partial, after_self, nothing, gain_rows[2],
            exchange((normed_two,)),
        )
        [split_two] = map(split, (normed_two,), halves or none)
        grad_hidden = tie(product("sd,fd->sf", grad_three, w_down), ())
        if paired:
            wanted = wanted_of(normed_three)
            low_three = beside(wanted)
            split_three = normed_three, low_three, core(low_three)
            normed_three = tie(normed_three, (grad_hidden, mixed_far, wanted))
        else:
            split_three, low_three = (normed_three,), normed_three
        gate_pre, up_pre = matmul(normed_three, w_gate), matmul(normed_three, w_up)
        hidden, pull = jax.vjp(gated_unit, gate_pre, up_pre)
        hidden = hidden.astype(BF16)
        grad_gate, grad_up = [g.astype(BF16) for g in pull(grad_hidden)]

        results, turned = {}, {}

        def line(name, split, grad, grad_far, rows_first, after=()):
            turned[name] = not rows_first
            if not paired:
                partial = product("td,te->de", split[0], grad).astype(BF16)
                total = lax.psum_scatter(partial, "dp", scatter_dimension=0, tiled=True)
                results[name] = total.astype(F32)
                return ()
            results[name] = pair_grad(
                lane_columns(line_place()[0]), *split, grad, grad_far, after
            )
            return results[name]

        def line_out(name):
            return outer_swap(results[name][1]) if paired else None

        def line_merge(name, incoming, after):
            if paired:
                first, rest = results[name]
                results[name] = first, merge(rest, incoming, after)

        def line_across(name):
            if paired:
                inner = line_place()[2]
                first, rest = results[name]
                results[name] = cross_add(inner.reshape(1), first, rest, inner_swap(rest[1:]))

        hidden_far = far_of(tie(hidden, low_three))
        partial = (
            product("sf,df->sd", grad_gate, w_gate) + product("sf,df->sd", grad_up, w_up)
        ).astype(BF16)
        gate_far, up_far = [far_of(v) for v in tie((grad_gate, grad_up), partial)]
        sent = line("down", split_cotangent, hidden, hidden_far, False, (partial,))
        incoming_down = line_out("down")
        grad_rows, grad_two, gain_three = boundary(
            "backward", 4, tie(partial, sent), cotangent[0], after_cross, gain_rows[2]
        )
        sent = line("gate", split_three, grad_gate, gate_far, True, (grad_two,))
        incoming_gate = line_out("gate")
        grad_two = tie(grad_two, sent)

        grad_mixed = product("sd,ed->se", grad_two, c_out).astype(BF16)
        grad_cq, grad_ck, grad_cv = attend_back(
            cross_queries, cross_keys, cross_values, cross_rows, cross_cols, grad_mixed, False
        )
        cq_far, ck_far, cv_far = far_of(grad_cq), far_of(grad_ck), far_of(grad_cv)
        partial = product("se,de->sd", grad_cq, c_query).astype(BF16)
        sent = line("up", split_three, grad_up, up_far, True, (partial,))
        incoming_up = line_out("up")
        line_merge("down", incoming_down, (partial,))
        grad_rows, grad_one, gain_two = boundary(
            "backward", 5, tie(partial, (sent, results["down"])), grad_rows, after_self, gain_rows[1]
        )
        line_across("down")

        grad_mixed = product("sd,ed->se", grad_one, w_out).astype(BF16)
        grad_sq, grad_sk, grad_sv = attend_back(
            queries, key_rows, value_rows, self_rows, self_cols, grad_mixed, True
        )
        partial = (
            product("se,de->sd", grad_sq, w_query)
            + product("se,de->sd", grad_sk, w_key)
            + product("se,de->sd", grad_sv, w_value)
        ).astype(BF16)
        width = model // (n_dp * n_mp)

        def projected_block(k):
            def rows_of(weight):
                cut = weight.reshape(n_dp, n_mp, width, weight.shape[1])
                return lax.dynamic_index_in_dim(cut, k, 1, keepdims=False).reshape(
                    n_dp * width, weight.shape[1]
                )

            return (cols_dot(late_ck, rows_of(c_key)) + cols_dot(late_cv, rows_of(c_value))).astype(
                BF16
            )

        late_ck, late_cv = tie((grad_ck, grad_cv), grad_one)
        block = [projected_block(k) for k in order]
        far = (block[1].astype(F32) + core(block[3]).astype(F32)).astype(BF16)
        near = (block[0].astype(F32) + core(block[2]).astype(F32)).astype(BF16)
        far_in = chip(far)
        line_merge("gate", incoming_gate, (partial,))
        line("c_query", split_two, grad_cq, cq_far, True, (partial,))
        split_patch = (projected,)
        if paired:
            swapped = core_bit == 1
            split_patch = (
                projected,
                jnp.where(swapped, patch_high, patch_low),
                jnp.where(swapped, patch_low, patch_high),
            )
        sent = line("c_key", split_patch, grad_ck, ck_far, True, (partial,))
        grad_rows, gain_one, *halves = boundary(
            "last", 6, tie(partial, (sent, far, near, results["gate"], results["down"])), grad_rows,
            residual, gain_rows[0], exchange((grad_two,), (grad_one,)),
        )
        line_across("gate")
        split_grad_two, split_grad_one = map(split, (grad_two, grad_one), halves or none)
        grad_projected = (near.astype(F32) + far_in.astype(F32)).astype(BF16)
        patch_partial = rows_dot(grad_projected, patch_own).astype(BF16)
        x, flip, unused = line_place()
        patch_parts = patch_partial.reshape(n_dp // 2, 2, width, patches.shape[2])
        patch_sent = lax.dynamic_index_in_dim(patch_parts, 1 - x, 1, keepdims=False)
        partial = matmul(tie(hidden, grad_rows), w_down).astype(BF16)
        gains = jnp.concatenate([gain_one, gain_two, gain_three], axis=0)
        gains_wide = jnp.pad(gains, ((0, 5), (0, 0)))
        output, gains_near, *patch_got = boundary(
            "sum", 7, partial, after_cross, gains_wide, gain_rows[0],
            [patch_sent.reshape(-1, patches.shape[2])] if paired else [], True,
        )
        line("c_value", split_patch, grad_cv, cv_far, True, (grad_rows,))
        line("c_out", split_grad_two, cross_mixed, mixed_far, False, (grad_rows,))
        line("w_out", split_grad_one, self_mixed, self_far, False, (grad_rows,))
        line_merge("up", incoming_up, (grad_rows,))
        if paired:
            kept = lax.dynamic_index_in_dim(patch_parts, x, 1, keepdims=False)
            summed = kept.astype(F32) + patch_got[0].reshape(kept.shape).astype(F32)
            summed = jnp.where(flip == 1, summed[::-1], summed).astype(BF16)
            results["patch"] = summed[:1], summed[1:]
            mine = lax.dynamic_index_in_dim(
                gains_near[:3].reshape(3, 4, 2, n_mp, width), x, 2, keepdims=False
            )
            mine = lax.dynamic_index_in_dim(mine, m, 2, keepdims=False).transpose(1, 0, 2)
            mine = jnp.where(flip == 1, mine[::-1], mine)
            mine = jnp.pad(mine, ((0, 0), (0, 29), (0, 128 - width))).astype(BF16)
            results["gains"] = mine[:1], mine[1:]
            early, late = ["down", "gate", "up"], ["c_out", "c_query", "c_key", "c_value", "w_out"]
            late += ["patch", "gains"]
            names = early + late + ["w_query", "w_key", "w_value"]
            sums = line_sums(
                [results["down"], results["gate"]], [results["up"]], [results[n] for n in late],
                [grad_sq, grad_sk, grad_sv], *split_one,
            )
            results.update(zip(names, sums))
        else:
            results["patch"] = lax.psum_scatter(
                patch_partial, "dp", scatter_dimension=0, tiled=True
            ).astype(F32)
            line("w_query", split_one, grad_sq, grad_sq, True)
            line("w_key", split_one, grad_sk, grad_sk, True)
            line("w_value", split_one, grad_sv, grad_sv, True)
        turned["patch"] = True
        results = {n: v.T if turned.get(n) else v for n, v in results.items()}
        patch_total = results["patch"]
        if paired:
            gain_total = results["gains"][:3, :width]
        else:
            gain_total = lax.psum_scatter(
                gains, ("dp", "mp"), scatter_dimension=1, tiled=True,
            )
        sum_query, sum_key, sum_value = results["w_query"], results["w_key"], results["w_value"]
        sum_cquery, sum_ckey, sum_cvalue = results["c_query"], results["c_key"], results["c_value"]
        sum_out, sum_cout, sum_down = results["w_out"], results["c_out"], results["down"]
        sum_gate, sum_up = results["gate"], results["up"]
        return (
            output.astype(BF16)[None], grad_rows[None], gain_total,
            sum_query, sum_key, sum_value, sum_out,
            sum_cquery, sum_ckey, sum_cvalue, sum_cout,
            patch_total, sum_gate, sum_up, sum_down,
        )

    return shards


def solution(mesh):
    columns, rows = P(None, "mp"), P("mp", None)
    return jax.shard_map(
        layer(mesh.shape["dp"], mesh.shape["mp"]),
        mesh=mesh,
        in_specs=(
            P("dp", "mp", None), P(), columns, columns, columns, rows, columns, columns, columns,
            rows, P(), columns, columns, rows, P("dp", None, None), P("dp", None), P("dp", None),
            P("dp", "mp", None),
        ),
        out_specs=(
            P("dp", "mp", None), P("dp", "mp", None), P(None, ("dp", "mp")),
            P("dp", "mp"), P("dp", "mp"), P("dp", "mp"), P("mp", "dp"),
            P("dp", "mp"), P("dp", "mp"), P("dp", "mp"), P("mp", "dp"),
            P(None, ("dp", "mp")), P("dp", "mp"), P("dp", "mp"), P("mp", "dp"),
        ),
        check_vma=False,
    )
```

```python
import functools

import jax
import jax.numpy as jnp
from jax import lax
from jax.experimental import pallas as pl
from jax.experimental.pallas import tpu as pltpu
from jax.sharding import PartitionSpec as P

HEAD_DIM = 128
SEGS = 4
EPSILON = 1e-06
MASKED = -1000000000.0
F32 = jnp.float32
BF16 = jnp.bfloat16


def matmul(left, right):
    return jnp.dot(left, right, preferred_element_type=F32)


def product(spec, left, right):
    return jnp.einsum(spec, left, right, preferred_element_type=F32)


def rows_dot(left, right):
    return lax.dot_general(left, right, (((0,), (0,)), ((), ())), preferred_element_type=F32)


def cols_dot(left, right):
    return lax.dot_general(left, right, (((1,), (1,)), ((), ())), preferred_element_type=F32)


def tie(value, after):
    return lax.optimization_barrier((value, after))[0]


def inverse_rms(rows):
    return lax.rsqrt(jnp.mean(rows * rows, axis=-1, keepdims=True) + EPSILON)


def norm_rows(rows, gain):
    return (rows * inverse_rms(rows) * gain).astype(BF16)


def norm_back(rows, gain, grad):
    inv = inverse_rms(rows)
    weighted = gain * grad
    inner = jnp.mean(rows * weighted, axis=-1, keepdims=True)
    grad_rows = inv * weighted - rows * (inv * inv * inv) * inner
    return grad_rows, jnp.sum(grad * rows * inv, axis=0)


VMEM_LIMIT = 20 * 2**20
ANY = pl.BlockSpec(memory_space=pl.ANY)


def params(grid_rank):
    return pltpu.CompilerParams(
        dimension_semantics=("arbitrary",) * grid_rank, vmem_limit_bytes=VMEM_LIMIT
    )


def cost(flops, size):
    return pl.CostEstimate(flops=flops, bytes_accessed=size, transcendentals=0)


def masked_scores(q_ref, k_ref, row_ref, col_ref, causal):
    scores = cols_dot(q_ref[...], k_ref[...]) * (HEAD_DIM ** (-0.5))
    allowed = row_ref[:, 0:1] == col_ref[0:1, :]
    if causal:
        allowed = allowed & (col_ref[1:2, :] <= row_ref[:, 1:2])
    return jnp.where(allowed, scores, MASKED)


def attend_kernel(causal, q_ref, k_ref, v_ref, row_ref, col_ref, out_ref):
    scores = masked_scores(q_ref, k_ref, row_ref, col_ref, causal)
    exponent = jnp.exp(scores - jnp.max(scores, axis=-1, keepdims=True))
    total = jnp.sum(exponent, axis=-1, keepdims=True)
    weights = (exponent * (1.0 / total)).astype(BF16)
    out_ref[...] = matmul(weights, v_ref[...]).astype(BF16)


def attend(queries, keys, values, rows, cols, causal):
    length, width = queries.shape
    spots = keys.shape[0]
    head = lambda size: pl.BlockSpec((size, HEAD_DIM), lambda h: (0, h))
    whole = lambda arr: pl.BlockSpec(arr.shape, lambda h: (0, 0))
    return pl.pallas_call(
        functools.partial(attend_kernel, causal),
        grid=(width // HEAD_DIM,),
        in_specs=[head(length), head(spots), head(spots), whole(rows), whole(cols)],
        out_specs=head(length),
        out_shape=jax.ShapeDtypeStruct((length, width), BF16),
        compiler_params=params(1),
        cost_estimate=pl.CostEstimate(
            flops=4 * length * spots * width,
            bytes_accessed=4 * (length + spots) * width,
            transcendentals=length * spots * width // HEAD_DIM,
        ),
    )(queries, keys, values, rows, cols)


def attend_back_kernel(causal, q_ref, k_ref, v_ref, row_ref, col_ref, do_ref, dq_ref, dk_ref, dv_ref):
    scale = HEAD_DIM ** (-0.5)
    scores = masked_scores(q_ref, k_ref, row_ref, col_ref, causal)
    exponent = jnp.exp(scores - jnp.max(scores, axis=-1, keepdims=True))
    weights = exponent * (1.0 / jnp.sum(exponent, axis=-1, keepdims=True))
    grad_weights = cols_dot(do_ref[...], v_ref[...])
    inner = jnp.sum(weights * grad_weights, axis=-1, keepdims=True)
    grad_scores = (weights * (grad_weights - inner)).astype(BF16)
    dq_ref[...] = (matmul(grad_scores, k_ref[...]) * scale).astype(BF16)
    dk_ref[...] = (rows_dot(grad_scores, q_ref[...]) * scale).astype(BF16)
    dv_ref[...] = rows_dot(weights.astype(BF16), do_ref[...]).astype(BF16)


def self_back_kernel(q_ref, k_ref, v_ref, row_ref, col_ref, do_ref, *outs):
    attend_back_kernel(
        True, q_ref, k_ref, v_ref, row_ref, col_ref, do_ref,
        *outs,
    )


def cross_back_kernel(q_ref, k_ref, v_ref, row_ref, col_ref, do_ref, dq_ref, out_ref):
    attend_back_kernel(
        False, q_ref, k_ref, v_ref, row_ref, col_ref, do_ref,
        dq_ref, out_ref.at[0], out_ref.at[1],
    )


def attend_back(queries, keys, values, rows, cols, grad_out, causal):
    length, width = queries.shape
    spots = keys.shape[0]
    head = lambda size: pl.BlockSpec((size, HEAD_DIM), lambda h: (0, h))
    whole = lambda arr: pl.BlockSpec(arr.shape, lambda h: (0, 0))
    shape = lambda *dims: jax.ShapeDtypeStruct(dims, BF16)
    if causal:
        out_specs, out_shape = (head(length),) * 3, (shape(length, width),) * 3
    else:
        out_specs = (head(length), pl.BlockSpec((2, spots, HEAD_DIM), lambda h: (0, 0, h)))
        out_shape = (shape(length, width), shape(2, spots, width))
    return pl.pallas_call(
        self_back_kernel if causal else cross_back_kernel,
        grid=(width // HEAD_DIM,),
        in_specs=[
            head(length), head(spots), head(spots), whole(rows), whole(cols), head(length),
        ],
        out_specs=out_specs,
        out_shape=out_shape,
        compiler_params=params(1),
        cost_estimate=pl.CostEstimate(
            flops=10 * length * spots * width,
            bytes_accessed=8 * (length + spots) * width,
            transcendentals=length * spots * width // HEAD_DIM,
        ),
    )(queries, keys, values, rows, cols, grad_out)


def assemble_kernel(*refs):
    *blocks, out_ref = refs
    step = blocks[0].shape[0]
    for k, block in enumerate(blocks):
        out_ref[k * step : (k + 1) * step] = block[...]


def assemble(blocks):
    step, width = blocks[0].shape
    columns = 512
    return pl.pallas_call(
        assemble_kernel,
        grid=(width // columns,),
        in_specs=[pl.BlockSpec((step, columns), lambda j: (0, j))] * len(blocks),
        out_specs=pl.BlockSpec((len(blocks) * step, columns), lambda j: (0, j)),
        out_shape=jax.ShapeDtypeStruct((len(blocks) * step, width), blocks[0].dtype),
        compiler_params=params(1),
        cost_estimate=cost(0, 4 * len(blocks) * step * width),
    )(*blocks)


def copy_kernel(at_ref, in_ref, out_ref):
    out_ref[...] = in_ref[...]


def pick_rows(at, arr, step):
    count, width = at.shape[0], arr.shape[1]
    return pl.pallas_call(
        copy_kernel,
        grid_spec=pltpu.PrefetchScalarGridSpec(
            num_scalar_prefetch=1,
            grid=(count,),
            in_specs=[pl.BlockSpec((step, width), lambda k, at: (at[k], 0))],
            out_specs=pl.BlockSpec((step, width), lambda k, at: (k, 0)),
        ),
        out_shape=jax.ShapeDtypeStruct((count * step, width), arr.dtype),
        compiler_params=params(1),
        cost_estimate=cost(0, 4 * count * step * width),
    )(at, arr)


def pick_columns(at, arr, rows, width):
    count = at.shape[0]
    return pl.pallas_call(
        copy_kernel,
        grid_spec=pltpu.PrefetchScalarGridSpec(
            num_scalar_prefetch=1,
            grid=(count,),
            in_specs=[pl.BlockSpec((rows, width), lambda k, at: (0, at[k]))],
            out_specs=pl.BlockSpec((rows, width), lambda k, at: (0, k)),
        ),
        out_shape=jax.ShapeDtypeStruct((rows, count * width), arr.dtype),
        compiler_params=params(1),
        cost_estimate=cost(0, 4 * count * rows * width),
    )(at, arr)


def pair_kernel(at_ref, a_ref, lo_ref, hi_ref, g_ref, far_ref, *rest):
    half = lo_ref.shape[0]
    if len(g_ref.shape) == 3:
        g_ref, far_ref = g_ref.at[0], far_ref.at[0]
    total = rows_dot(a_ref[...], g_ref[...])
    total += rows_dot(lo_ref[...], far_ref[:half])
    total += rows_dot(hi_ref[...], far_ref[half:])
    first_ref, rest_ref = rest[-2:]

    @pl.when(pl.program_id(0) == 0)
    def _():
        first_ref[0] = total.astype(BF16)

    @pl.when(pl.program_id(0) > 0)
    def _():
        rest_ref[0] = total.astype(BF16)


def pair_grad(at, own, low, high, grad, grad_far, after, pick=None):
    length, units = grad.shape[-2:]
    width = own.shape[1] // 8
    whole = pl.BlockSpec((length, units), lambda k, at: (0, 0))
    if pick is not None:
        whole = pl.BlockSpec((1, length, units), lambda k, at: (pick, 0, 0))
    side = pl.BlockSpec((length // 2, width), lambda k, at: (0, k))
    return pl.pallas_call(
        pair_kernel,
        grid_spec=pltpu.PrefetchScalarGridSpec(
            num_scalar_prefetch=1,
            grid=(4,),
            in_specs=[
                pl.BlockSpec((length, width), lambda k, at: (0, at[k])), side, side, whole, whole,
            ] + [ANY] * len(after),
            out_specs=(
                pl.BlockSpec((1, width, units), lambda k, at: (0, 0, 0)),
                pl.BlockSpec((1, width, units), lambda k, at: (jnp.maximum(k - 1, 0), 0, 0)),
            ),
        ),
        out_shape=tuple(jax.ShapeDtypeStruct((n, width, units), BF16) for n in (1, 3)),
        compiler_params=params(1),
        cost_estimate=cost(
            16 * length * width * units, 2 * units * (2 * length + 4 * width) + 16 * length * width
        ),
    )(at, own, low, high, grad, grad_far, *after)


def merge_kernel(left_ref, right_ref, *rest):
    rest[-1][...] = (left_ref[...].astype(F32) + right_ref[...].astype(F32)).astype(BF16)


def merge(left, right, after):
    spec = pl.BlockSpec((1,) + left.shape[1:], lambda k: (k, 0, 0))
    return pl.pallas_call(
        merge_kernel,
        grid=(left.shape[0],),
        in_specs=[spec, spec] + [ANY] * len(after),
        out_specs=spec,
        out_shape=jax.ShapeDtypeStruct(left.shape, BF16),
        compiler_params=params(1),
        cost_estimate=cost(left.size, 6 * left.size),
    )(left, right, *after)


def cross_kernel(at_ref, first_ref, rest_ref, in_ref, out_ref):
    part = jnp.where(pl.program_id(0) == 0, first_ref[...], rest_ref[...]).astype(F32)
    keep = jnp.where(at_ref[0] == 1, in_ref[...].astype(F32), 0.0)
    out_ref[...] = (part + keep).astype(BF16)


def cross_add(inner, first, rest, crossed):
    block = (1,) + rest.shape[1:]
    here = pl.BlockSpec(block, lambda k, at: (0, 0, 0))
    return pl.pallas_call(
        cross_kernel,
        grid_spec=pltpu.PrefetchScalarGridSpec(
            num_scalar_prefetch=1,
            grid=(2,),
            in_specs=[here, here, pl.BlockSpec(block, lambda k, at: (1 - k, 0, 0))],
            out_specs=pl.BlockSpec(block, lambda k, at: (k, 0, 0)),
        ),
        out_shape=jax.ShapeDtypeStruct((2,) + rest.shape[1:], BF16),
        compiler_params=params(1),
        cost_estimate=cost(crossed.size, 6 * crossed.size),
    )(inner, first, rest, crossed)


def add_rows(target, *sources):
    step = 32

    def body(i, carry):
        rows = pl.ds(pl.multiple_of(i * step, step), step)
        total = sources[0][rows].astype(F32)
        for source in sources[1:]:
            total = total + source[rows].astype(F32)
        target[rows] = total.astype(target.dtype)
        return carry

    lax.fori_loop(0, target.shape[0] // step, body, 0)


def line_kernel(ready, merged, count, pairs, *refs):
    refs = list(refs)
    take = lambda size: [refs.pop(0) for unused in range(size)]
    total = count + pairs + 1
    first = take(count)
    rest = dict(zip(range(ready, count), take(count - ready)))
    grads, [own, low, high, kept, sent] = take(pairs), take(5)
    outs = take(total)
    late = range(ready + merged, total)
    open_ends = range(ready, total)
    first += take(pairs + 1)
    rest.update(zip(range(count, total), take(pairs + 1)))
    far = take(pairs)
    [got] = take(1)
    from_outer = dict(zip(late, take(len(late))))
    from_inner = dict(zip(open_ends, take(len(open_ends))))
    last = take(total)
    send_out, got_out, send_in, got_in, send_last, got_last, send_x, got_x = refs
    dp, mp = lax.axis_index("dp"), lax.axis_index("mp")
    z, x = dp // 2, dp % 2
    beside = ((z + 1 - 2 * (z % 2)) * 2 + x, mp)
    across = ((3 - z) * 2 + x, mp)
    partner = (z * 2 + 1 - x, mp)
    flip = z // 2
    inner = (z == 1) | (z == 2)
    outer = (z == 0) | (z == 3)
    mesh_id = pl.DeviceIdType.MESH
    barrier = pltpu.get_barrier_semaphore()
    for device in (beside, partner):
        pl.semaphore_signal(barrier, inc=1, device_id=device, device_id_type=mesh_id)

    def copy(source, target, sent, got, device):
        return pltpu.make_async_remote_copy(
            src_ref=source, dst_ref=target, send_sem=sent, recv_sem=got,
            device_id=device, device_id_type=mesh_id,
        )

    def copy_out(g):
        return copy(rest[g], from_outer[g], send_out.at[g], got_out.at[g], beside)

    def copy_in(g):
        source = (from_outer if g in late else rest)[g].at[pl.ds(1, 2)]
        return copy(source, from_inner[g], send_in.at[g], got_in.at[g], across)

    def copy_last(g):
        source = first[g].at[0] if g < ready else from_inner[g].at[1]
        return copy(source, last[g], send_last.at[g], got_last.at[g], beside)

    def copy_grad(p):
        source, target = (grads[p], far[p]) if p < pairs else (sent, got)
        return copy(source, target, send_x.at[p], got_x.at[p], partner)

    def multiply(p):
        copy_grad(p).wait_recv()
        if p == pairs:
            add_rows(first[total - 1].at[0], kept.at[0], got.at[0])
            for k in range(3):
                add_rows(rest[total - 1].at[k], kept.at[k + 1], got.at[k + 1])
            return
        half, width = low.shape[0], first[count + p].shape[1]

        def body(k, carry):
            lane = k + flip * (3 - 2 * k)
            at = pl.ds(pl.multiple_of((2 * lane + x) * width, width), width)
            side = pl.ds(pl.multiple_of(k * width, width), width)
            value = rows_dot(own[:, at], grads[p][...])
            value += rows_dot(low[:, side], far[p][:half])
            value += rows_dot(high[:, side], far[p][half:])

            @pl.when(k == 0)
            def _():
                first[count + p][0] = value.astype(BF16)

            @pl.when(k > 0)
            def _():
                rest[count + p][jnp.maximum(k - 1, 0)] = value.astype(BF16)

            return carry

        lax.fori_loop(0, 4, body, 0)

    large = [g for g in late if g < count and first[g].shape[1] >= 256]
    small = [g for g in late if g < count and first[g].shape[1] < 256]
    sequence = large + list(range(count, total)) + small

    @pl.when(outer)
    def _():
        pl.semaphore_wait(barrier, 2)
        for p in range(pairs + 1):
            copy_grad(p).start()
        for g in sequence:
            if g >= count:
                multiply(g - count)
            copy_out(g).start()
        for g in list(range(ready + merged)) + sequence:
            copy_last(g).wait_recv()
            add_rows(outs[g], first[g].at[0], last[g])
        for g in late:
            copy_out(g).wait_send()

    @pl.when(inner)
    def _():
        pl.semaphore_signal(barrier, inc=1, device_id=across, device_id_type=mesh_id)
        pl.semaphore_wait(barrier, 3)
        for p in range(pairs + 1):
            copy_grad(p).start()
        for g in range(ready):
            copy_last(g).start()
        for g in range(ready, ready + merged):
            copy_in(g).start()

        def begin(g):
            copy_out(g).wait_recv()
            for k in (1, 2):
                add_rows(from_outer[g].at[k], rest[g].at[k], from_outer[g].at[k])
            copy_in(g).start()

        def finish(g):
            copy_in(g).wait_recv()
            add_rows(from_inner[g].at[1], first[g].at[0], from_inner[g].at[1])
            copy_last(g).start()
            near = [from_outer[g].at[0]] if g in late else []
            add_rows(outs[g], rest[g].at[0], from_inner[g].at[0], *near)

        for g in range(ready):
            add_rows(outs[g], first[g].at[1])
        waiting = list(range(ready, ready + merged))
        for g in sequence:
            if g >= count:
                multiply(g - count)
            begin(g)
            waiting.append(g)
            if len(waiting) > 2:
                finish(waiting.pop(0))
        for g in waiting:
            finish(g)
        for g in open_ends:
            copy_in(g).wait_send()
        for g in range(total):
            copy_last(g).wait_send()

    for p in range(pairs + 1):
        copy_grad(p).wait_send()


def line_sums(ready_parts, merged_parts, late_parts, grads, own, low, high, kept, sent):
    open_parts = list(merged_parts) + list(late_parts)
    parts = list(ready_parts) + [first for first, unused in open_parts]
    rests = [rest for unused, rest in open_parts]
    ready, merged, count, pairs = len(ready_parts), len(merged_parts), len(parts), len(grads)
    width = own.shape[1] // 8
    shapes = [p.shape[1:] for p in parts] + [(width, g.shape[1]) for g in grads] + [kept.shape[1:]]
    total, late = count + pairs + 1, shapes[ready + merged :]
    vmem = pl.BlockSpec(memory_space=pltpu.VMEM)
    sizes = [r * k for r, k in shapes]
    return pl.pallas_call(
        functools.partial(line_kernel, ready, merged, count, pairs),
        in_specs=[vmem] * (count + len(rests) + pairs + 5),
        out_specs=[vmem] * total,
        out_shape=[jax.ShapeDtypeStruct(shape, F32) for shape in shapes],
        scratch_shapes=[pltpu.VMEM((n,) + shape, BF16) for n in (1, 3) for shape in shapes[count:]]
        + [pltpu.VMEM(g.shape, BF16) for g in grads + [kept]]
        + [pltpu.VMEM((3,) + shape, BF16) for shape in late]
        + [pltpu.VMEM((2,) + shape, BF16) for shape in shapes[ready:]]
        + [pltpu.VMEM(shape, BF16) for shape in shapes]
        + [pltpu.SemaphoreType.DMA((total,))] * 6
        + [pltpu.SemaphoreType.DMA((pairs + 1,))] * 2,
        compiler_params=pltpu.CompilerParams(
            collective_id=0, has_side_effects=True, vmem_limit_bytes=56 * 2**20
        ),
        cost_estimate=cost(4 * sum(sizes), 40 * sum(sizes)),
    )(*parts, *rests, *grads, own, low, high, kept, sent)


CHUNKS = 4


def boundary_kernel(mode, jobs, early, partial, rows, kept, gain, *refs):
    refs = list(refs)
    take = lambda size: [refs.pop(0) for unused in range(size)]
    [gains] = take(1) if mode == "last" else [None]
    wanted, along = take(jobs), take(early)
    [sums] = take(1) if mode != "first" else [None]
    [gathered] = take(1) if mode not in ("last", "sum") else [None]
    [gain_out] = take(1) if mode in ("backward", "last") else [None]
    low_out, high_out, along_out = take(jobs), take(jobs), take(early)
    from_core, far_sum, from_chip, whole = take(4)
    low, high, from_lane = take(jobs), take(jobs), take(early)
    sends, gots = take(2)
    if jobs:
        send_jobs, got_jobs = take(2)
    if early:
        send_along, got_along = take(2)
    if mode == "last":
        others, send_gains, got_gains = take(3)
    dp, mp = lax.axis_index("dp"), lax.axis_index("mp")
    core = (dp, mp + 1 - 2 * (mp % 2))
    chip = (dp, (mp + 2) % 4)
    mesh_id = pl.DeviceIdType.MESH
    step = rows.shape[0]
    size = step // CHUNKS
    barrier = pltpu.get_barrier_semaphore()
    beside = (dp + 1 - 2 * (dp % 2), mp)
    lane = dp // 2
    next_lane = ((lane + 1 - 2 * (lane % 2)) * 2 + dp % 2, mp)
    near = (core, chip, beside) if jobs else (core, chip)
    greeted = near + ((next_lane,) if early else ())
    for device in greeted:
        pl.semaphore_signal(barrier, inc=1, device_id=device, device_id_type=mesh_id)
    pl.semaphore_wait(barrier, len(greeted))

    def along_copy(k):
        return pltpu.make_async_remote_copy(
            src_ref=along[k], dst_ref=from_lane[k], send_sem=send_along.at[k],
            recv_sem=got_along.at[k], device_id=next_lane, device_id_type=mesh_id,
        )

    for k in range(early):
        along_copy(k).start()

    def job(hop, k):
        source, target = ((wanted, low), (low, high))[hop]
        return pltpu.make_async_remote_copy(
            src_ref=source[k], dst_ref=target[k], send_sem=send_jobs.at[hop, k],
            recv_sem=got_jobs.at[hop, k], device_id=(beside, core)[hop], device_id_type=mesh_id,
        )

    for k in range(jobs):
        job(0, k).start()

    def copy(kind, c, source, target, device):
        return pltpu.make_async_remote_copy(
            src_ref=source, dst_ref=target, send_sem=sends.at[kind, c], recv_sem=gots.at[kind, c],
            device_id=device, device_id_type=mesh_id,
        )

    def part(block, c):
        return pl.ds(block * step + c * size, size)

    def core_sum(block, c):
        return copy(
            block, c, partial.at[part(2 + block, c)], from_core.at[part(block, c)], core
        )

    def chip_sum(c):
        return copy(2, c, far_sum.at[part(0, c)], from_chip.at[part(0, c)], chip)

    def chip_row(c):
        return copy(3, c, whole.at[part(0, c)], whole.at[part(1, c)], chip)

    def core_row(block, c):
        return copy(
            4 + block, c, whole.at[part(block, c)], whole.at[part(2 + block, c)], core
        )

    every = range(CHUNKS)
    wide = lambda value: value.astype(F32)
    if mode != "first":
        for block in (1, 0):
            for c in every:
                core_sum(block, c).start()
        for c in every:
            core_sum(1, c).wait_recv()
            total = wide(partial[part(1, c)]) + wide(from_core[part(1, c)])
            far_sum[part(0, c)] = total.astype(BF16)
            chip_sum(c).start()
    if gain_out is not None:
        gain_out[...] = jnp.zeros_like(gain_out) if mode != "last" else gains[...]
    for c in every:
        here = part(0, c)
        if mode == "first":
            value = wide(rows[here])
        else:
            core_sum(0, c).wait_recv()
            chip_sum(c).wait_recv()
            total = wide(partial[here]) + wide(from_core[here]) + wide(from_chip[here])
            if mode in ("forward", "sum"):
                value = wide(rows[here]) + total
                sums[here] = value
            else:
                old = kept[here]
                inv = inverse_rms(old)
                weighted = gain[...] * total
                inner = jnp.mean(old * weighted, axis=-1, keepdims=True)
                value = wide(rows[here]) + inv * weighted - old * (inv * inv * inv) * inner
                gain_out[0:1] += jnp.sum(total * old * inv, axis=0, keepdims=True)
                sums[here] = value
        if gathered is not None:
            if mode != "backward":
                value = value * inverse_rms(value) * gain[...]
            whole[here] = value.astype(BF16)
            chip_row(c).start()
            core_row(0, c).start()
    if gathered is not None:
        for c in every:
            chip_row(c).wait_recv()
            core_row(1, c).start()
        for c in every:
            for block in range(2):
                core_row(block, c).wait_recv()
        gathered[...] = whole[...]
    if mode == "last":
        for k, device in enumerate(near):
            others[0] = gain_out[...]
            hop = pltpu.make_async_remote_copy(
                src_ref=others.at[0], dst_ref=others.at[k + 1], send_sem=send_gains.at[k],
                recv_sem=got_gains.at[k], device_id=device, device_id_type=mesh_id,
            )
            hop.start()
            hop.wait()
            gain_out[...] += others[k + 1]
    for k in range(jobs):
        job(0, k).wait_recv()
        job(1, k).start()
        low_out[k][...] = low[k][...]
    for k in range(jobs):
        job(0, k).wait_send()
        job(1, k).wait_recv()
        high_out[k][...] = high[k][...]
        job(1, k).wait_send()
    for k in range(early):
        along_copy(k).wait()
        along_out[k][...] = from_lane[k][...]
    for c in every:
        if mode != "first":
            core_sum(0, c).wait_send()
            core_sum(1, c).wait_send()
            chip_sum(c).wait_send()
        if gathered is not None:
            chip_row(c).wait_send()
            core_row(0, c).wait_send()
            core_row(1, c).wait_send()


def boundary(mode, number, partial, rows, kept, gain, wanted=(), gains=None, along=()):
    step, width = rows.shape
    vmem = pl.BlockSpec(memory_space=pltpu.VMEM)
    shapes = []
    if mode != "first":
        shapes.append(jax.ShapeDtypeStruct((step, width), F32))
    if mode not in ("last", "sum"):
        shapes.append(jax.ShapeDtypeStruct((4 * step, width), BF16))
    if mode in ("backward", "last"):
        shapes.append(jax.ShapeDtypeStruct((1 if mode == "backward" else 8, width), F32))
    given = [gains] if mode == "last" else []
    jobs, early = len(wanted), len(along)
    moved = list(wanted) * 2 + list(along)
    shapes += [jax.ShapeDtypeStruct(w.shape, BF16) for w in moved]
    scratch = [pltpu.VMEM(w.shape, BF16) for w in moved]
    outs = pl.pallas_call(
        functools.partial(boundary_kernel, mode, jobs, early),
        in_specs=[vmem] * (4 + len(given) + jobs + early),
        out_specs=[vmem] * len(shapes),
        out_shape=shapes,
        scratch_shapes=[
            pltpu.VMEM((2 * step, width), BF16),
            pltpu.VMEM((step, width), BF16),
            pltpu.VMEM((step, width), BF16),
            pltpu.VMEM((4 * step, width), BF16),
        ]
        + scratch
        + [pltpu.SemaphoreType.DMA((6, CHUNKS))] * 2
        + ([pltpu.SemaphoreType.DMA((2, jobs))] * 2 if jobs else [])
        + ([pltpu.SemaphoreType.DMA((early,))] * 2 if early else [])
        + (
            [pltpu.VMEM((4, 8, width), F32)] + [pltpu.SemaphoreType.DMA((3,))] * 2
            if mode == "last"
            else []
        ),
        compiler_params=pltpu.CompilerParams(
            collective_id=number, has_side_effects=True, vmem_limit_bytes=2 * VMEM_LIMIT
        ),
        cost_estimate=cost(10 * step * width, 60 * 2**20),
    )(partial, rows, kept, gain, *given, *wanted, *along)
    if not jobs:
        return outs
    outs = list(outs)
    plain = len(outs) - 2 * jobs - early
    halves = list(zip(outs[plain : plain + jobs], outs[plain + jobs :]))
    return outs[:plain] + halves + outs[plain + 2 * jobs :]


def gated_unit(gate_arg, up_arg):
    return jax.nn.gelu(gate_arg, approximate=True) * up_arg


def layer(n_dp, n_mp):
    lanes = n_dp // 2
    paired = n_dp == 8

    def swap(value, axis, size, bit):
        return lax.ppermute(value, axis, [(i, i ^ bit) for i in range(size)])

    def core(value):
        return swap(value, "mp", n_mp, 1)

    def chip(value):
        return swap(value, "mp", n_mp, 2)

    def beside(value):
        return swap(value, "dp", n_dp, 1)

    def gather(mine):
        far = chip(mine)
        return assemble([mine, far, core(mine), core(far)])

    def gather_after(mine, after):
        return gather(tie(mine, after))

    def scatter_rows(partial):
        step = partial.shape[0] // 4
        block = [partial[k * step : (k + 1) * step] for k in range(4)]
        far = (block[1].astype(F32) + core(block[3]).astype(F32)).astype(BF16)
        far_in = chip(far)
        return block[0].astype(F32) + core(block[2]).astype(F32) + far_in.astype(F32)

    def line_place():
        z = lax.axis_index("dp") // 2
        number = lambda value: jnp.asarray(value).astype(jnp.int32)
        return lax.axis_index("dp") % 2, number(z >= 2), number((z == 1) | (z == 2))

    def outer_swap(value):
        return swap(value, "dp", n_dp, 2)

    def inner_swap(value):
        pairs = []
        for d in range(n_dp):
            for m in range(n_mp):
                inner = d // 2 in (1, 2)
                to = (d ^ 6) * n_mp + m if inner else d * n_mp + (m ^ 1)
                pairs.append((d * n_mp + m, to))
        return lax.ppermute(value, ("dp", "mp"), pairs)

    def lane_columns(parity):
        flip = line_place()[1]
        k = jnp.arange(4, dtype=jnp.int32)
        return 2 * (k + flip * (3 - 2 * k)) + parity

    def wanted_of(value, half=None):
        rows = value.shape[0] // 2
        if half is not None:
            value = pick_rows(jnp.stack([half]).astype(jnp.int32), value, rows)
        x = line_place()[0]
        return pick_columns(lane_columns(1 - x), value, rows, value.shape[1] // n_dp)

    def shards(
        tokens, norm_gains, w_query, w_key, w_value, w_out, c_query, c_key, c_value, c_out,
        patch_proj, w_gate, w_up, w_down, patches, segment_ids, image_index, cotangent,
    ):
        length = segment_ids.shape[1]
        model = tokens.shape[2]
        patch_rows = patches.shape[0] * patches.shape[1]
        m = lax.axis_index("mp")
        order = [m, m ^ 2, m ^ 1, m ^ 3]

        def blocks(arr, axis=0):
            step = arr.shape[axis] // 4
            return jnp.concatenate(
                [lax.dynamic_slice_in_dim(arr, k * step, step, axis) for k in order], axis=axis
            )

        places = blocks(jnp.arange(length, dtype=jnp.int32))
        segment_row = blocks(segment_ids[0])
        slots = jnp.arange(SEGS, dtype=jnp.int32)
        token_image = jnp.sum(
            jnp.where(segment_row[:, None] == slots, image_index[0][None, :], 0), axis=-1
        )
        patch_image = jnp.arange(patch_rows, dtype=jnp.int32) // patches.shape[1]

        far_of = beside if paired else (lambda value: value)
        core_bit = m % 2

        def exchange(*values):
            return [wanted_of(*value) for value in values] if paired else []

        def split(value, halves):
            return (value, *halves) if paired else (value,)

        def split_now(value):
            if not paired:
                return (value,)
            wanted = wanted_of(value)
            low = beside(wanted)
            return value, low, core(low)

        self_rows = jnp.stack([segment_row, places], axis=1)
        self_cols = self_rows.T
        cross_rows, cross_cols = token_image[:, None], patch_image[None, :]
        residual = tokens[0].astype(F32)
        gain_rows = [norm_gains[k : k + 1] for k in range(3)]
        nothing = jnp.zeros((16, 128), BF16)
        none = [None] * 4
        [normed_one] = boundary("first", 1, nothing, tokens[0], nothing, gain_rows[0])
        patch_own = patches.reshape(patch_rows, patches.shape[2])
        projected = matmul(patch_own, patch_proj).astype(BF16)
        queries = matmul(normed_one, w_query).astype(BF16)
        key_rows = matmul(normed_one, w_key).astype(BF16)
        value_rows = matmul(normed_one, w_value).astype(BF16)
        self_mixed = attend(queries, key_rows, value_rows, self_rows, self_cols, True)
        self_far = far_of(self_mixed)
        grad_three = gather_after(cotangent[0], normed_one)
        split_one = split_now(normed_one)
        self_mixed = tie(self_mixed, (grad_three, split_one))
        partial = matmul(self_mixed, w_out).astype(BF16)
        after_self, normed_two, *halves = boundary(
            "forward", 2, partial, tokens[0], nothing, gain_rows[1], exchange((projected, core_bit))
        )
        patch_low, patch_high = halves[0] if paired else (None, None)
        normed_two = tie(normed_two, self_far)
        cross_keys = matmul(projected, c_key).astype(BF16)
        cross_values = matmul(projected, c_value).astype(BF16)
        cross_queries = matmul(normed_two, c_query).astype(BF16)
        cross_mixed = attend(
            cross_queries, cross_keys, cross_values, cross_rows, cross_cols, False
        )
        partial = matmul(cross_mixed, c_out).astype(BF16)
        after_cross, normed_three, *halves = boundary(
            "forward", 3, partial, after_self, nothing, gain_rows[2],
            exchange((grad_three,), (normed_two,)),
        )
        split_cotangent, split_two = map(split, (grad_three, normed_two), halves or none)
        grad_hidden = tie(product("sd,fd->sf", grad_three, w_down), ())
        if paired:
            wanted = wanted_of(normed_three)
            low_three = beside(wanted)
            split_three = normed_three, low_three, core(low_three)
            normed_three = tie(normed_three, (grad_hidden, wanted))
        else:
            split_three, low_three = (normed_three,), normed_three
        gate_pre, up_pre = matmul(normed_three, w_gate), matmul(normed_three, w_up)
        hidden, pull = jax.vjp(gated_unit, gate_pre, up_pre)
        hidden = hidden.astype(BF16)
        grad_gate, grad_up = [g.astype(BF16) for g in pull(grad_hidden)]

        results, turned = {}, {}

        def line(name, split, grad, grad_far, rows_first, after=(), pick=None):
            turned[name] = not rows_first
            if not paired:
                grad = grad if pick is None else grad[pick]
                partial = product("td,te->de", split[0], grad).astype(BF16)
                total = lax.psum_scatter(partial, "dp", scatter_dimension=0, tiled=True)
                results[name] = total.astype(F32)
                return ()
            results[name] = pair_grad(
                lane_columns(line_place()[0]), *split, grad, grad_far, after, pick
            )
            return results[name]

        def line_out(name):
            return outer_swap(results[name][1]) if paired else None

        def line_merge(name, incoming, after):
            if paired:
                first, rest = results[name]
                results[name] = first, merge(rest, incoming, after)

        def line_across(name):
            if paired:
                inner = line_place()[2]
                first, rest = results[name]
                results[name] = cross_add(inner.reshape(1), first, rest, inner_swap(rest[1:]))

        hidden_far = far_of(tie(hidden, low_three))
        partial = (
            product("sf,df->sd", grad_gate, w_gate) + product("sf,df->sd", grad_up, w_up)
        ).astype(BF16)
        gate_far, up_far = [far_of(v) for v in tie((grad_gate, grad_up), partial)]
        partial_out = matmul(tie(hidden, partial), w_down).astype(BF16)
        [output] = boundary("sum", 7, partial_out, after_cross, nothing, gain_rows[0])
        sent = line("down", split_cotangent, hidden, hidden_far, False, (output,))
        incoming_down = line_out("down")
        grad_rows, grad_two, gain_three = boundary(
            "backward", 4, tie(partial, sent), cotangent[0], after_cross, gain_rows[2]
        )
        sent = line("gate", split_three, grad_gate, gate_far, True, (grad_two,))
        incoming_gate = line_out("gate")
        grad_two = tie(grad_two, sent)

        grad_mixed = product("sd,ed->se", grad_two, c_out).astype(BF16)
        grad_cq, grad_ckv = attend_back(
            cross_queries, cross_keys, cross_values, cross_rows, cross_cols, grad_mixed, False
        )
        cq_far, ckv_far = far_of(grad_cq), far_of(grad_ckv)
        partial = product("se,de->sd", grad_cq, c_query).astype(BF16)
        sent = line("up", split_three, grad_up, up_far, True, (partial,))
        incoming_up = line_out("up")
        line_merge("down", incoming_down, (partial,))
        grad_rows, grad_one, gain_two = boundary(
            "backward", 5, tie(partial, (sent, results["down"])), grad_rows, after_self, gain_rows[1]
        )
        line_across("down")

        width = model // (n_dp * n_mp)

        def projected_block(k):
            def rows_of(weight):
                cut = weight.reshape(n_dp, n_mp, width, weight.shape[1])
                return lax.dynamic_index_in_dim(cut, k, 1, keepdims=False).reshape(
                    n_dp * width, weight.shape[1]
                )

            return (
                cols_dot(grad_ckv_late[0], rows_of(c_key))
                + cols_dot(grad_ckv_late[1], rows_of(c_value))
            ).astype(
                BF16
            )

        grad_ckv_late = tie(grad_ckv, grad_one)
        block = [projected_block(k) for k in order]
        far_core = core(block[3])

        grad_mixed = product(
            "sd,ed->se", tie(grad_one, (block[1], block[3])), w_out
        ).astype(BF16)
        grad_sq, grad_sk, grad_sv = attend_back(
            queries, key_rows, value_rows, self_rows, self_cols, grad_mixed, True
        )
        far = (block[1].astype(F32) + far_core.astype(F32)).astype(BF16)
        grad_sq, grad_sk, grad_sv = tie((grad_sq, grad_sk, grad_sv), far)
        far_in = chip(far)
        near = (block[0].astype(F32) + core(block[2]).astype(F32)).astype(BF16)
        partial = (
            product("se,de->sd", grad_sq, w_query)
            + product("se,de->sd", grad_sk, w_key)
            + product("se,de->sd", grad_sv, w_value)
        ).astype(BF16)
        line_merge("gate", incoming_gate, (partial,))
        line("c_query", split_two, grad_cq, cq_far, True, (partial,))
        split_patch = (projected,)
        if paired:
            swapped = core_bit == 1
            split_patch = (
                projected,
                jnp.where(swapped, patch_high, patch_low),
                jnp.where(swapped, patch_low, patch_high),
            )
        sent = line("c_key", split_patch, grad_ckv, ckv_far, True, (partial,), 0)
        gains = jnp.pad(jnp.concatenate([gain_two, gain_three], axis=0), ((1, 5), (0, 0)))
        along = [results["c_query"][1], results["c_key"][1]] if paired else []
        grad_rows, gains_near, *halves = boundary(
            "last", 6, tie(partial, (sent, far, near, results["gate"], results["down"])), grad_rows,
            residual, gain_rows[0], exchange((grad_two,), (grad_one,)), gains, along,
        )
        if paired:
            line_merge("c_query", halves[2], ())
            line_merge("c_key", halves[3], ())
        mixed_far = far_of(tie(cross_mixed, grad_rows))
        line_across("gate")
        split_grad_two, split_grad_one = map(split, (grad_two, grad_one), halves[:2] or none)
        grad_projected = (near.astype(F32) + far_in.astype(F32)).astype(BF16)
        patch_partial = rows_dot(grad_projected, patch_own).astype(BF16)
        x, flip, unused = line_place()
        patch_parts = patch_partial.reshape(n_dp // 2, 2, width, patches.shape[2])
        patch_sent = lax.dynamic_index_in_dim(patch_parts, 1 - x, 1, keepdims=False)
        line("c_value", split_patch, grad_ckv, ckv_far, True, (grad_rows,), 1)
        line("c_out", split_grad_two, cross_mixed, mixed_far, False, (grad_rows,))
        line("w_out", split_grad_one, self_mixed, self_far, False, (grad_rows,))
        line_merge("up", incoming_up, (grad_rows,))
        if paired:
            patch_kept = lax.dynamic_index_in_dim(patch_parts, x, 1, keepdims=False)
            patch_kept, patch_sent = [
                jnp.where(flip == 1, v.astype(F32)[::-1], v.astype(F32)).astype(BF16)
                for v in (patch_kept, patch_sent)
            ]
            mine = lax.dynamic_index_in_dim(
                gains_near[:3].reshape(3, 4, 2, n_mp, width), x, 2, keepdims=False
            )
            mine = lax.dynamic_index_in_dim(mine, m, 2, keepdims=False).transpose(1, 0, 2)
            mine = jnp.where(flip == 1, mine[::-1], mine)
            mine = jnp.pad(mine, ((0, 0), (0, 29), (0, 128 - width))).astype(BF16)
            results["gains"] = mine[:1], mine[1:]
            early, late = ["down", "gate"], ["c_value", "w_out", "c_out"]
            merged = ["up", "c_query", "c_key"]
            late.append("gains")
            names = early + merged + late + ["w_query", "w_key", "w_value", "patch"]
            sums = line_sums(
                *[[results[n] for n in group] for group in (early, merged, late)],
                [grad_sq, grad_sk, grad_sv], *split_one, patch_kept, patch_sent,
            )
            results.update(zip(names, sums))
        else:
            results["patch"] = lax.psum_scatter(
                patch_partial, "dp", scatter_dimension=0, tiled=True
            ).astype(F32)
            line("w_query", split_one, grad_sq, grad_sq, True)
            line("w_key", split_one, grad_sk, grad_sk, True)
            line("w_value", split_one, grad_sv, grad_sv, True)
        turned["patch"] = True
        results = {n: v.T if turned.get(n) else v for n, v in results.items()}
        patch_total = results["patch"]
        if paired:
            gain_total = results["gains"][:3, :width]
        else:
            gain_total = lax.dynamic_index_in_dim(
                gains_near[:3].reshape(3, n_dp, n_mp, width), m, 2, keepdims=False
            )
            gain_total = lax.psum_scatter(
                gain_total.reshape(3, n_dp * width), "dp", scatter_dimension=1, tiled=True
            )
        sum_query, sum_key, sum_value = results["w_query"], results["w_key"], results["w_value"]
        sum_cquery, sum_ckey, sum_cvalue = results["c_query"], results["c_key"], results["c_value"]
        sum_out, sum_cout, sum_down = results["w_out"], results["c_out"], results["down"]
        sum_gate, sum_up = results["gate"], results["up"]
        return (
            output.astype(BF16)[None], grad_rows[None], gain_total,
            sum_query, sum_key, sum_value, sum_out,
            sum_cquery, sum_ckey, sum_cvalue, sum_cout,
            patch_total, sum_gate, sum_up, sum_down,
        )

    return shards


def solution(mesh):
    columns, rows = P(None, "mp"), P("mp", None)
    return jax.shard_map(
        layer(mesh.shape["dp"], mesh.shape["mp"]),
        mesh=mesh,
        in_specs=(
            P("dp", "mp", None), P(), columns, columns, columns, rows, columns, columns, columns,
            rows, P(), columns, columns, rows, P("dp", None, None), P("dp", None), P("dp", None),
            P("dp", "mp", None),
        ),
        out_specs=(
            P("dp", "mp", None), P("dp", "mp", None), P(None, ("dp", "mp")),
            P("dp", "mp"), P("dp", "mp"), P("dp", "mp"), P("mp", "dp"),
            P("dp", "mp"), P("dp", "mp"), P("dp", "mp"), P("mp", "dp"),
            P(None, ("dp", "mp")), P("dp", "mp"), P("dp", "mp"), P("mp", "dp"),
        ),
        check_vma=False,
    )
```

```python
import functools

import jax
import jax.numpy as jnp
from jax import lax
from jax.experimental import pallas as pl
from jax.experimental.pallas import tpu as pltpu
from jax.sharding import PartitionSpec as P

HEAD_DIM = 128
SEGS = 4
EPSILON = 1e-06
MASKED = -1000000000.0
F32 = jnp.float32
BF16 = jnp.bfloat16


def matmul(left, right):
    return jnp.dot(left, right, preferred_element_type=F32)


def product(spec, left, right):
    return jnp.einsum(spec, left, right, preferred_element_type=F32)


def rows_dot(left, right):
    return lax.dot_general(left, right, (((0,), (0,)), ((), ())), preferred_element_type=F32)


def cols_dot(left, right):
    return lax.dot_general(left, right, (((1,), (1,)), ((), ())), preferred_element_type=F32)


def tie(value, after):
    return lax.optimization_barrier((value, after))[0]


def inverse_rms(rows):
    return lax.rsqrt(jnp.mean(rows * rows, axis=-1, keepdims=True) + EPSILON)


def norm_rows(rows, gain):
    return (rows * inverse_rms(rows) * gain).astype(BF16)


def norm_back(rows, gain, grad):
    inv = inverse_rms(rows)
    weighted = gain * grad
    inner = jnp.mean(rows * weighted, axis=-1, keepdims=True)
    grad_rows = inv * weighted - rows * (inv * inv * inv) * inner
    return grad_rows, jnp.sum(grad * rows * inv, axis=0)


VMEM_LIMIT = 17 * 2**20
GELU_SCALE = 0.7978845608028654
GELU_CUBE = 0.044715
ANY = pl.BlockSpec(memory_space=pl.ANY)


def params(grid_rank):
    return pltpu.CompilerParams(
        dimension_semantics=("arbitrary",) * grid_rank, vmem_limit_bytes=VMEM_LIMIT
    )


def wide_params(grid_rank, size=28):
    return pltpu.CompilerParams(
        dimension_semantics=("arbitrary",) * grid_rank, vmem_limit_bytes=size * 2**20
    )


def cost(flops, size):
    return pl.CostEstimate(flops=flops, bytes_accessed=size, transcendentals=0)


def masked_scores(q_ref, k_ref, row_ref, col_ref, causal):
    scores = cols_dot(q_ref[...], k_ref[...]) * (HEAD_DIM ** (-0.5))
    allowed = row_ref[:, 0:1] == col_ref[0:1, :]
    if causal:
        allowed = allowed & (col_ref[1:2, :] <= row_ref[:, 1:2])
    return jnp.where(allowed, scores, MASKED)


def attend_kernel(causal, q_ref, k_ref, v_ref, row_ref, col_ref, out_ref):
    scores = masked_scores(q_ref, k_ref, row_ref, col_ref, causal)
    exponent = jnp.exp(scores - jnp.max(scores, axis=-1, keepdims=True))
    total = jnp.sum(exponent, axis=-1, keepdims=True)
    weights = (exponent * (1.0 / total)).astype(BF16)
    out_ref[...] = matmul(weights, v_ref[...]).astype(BF16)


def attend(queries, keys, values, rows, cols, causal):
    length, width = queries.shape
    spots = keys.shape[0]
    head = lambda size: pl.BlockSpec((size, HEAD_DIM), lambda h: (0, h))
    whole = lambda arr: pl.BlockSpec(arr.shape, lambda h: (0, 0))
    return pl.pallas_call(
        functools.partial(attend_kernel, causal),
        grid=(width // HEAD_DIM,),
        in_specs=[head(length), head(spots), head(spots), whole(rows), whole(cols)],
        out_specs=head(length),
        out_shape=jax.ShapeDtypeStruct((length, width), BF16),
        compiler_params=params(1),
        cost_estimate=pl.CostEstimate(
            flops=4 * length * spots * width,
            bytes_accessed=4 * (length + spots) * width,
            transcendentals=length * spots * width // HEAD_DIM,
        ),
    )(queries, keys, values, rows, cols)


def attend_back_kernel(causal, q_ref, k_ref, v_ref, row_ref, col_ref, do_ref, dq_ref, dk_ref, dv_ref):
    scale = HEAD_DIM ** (-0.5)
    scores = masked_scores(q_ref, k_ref, row_ref, col_ref, causal)
    exponent = jnp.exp(scores - jnp.max(scores, axis=-1, keepdims=True))
    weights = exponent * (1.0 / jnp.sum(exponent, axis=-1, keepdims=True))
    grad_weights = cols_dot(do_ref[...], v_ref[...])
    inner = jnp.sum(weights * grad_weights, axis=-1, keepdims=True)
    grad_scores = (weights * (grad_weights - inner)).astype(BF16)
    dq_ref[...] = (matmul(grad_scores, k_ref[...]) * scale).astype(BF16)
    dk_ref[...] = (rows_dot(grad_scores, q_ref[...]) * scale).astype(BF16)
    dv_ref[...] = rows_dot(weights.astype(BF16), do_ref[...]).astype(BF16)


def self_back_kernel(q_ref, k_ref, v_ref, row_ref, col_ref, do_ref, *outs):
    attend_back_kernel(
        True, q_ref, k_ref, v_ref, row_ref, col_ref, do_ref,
        *outs,
    )


def cross_back_kernel(q_ref, k_ref, v_ref, row_ref, col_ref, do_ref, dq_ref, out_ref):
    attend_back_kernel(
        False, q_ref, k_ref, v_ref, row_ref, col_ref, do_ref,
        dq_ref, out_ref.at[0], out_ref.at[1],
    )


def attend_back(queries, keys, values, rows, cols, grad_out, causal):
    length, width = queries.shape
    spots = keys.shape[0]
    head = lambda size: pl.BlockSpec((size, HEAD_DIM), lambda h: (0, h))
    whole = lambda arr: pl.BlockSpec(arr.shape, lambda h: (0, 0))
    shape = lambda *dims: jax.ShapeDtypeStruct(dims, BF16)
    if causal:
        out_specs, out_shape = (head(length),) * 3, (shape(length, width),) * 3
    else:
        out_specs = (head(length), pl.BlockSpec((2, spots, HEAD_DIM), lambda h: (0, 0, h)))
        out_shape = (shape(length, width), shape(2, spots, width))
    return pl.pallas_call(
        self_back_kernel if causal else cross_back_kernel,
        grid=(width // HEAD_DIM,),
        in_specs=[
            head(length), head(spots), head(spots), whole(rows), whole(cols), head(length),
        ],
        out_specs=out_specs,
        out_shape=out_shape,
        compiler_params=params(1),
        cost_estimate=pl.CostEstimate(
            flops=10 * length * spots * width,
            bytes_accessed=8 * (length + spots) * width,
            transcendentals=length * spots * width // HEAD_DIM,
        ),
    )(queries, keys, values, rows, cols, grad_out)


def assemble_kernel(*refs):
    *blocks, out_ref = refs
    step = blocks[0].shape[0]
    for k, block in enumerate(blocks):
        out_ref[k * step : (k + 1) * step] = block[...]


def assemble(blocks):
    step, width = blocks[0].shape
    columns = 512
    return pl.pallas_call(
        assemble_kernel,
        grid=(width // columns,),
        in_specs=[pl.BlockSpec((step, columns), lambda j: (0, j))] * len(blocks),
        out_specs=pl.BlockSpec((len(blocks) * step, columns), lambda j: (0, j)),
        out_shape=jax.ShapeDtypeStruct((len(blocks) * step, width), blocks[0].dtype),
        compiler_params=params(1),
        cost_estimate=cost(0, 4 * len(blocks) * step * width),
    )(*blocks)


def copy_kernel(at_ref, in_ref, out_ref):
    out_ref[...] = in_ref[...]


def pick_rows(at, arr, step):
    count, width = at.shape[0], arr.shape[1]
    return pl.pallas_call(
        copy_kernel,
        grid_spec=pltpu.PrefetchScalarGridSpec(
            num_scalar_prefetch=1,
            grid=(count,),
            in_specs=[pl.BlockSpec((step, width), lambda k, at: (at[k], 0))],
            out_specs=pl.BlockSpec((step, width), lambda k, at: (k, 0)),
        ),
        out_shape=jax.ShapeDtypeStruct((count * step, width), arr.dtype),
        compiler_params=params(1),
        cost_estimate=cost(0, 4 * count * step * width),
    )(at, arr)


def pick_columns(at, arr, rows, width):
    count = at.shape[0]
    return pl.pallas_call(
        copy_kernel,
        grid_spec=pltpu.PrefetchScalarGridSpec(
            num_scalar_prefetch=1,
            grid=(count,),
            in_specs=[pl.BlockSpec((rows, width), lambda k, at: (0, at[k]))],
            out_specs=pl.BlockSpec((rows, width), lambda k, at: (0, k)),
        ),
        out_shape=jax.ShapeDtypeStruct((rows, count * width), arr.dtype),
        compiler_params=params(1),
        cost_estimate=cost(0, 4 * count * rows * width),
    )(at, arr)


def pair_kernel(at_ref, a_ref, lo_ref, hi_ref, g_ref, far_ref, *rest):
    half = lo_ref.shape[0]
    if len(g_ref.shape) == 3:
        g_ref, far_ref = g_ref.at[0], far_ref.at[0]
    total = rows_dot(a_ref[...], g_ref[...])
    total += rows_dot(lo_ref[...], far_ref[:half])
    total += rows_dot(hi_ref[...], far_ref[half:])
    first_ref, rest_ref = rest[-2:]

    @pl.when(pl.program_id(0) == 0)
    def _():
        first_ref[0] = total.astype(BF16)

    @pl.when(pl.program_id(0) > 0)
    def _():
        rest_ref[0] = total.astype(BF16)


def pair_grad(at, own, low, high, grad, grad_far, after, pick=None):
    length, units = grad.shape[-2:]
    width = own.shape[1] // 8
    whole = pl.BlockSpec((length, units), lambda k, at: (0, 0))
    if pick is not None:
        whole = pl.BlockSpec((1, length, units), lambda k, at: (pick, 0, 0))
    side = pl.BlockSpec((length // 2, width), lambda k, at: (0, k))
    return pl.pallas_call(
        pair_kernel,
        grid_spec=pltpu.PrefetchScalarGridSpec(
            num_scalar_prefetch=1,
            grid=(4,),
            in_specs=[
                pl.BlockSpec((length, width), lambda k, at: (0, at[k])), side, side, whole, whole,
            ] + [ANY] * len(after),
            out_specs=(
                pl.BlockSpec((1, width, units), lambda k, at: (0, 0, 0)),
                pl.BlockSpec((1, width, units), lambda k, at: (jnp.maximum(k - 1, 0), 0, 0)),
            ),
        ),
        out_shape=tuple(jax.ShapeDtypeStruct((n, width, units), BF16) for n in (1, 3)),
        compiler_params=params(1),
        cost_estimate=cost(
            16 * length * width * units, 2 * units * (2 * length + 4 * width) + 16 * length * width
        ),
    )(at, own, low, high, grad, grad_far, *after)


def merge_kernel(left_ref, right_ref, *rest):
    rest[-1][...] = (left_ref[...].astype(F32) + right_ref[...].astype(F32)).astype(BF16)


def merge(left, right, after):
    spec = pl.BlockSpec((1,) + left.shape[1:], lambda k: (k, 0, 0))
    return pl.pallas_call(
        merge_kernel,
        grid=(left.shape[0],),
        in_specs=[spec, spec] + [ANY] * len(after),
        out_specs=spec,
        out_shape=jax.ShapeDtypeStruct(left.shape, BF16),
        compiler_params=params(1),
        cost_estimate=cost(left.size, 6 * left.size),
    )(left, right, *after)


def cross_kernel(at_ref, first_ref, rest_ref, in_ref, out_ref):
    part = jnp.where(pl.program_id(0) == 0, first_ref[...], rest_ref[...]).astype(F32)
    keep = jnp.where(at_ref[0] == 1, in_ref[...].astype(F32), 0.0)
    out_ref[...] = (part + keep).astype(BF16)


def cross_add(inner, first, rest, crossed):
    block = (1,) + rest.shape[1:]
    here = pl.BlockSpec(block, lambda k, at: (0, 0, 0))
    return pl.pallas_call(
        cross_kernel,
        grid_spec=pltpu.PrefetchScalarGridSpec(
            num_scalar_prefetch=1,
            grid=(2,),
            in_specs=[here, here, pl.BlockSpec(block, lambda k, at: (1 - k, 0, 0))],
            out_specs=pl.BlockSpec(block, lambda k, at: (k, 0, 0)),
        ),
        out_shape=jax.ShapeDtypeStruct((2,) + rest.shape[1:], BF16),
        compiler_params=params(1),
        cost_estimate=cost(crossed.size, 6 * crossed.size),
    )(inner, first, rest, crossed)


def add_rows(target, *sources):
    step = 32

    def body(i, carry):
        rows = pl.ds(pl.multiple_of(i * step, step), step)
        total = sources[0][rows].astype(F32)
        for source in sources[1:]:
            total = total + source[rows].astype(F32)
        target[rows] = total.astype(target.dtype)
        return carry

    lax.fori_loop(0, target.shape[0] // step, body, 0)


def line_kernel(ready, merged, count, pairs, *refs):
    refs = list(refs)
    take = lambda size: [refs.pop(0) for unused in range(size)]
    total = count + pairs + 1
    first = take(count)
    rest = dict(zip(range(ready, count), take(count - ready)))
    grads, [own, low, high, kept, sent] = take(pairs), take(5)
    outs = take(total)
    late = range(ready + merged, total)
    open_ends = range(ready, total)
    first += take(pairs + 1)
    rest.update(zip(range(count, total), take(pairs + 1)))
    far = take(pairs)
    [got] = take(1)
    from_outer = dict(zip(late, take(len(late))))
    from_inner = dict(zip(open_ends, take(len(open_ends))))
    last = take(total)
    send_out, got_out, send_in, got_in, send_last, got_last, send_x, got_x = refs
    dp, mp = lax.axis_index("dp"), lax.axis_index("mp")
    z, x = dp // 2, dp % 2
    beside = ((z + 1 - 2 * (z % 2)) * 2 + x, mp)
    across = ((3 - z) * 2 + x, mp)
    partner = (z * 2 + 1 - x, mp)
    flip = z // 2
    inner = (z == 1) | (z == 2)
    outer = (z == 0) | (z == 3)
    mesh_id = pl.DeviceIdType.MESH
    barrier = pltpu.get_barrier_semaphore()
    for device in (beside, partner):
        pl.semaphore_signal(barrier, inc=1, device_id=device, device_id_type=mesh_id)

    def copy(source, target, sent, got, device):
        return pltpu.make_async_remote_copy(
            src_ref=source, dst_ref=target, send_sem=sent, recv_sem=got,
            device_id=device, device_id_type=mesh_id,
        )

    def copy_out(g):
        return copy(rest[g], from_outer[g], send_out.at[g], got_out.at[g], beside)

    def copy_in(g):
        source = (from_outer if g in late else rest)[g].at[pl.ds(1, 2)]
        return copy(source, from_inner[g], send_in.at[g], got_in.at[g], across)

    def copy_last(g):
        source = first[g].at[0] if g < ready else from_inner[g].at[1]
        return copy(source, last[g], send_last.at[g], got_last.at[g], beside)

    def copy_grad(p):
        source, target = (grads[p], far[p]) if p < pairs else (sent, got)
        return copy(source, target, send_x.at[p], got_x.at[p], partner)

    def multiply(p):
        copy_grad(p).wait_recv()
        if p == pairs:
            add_rows(first[total - 1].at[0], kept.at[0], got.at[0])
            for k in range(3):
                add_rows(rest[total - 1].at[k], kept.at[k + 1], got.at[k + 1])
            return
        half, width = low.shape[0], first[count + p].shape[1]

        def body(k, carry):
            lane = k + flip * (3 - 2 * k)
            at = pl.ds(pl.multiple_of((2 * lane + x) * width, width), width)
            side = pl.ds(pl.multiple_of(k * width, width), width)
            value = rows_dot(own[:, at], grads[p][...])
            value += rows_dot(low[:, side], far[p][:half])
            value += rows_dot(high[:, side], far[p][half:])

            @pl.when(k == 0)
            def _():
                first[count + p][0] = value.astype(BF16)

            @pl.when(k > 0)
            def _():
                rest[count + p][jnp.maximum(k - 1, 0)] = value.astype(BF16)

            return carry

        lax.fori_loop(0, 4, body, 0)

    large = [g for g in late if g < count and first[g].shape[1] >= 256]
    small = [g for g in late if g < count and first[g].shape[1] < 256]
    sequence = large + list(range(count, total)) + small

    @pl.when(outer)
    def _():
        pl.semaphore_wait(barrier, 2)
        for p in range(pairs + 1):
            copy_grad(p).start()
        for g in sequence:
            if g >= count:
                multiply(g - count)
            copy_out(g).start()
        for g in list(range(ready + merged)) + sequence:
            copy_last(g).wait_recv()
            add_rows(outs[g], first[g].at[0], last[g])
        for g in late:
            copy_out(g).wait_send()

    @pl.when(inner)
    def _():
        pl.semaphore_signal(barrier, inc=1, device_id=across, device_id_type=mesh_id)
        pl.semaphore_wait(barrier, 3)
        for p in range(pairs + 1):
            copy_grad(p).start()
        for g in range(ready):
            copy_last(g).start()
        for g in range(ready, ready + merged):
            copy_in(g).start()

        def begin(g):
            copy_out(g).wait_recv()
            for k in (1, 2):
                add_rows(from_outer[g].at[k], rest[g].at[k], from_outer[g].at[k])
            copy_in(g).start()

        def finish(g):
            copy_in(g).wait_recv()
            add_rows(from_inner[g].at[1], first[g].at[0], from_inner[g].at[1])
            copy_last(g).start()
            near = [from_outer[g].at[0]] if g in late else []
            add_rows(outs[g], rest[g].at[0], from_inner[g].at[0], *near)

        for g in range(ready):
            add_rows(outs[g], first[g].at[1])
        waiting = list(range(ready, ready + merged))
        for g in sequence:
            if g >= count:
                multiply(g - count)
            begin(g)
            waiting.append(g)
            if len(waiting) > 2:
                finish(waiting.pop(0))
        for g in waiting:
            finish(g)
        for g in open_ends:
            copy_in(g).wait_send()
        for g in range(total):
            copy_last(g).wait_send()

    for p in range(pairs + 1):
        copy_grad(p).wait_send()


def line_sums(ready_parts, merged_parts, late_parts, grads, own, low, high, kept, sent):
    open_parts = list(merged_parts) + list(late_parts)
    parts = list(ready_parts) + [first for first, unused in open_parts]
    rests = [rest for unused, rest in open_parts]
    ready, merged, count, pairs = len(ready_parts), len(merged_parts), len(parts), len(grads)
    width = own.shape[1] // 8
    shapes = [p.shape[1:] for p in parts] + [(width, g.shape[1]) for g in grads] + [kept.shape[1:]]
    total, late = count + pairs + 1, shapes[ready + merged :]
    vmem = pl.BlockSpec(memory_space=pltpu.VMEM)
    sizes = [r * k for r, k in shapes]
    return pl.pallas_call(
        functools.partial(line_kernel, ready, merged, count, pairs),
        in_specs=[vmem] * (count + len(rests) + pairs + 5),
        out_specs=[vmem] * total,
        out_shape=[jax.ShapeDtypeStruct(shape, F32) for shape in shapes],
        scratch_shapes=[pltpu.VMEM((n,) + shape, BF16) for n in (1, 3) for shape in shapes[count:]]
        + [pltpu.VMEM(g.shape, BF16) for g in grads + [kept]]
        + [pltpu.VMEM((3,) + shape, BF16) for shape in late]
        + [pltpu.VMEM((2,) + shape, BF16) for shape in shapes[ready:]]
        + [pltpu.VMEM(shape, BF16) for shape in shapes]
        + [pltpu.SemaphoreType.DMA((total,))] * 6
        + [pltpu.SemaphoreType.DMA((pairs + 1,))] * 2,
        compiler_params=pltpu.CompilerParams(
            collective_id=0, has_side_effects=True, vmem_limit_bytes=56 * 2**20
        ),
        cost_estimate=cost(4 * sum(sizes), 40 * sum(sizes)),
    )(*parts, *rests, *grads, own, low, high, kept, sent)


def feed_kernel(n_ref, g_ref, u_ref, three_ref, down_ref, hid_ref, gate_ref, up_ref):
    gate = matmul(n_ref[...], g_ref[...])
    up = matmul(n_ref[...], u_ref[...])
    grad = cols_dot(three_ref[...], down_ref[...])
    square = gate * gate
    tanh = jnp.tanh(GELU_SCALE * (gate + GELU_CUBE * (gate * square)))
    half = 0.5 * (1.0 + tanh)
    gelu = gate * half
    slope = half + 0.5 * gate * (1.0 - tanh * tanh) * (
        GELU_SCALE * (1.0 + 3.0 * GELU_CUBE * square)
    )
    hid_ref[...] = (gelu * up).astype(BF16)
    gate_ref[...] = (grad * up * slope).astype(BF16)
    up_ref[...] = (grad * gelu).astype(BF16)


def feed(normed, w_gate, w_up, grad_three, w_down):
    length, model = normed.shape
    units = w_gate.shape[1]
    tile = 256
    column = lambda rows: pl.BlockSpec((rows, tile), lambda j: (0, j))
    whole = pl.BlockSpec((length, model), lambda j: (0, 0))
    return pl.pallas_call(
        feed_kernel,
        grid=(units // tile,),
        in_specs=[
            whole, column(model), column(model), whole,
            pl.BlockSpec((tile, model), lambda j: (j, 0)),
        ],
        out_specs=(column(length),) * 3,
        out_shape=(jax.ShapeDtypeStruct((length, units), BF16),) * 3,
        compiler_params=wide_params(1),
        cost_estimate=cost(6 * length * model * units, 6 * model * units + 6 * length * units),
    )(normed, w_gate, w_up, grad_three, w_down)


def feed_back_kernel(gate_ref, up_ref, g_ref, u_ref, out_ref):
    total = cols_dot(gate_ref[...], g_ref[...]) + cols_dot(up_ref[...], u_ref[...])
    out_ref[...] = total.astype(BF16)


def feed_back(grad_gate, grad_up, w_gate, w_up):
    length, units = grad_gate.shape
    model = w_gate.shape[0]
    tile = 512
    whole = pl.BlockSpec((length, units), lambda j: (0, 0))
    row = pl.BlockSpec((tile, units), lambda j: (j, 0))
    return pl.pallas_call(
        feed_back_kernel,
        grid=(model // tile,),
        in_specs=[whole, whole, row, row],
        out_specs=pl.BlockSpec((length, tile), lambda j: (0, j)),
        out_shape=jax.ShapeDtypeStruct((length, model), BF16),
        compiler_params=wide_params(1),
        cost_estimate=cost(4 * length * model * units, 4 * model * units + 4 * length * units),
    )(grad_gate, grad_up, w_gate, w_up)


def finish_kernel(turned, *refs):
    for turn, source, target in zip(turned, refs[: len(turned)], refs[len(turned) :]):
        target[...] = source[...].T if turn else source[...]


def finish(arrays, turned):
    steps = 2
    in_specs, out_specs, shapes = [], [], []
    for arr, turn in zip(arrays, turned):
        rows, width = arr.shape
        cut = rows // steps if rows // steps >= 128 else rows
        at = (lambda i: i) if cut < rows else (lambda i: 0)
        in_specs.append(pl.BlockSpec((cut, width), lambda i, at=at: (at(i), 0)))
        if turn:
            out_specs.append(pl.BlockSpec((width, cut), lambda i, at=at: (0, at(i))))
            shapes.append(jax.ShapeDtypeStruct((width, rows), F32))
        else:
            out_specs.append(pl.BlockSpec((cut, width), lambda i, at=at: (at(i), 0)))
            shapes.append(jax.ShapeDtypeStruct((rows, width), F32))
    return pl.pallas_call(
        functools.partial(finish_kernel, turned),
        grid=(steps,),
        in_specs=in_specs,
        out_specs=out_specs,
        out_shape=shapes,
        compiler_params=wide_params(1, 60),
        cost_estimate=cost(0, 8 * sum(a.size for a in arrays)),
    )(*arrays)


CHUNKS = 4


def boundary_kernel(mode, jobs, early, partial, rows, kept, gain, *refs):
    refs = list(refs)
    take = lambda size: [refs.pop(0) for unused in range(size)]
    [gains] = take(1) if mode == "last" else [None]
    wanted, along = take(jobs), take(early)
    [sums] = take(1) if mode != "first" else [None]
    [gathered] = take(1) if mode not in ("last", "sum") else [None]
    [gain_out] = take(1) if mode in ("backward", "last") else [None]
    low_out, high_out, along_out = take(jobs), take(jobs), take(early)
    from_core, far_sum, from_chip, whole = take(4)
    low, high, from_lane = take(jobs), take(jobs), take(early)
    sends, gots = take(2)
    if jobs:
        send_jobs, got_jobs = take(2)
    if early:
        send_along, got_along = take(2)
    if mode == "last":
        others, send_gains, got_gains = take(3)
    dp, mp = lax.axis_index("dp"), lax.axis_index("mp")
    core = (dp, mp + 1 - 2 * (mp % 2))
    chip = (dp, (mp + 2) % 4)
    mesh_id = pl.DeviceIdType.MESH
    step = rows.shape[0]
    size = step // CHUNKS
    barrier = pltpu.get_barrier_semaphore()
    beside = (dp + 1 - 2 * (dp % 2), mp)
    lane = dp // 2
    next_lane = ((lane + 1 - 2 * (lane % 2)) * 2 + dp % 2, mp)
    near = (core, chip, beside) if jobs else (core, chip)
    greeted = near + ((next_lane,) if early else ())
    for device in greeted:
        pl.semaphore_signal(barrier, inc=1, device_id=device, device_id_type=mesh_id)
    pl.semaphore_wait(barrier, len(greeted))

    def along_copy(k):
        return pltpu.make_async_remote_copy(
            src_ref=along[k], dst_ref=from_lane[k], send_sem=send_along.at[k],
            recv_sem=got_along.at[k], device_id=next_lane, device_id_type=mesh_id,
        )

    for k in range(early):
        along_copy(k).start()

    def job(hop, k):
        source, target = ((wanted, low), (low, high))[hop]
        return pltpu.make_async_remote_copy(
            src_ref=source[k], dst_ref=target[k], send_sem=send_jobs.at[hop, k],
            recv_sem=got_jobs.at[hop, k], device_id=(beside, core)[hop], device_id_type=mesh_id,
        )

    for k in range(jobs):
        job(0, k).start()

    def copy(kind, c, source, target, device):
        return pltpu.make_async_remote_copy(
            src_ref=source, dst_ref=target, send_sem=sends.at[kind, c], recv_sem=gots.at[kind, c],
            device_id=device, device_id_type=mesh_id,
        )

    def part(block, c):
        return pl.ds(block * step + c * size, size)

    def core_sum(block, c):
        return copy(
            block, c, partial.at[part(2 + block, c)], from_core.at[part(block, c)], core
        )

    def chip_sum(c):
        return copy(2, c, far_sum.at[part(0, c)], from_chip.at[part(0, c)], chip)

    def chip_row(c):
        return copy(3, c, whole.at[part(0, c)], whole.at[part(1, c)], chip)

    def core_row(block, c):
        return copy(
            4 + block, c, whole.at[part(block, c)], whole.at[part(2 + block, c)], core
        )

    every = range(CHUNKS)
    wide = lambda value: value.astype(F32)
    if mode != "first":
        for block in (1, 0):
            for c in every:
                core_sum(block, c).start()
        for c in every:
            core_sum(1, c).wait_recv()
            total = wide(partial[part(1, c)]) + wide(from_core[part(1, c)])
            far_sum[part(0, c)] = total.astype(BF16)
            chip_sum(c).start()
    if gain_out is not None:
        gain_out[...] = jnp.zeros_like(gain_out) if mode != "last" else gains[...]
    for c in every:
        here = part(0, c)
        if mode == "first":
            value = wide(rows[here])
        else:
            core_sum(0, c).wait_recv()
            chip_sum(c).wait_recv()
            total = wide(partial[here]) + wide(from_core[here]) + wide(from_chip[here])
            if mode in ("forward", "sum"):
                value = wide(rows[here]) + total
                sums[here] = value
            else:
                old = kept[here]
                inv = inverse_rms(old)
                weighted = gain[...] * total
                inner = jnp.mean(old * weighted, axis=-1, keepdims=True)
                value = wide(rows[here]) + inv * weighted - old * (inv * inv * inv) * inner
                gain_out[0:1] += jnp.sum(total * old * inv, axis=0, keepdims=True)
                sums[here] = value
        if gathered is not None:
            if mode != "backward":
                value = value * inverse_rms(value) * gain[...]
            whole[here] = value.astype(BF16)
            chip_row(c).start()
            core_row(0, c).start()
    if gathered is not None:
        for c in every:
            chip_row(c).wait_recv()
            core_row(1, c).start()
        for c in every:
            for block in range(2):
                core_row(block, c).wait_recv()
        gathered[...] = whole[...]
    if mode == "last":
        for k, device in enumerate(near):
            others[0] = gain_out[...]
            hop = pltpu.make_async_remote_copy(
                src_ref=others.at[0], dst_ref=others.at[k + 1], send_sem=send_gains.at[k],
                recv_sem=got_gains.at[k], device_id=device, device_id_type=mesh_id,
            )
            hop.start()
            hop.wait()
            gain_out[...] += others[k + 1]
    for k in range(jobs):
        job(0, k).wait_recv()
        job(1, k).start()
        low_out[k][...] = low[k][...]
    for k in range(jobs):
        job(0, k).wait_send()
        job(1, k).wait_recv()
        high_out[k][...] = high[k][...]
        job(1, k).wait_send()
    for k in range(early):
        along_copy(k).wait()
        along_out[k][...] = from_lane[k][...]
    for c in every:
        if mode != "first":
            core_sum(0, c).wait_send()
            core_sum(1, c).wait_send()
            chip_sum(c).wait_send()
        if gathered is not None:
            chip_row(c).wait_send()
            core_row(0, c).wait_send()
            core_row(1, c).wait_send()


def boundary(mode, number, partial, rows, kept, gain, wanted=(), gains=None, along=()):
    step, width = rows.shape
    vmem = pl.BlockSpec(memory_space=pltpu.VMEM)
    shapes = []
    if mode != "first":
        shapes.append(jax.ShapeDtypeStruct((step, width), F32))
    if mode not in ("last", "sum"):
        shapes.append(jax.ShapeDtypeStruct((4 * step, width), BF16))
    if mode in ("backward", "last"):
        shapes.append(jax.ShapeDtypeStruct((1 if mode == "backward" else 8, width), F32))
    given = [gains] if mode == "last" else []
    jobs, early = len(wanted), len(along)
    moved = list(wanted) * 2 + list(along)
    shapes += [jax.ShapeDtypeStruct(w.shape, BF16) for w in moved]
    scratch = [pltpu.VMEM(w.shape, BF16) for w in moved]
    outs = pl.pallas_call(
        functools.partial(boundary_kernel, mode, jobs, early),
        in_specs=[vmem] * (4 + len(given) + jobs + early),
        out_specs=[vmem] * len(shapes),
        out_shape=shapes,
        scratch_shapes=[
            pltpu.VMEM((2 * step, width), BF16),
            pltpu.VMEM((step, width), BF16),
            pltpu.VMEM((step, width), BF16),
            pltpu.VMEM((4 * step, width), BF16),
        ]
        + scratch
        + [pltpu.SemaphoreType.DMA((6, CHUNKS))] * 2
        + ([pltpu.SemaphoreType.DMA((2, jobs))] * 2 if jobs else [])
        + ([pltpu.SemaphoreType.DMA((early,))] * 2 if early else [])
        + (
            [pltpu.VMEM((4, 8, width), F32)] + [pltpu.SemaphoreType.DMA((3,))] * 2
            if mode == "last"
            else []
        ),
        compiler_params=pltpu.CompilerParams(
            collective_id=number, has_side_effects=True, vmem_limit_bytes=22 * 2**20
        ),
        cost_estimate=cost(10 * step * width, 60 * 2**20),
    )(partial, rows, kept, gain, *given, *wanted, *along)
    if not jobs:
        return outs
    outs = list(outs)
    plain = len(outs) - 2 * jobs - early
    halves = list(zip(outs[plain : plain + jobs], outs[plain + jobs :]))
    return outs[:plain] + halves + outs[plain + 2 * jobs :]


def layer(n_dp, n_mp):
    lanes = n_dp // 2
    paired = n_dp == 8

    def swap(value, axis, size, bit):
        return lax.ppermute(value, axis, [(i, i ^ bit) for i in range(size)])

    def core(value):
        return swap(value, "mp", n_mp, 1)

    def chip(value):
        return swap(value, "mp", n_mp, 2)

    def beside(value):
        return swap(value, "dp", n_dp, 1)

    def gather(mine):
        far = chip(mine)
        return assemble([mine, far, core(mine), core(far)])

    def gather_after(mine, after):
        return gather(tie(mine, after))

    def scatter_rows(partial):
        step = partial.shape[0] // 4
        block = [partial[k * step : (k + 1) * step] for k in range(4)]
        far = (block[1].astype(F32) + core(block[3]).astype(F32)).astype(BF16)
        far_in = chip(far)
        return block[0].astype(F32) + core(block[2]).astype(F32) + far_in.astype(F32)

    def line_place():
        z = lax.axis_index("dp") // 2
        number = lambda value: jnp.asarray(value).astype(jnp.int32)
        return lax.axis_index("dp") % 2, number(z >= 2), number((z == 1) | (z == 2))

    def outer_swap(value):
        return swap(value, "dp", n_dp, 2)

    def inner_swap(value):
        pairs = []
        for d in range(n_dp):
            for m in range(n_mp):
                inner = d // 2 in (1, 2)
                to = (d ^ 6) * n_mp + m if inner else d * n_mp + (m ^ 1)
                pairs.append((d * n_mp + m, to))
        return lax.ppermute(value, ("dp", "mp"), pairs)

    def lane_columns(parity):
        flip = line_place()[1]
        k = jnp.arange(4, dtype=jnp.int32)
        return 2 * (k + flip * (3 - 2 * k)) + parity

    def wanted_of(value, half=None):
        rows = value.shape[0] // 2
        if half is not None:
            value = pick_rows(jnp.stack([half]).astype(jnp.int32), value, rows)
        x = line_place()[0]
        return pick_columns(lane_columns(1 - x), value, rows, value.shape[1] // n_dp)

    def shards(
        tokens, norm_gains, w_query, w_key, w_value, w_out, c_query, c_key, c_value, c_out,
        patch_proj, w_gate, w_up, w_down, patches, segment_ids, image_index, cotangent,
    ):
        length = segment_ids.shape[1]
        model = tokens.shape[2]
        patch_rows = patches.shape[0] * patches.shape[1]
        m = lax.axis_index("mp")
        order = [m, m ^ 2, m ^ 1, m ^ 3]

        def blocks(arr, axis=0):
            step = arr.shape[axis] // 4
            return jnp.concatenate(
                [lax.dynamic_slice_in_dim(arr, k * step, step, axis) for k in order], axis=axis
            )

        places = blocks(jnp.arange(length, dtype=jnp.int32))
        segment_row = blocks(segment_ids[0])
        slots = jnp.arange(SEGS, dtype=jnp.int32)
        token_image = jnp.sum(
            jnp.where(segment_row[:, None] == slots, image_index[0][None, :], 0), axis=-1
        )
        patch_image = jnp.arange(patch_rows, dtype=jnp.int32) // patches.shape[1]

        far_of = beside if paired else (lambda value: value)
        core_bit = m % 2

        def exchange(*values):
            return [wanted_of(*value) for value in values] if paired else []

        def split(value, halves):
            return (value, *halves) if paired else (value,)

        def split_now(value):
            if not paired:
                return (value,)
            wanted = wanted_of(value)
            low = beside(wanted)
            return value, low, core(low)

        self_rows = jnp.stack([segment_row, places], axis=1)
        self_cols = self_rows.T
        cross_rows, cross_cols = token_image[:, None], patch_image[None, :]
        residual = tokens[0].astype(F32)
        gain_rows = [norm_gains[k : k + 1] for k in range(3)]
        nothing = jnp.zeros((16, 128), BF16)
        none = [None] * 4
        [normed_one] = boundary("first", 1, nothing, tokens[0], nothing, gain_rows[0])
        patch_own = patches.reshape(patch_rows, patches.shape[2])
        projected = matmul(patch_own, patch_proj).astype(BF16)
        queries = matmul(normed_one, w_query).astype(BF16)
        key_rows = matmul(normed_one, w_key).astype(BF16)
        value_rows = matmul(normed_one, w_value).astype(BF16)
        self_mixed = attend(queries, key_rows, value_rows, self_rows, self_cols, True)
        self_far = far_of(self_mixed)
        grad_three = gather_after(cotangent[0], normed_one)
        split_one = split_now(normed_one)
        self_mixed = tie(self_mixed, (grad_three, split_one))
        partial = matmul(self_mixed, w_out).astype(BF16)
        after_self, normed_two, *halves = boundary(
            "forward", 2, partial, tokens[0], nothing, gain_rows[1], exchange((projected, core_bit))
        )
        patch_low, patch_high = halves[0] if paired else (None, None)
        normed_two = tie(normed_two, self_far)
        cross_keys = matmul(projected, c_key).astype(BF16)
        cross_values = matmul(projected, c_value).astype(BF16)
        cross_queries = matmul(normed_two, c_query).astype(BF16)
        cross_mixed = attend(
            cross_queries, cross_keys, cross_values, cross_rows, cross_cols, False
        )
        partial = matmul(cross_mixed, c_out).astype(BF16)
        after_cross, normed_three, *halves = boundary(
            "forward", 3, partial, after_self, nothing, gain_rows[2],
            exchange((grad_three,), (normed_two,)),
        )
        split_cotangent, split_two = map(split, (grad_three, normed_two), halves or none)
        if paired:
            wanted = wanted_of(normed_three)
            low_three = beside(wanted)
            split_three = normed_three, low_three, core(low_three)
            normed_three = tie(normed_three, wanted)
        else:
            split_three, low_three = (normed_three,), normed_three
        hidden, grad_gate, grad_up = feed(normed_three, w_gate, w_up, grad_three, w_down)

        results, turned = {}, {}

        def line(name, split, grad, grad_far, rows_first, after=(), pick=None):
            turned[name] = not rows_first
            if not paired:
                grad = grad if pick is None else grad[pick]
                partial = product("td,te->de", split[0], grad).astype(BF16)
                total = lax.psum_scatter(partial, "dp", scatter_dimension=0, tiled=True)
                results[name] = total.astype(F32)
                return ()
            results[name] = pair_grad(
                lane_columns(line_place()[0]), *split, grad, grad_far, after, pick
            )
            return results[name]

        def line_out(name):
            return outer_swap(results[name][1]) if paired else None

        def line_merge(name, incoming, after):
            if paired:
                first, rest = results[name]
                results[name] = first, merge(rest, incoming, after)

        def line_across(name):
            if paired:
                inner = line_place()[2]
                first, rest = results[name]
                results[name] = cross_add(inner.reshape(1), first, rest, inner_swap(rest[1:]))

        hidden_far = far_of(tie(hidden, low_three))
        partial = feed_back(grad_gate, grad_up, w_gate, w_up)
        gate_far, up_far = [far_of(v) for v in tie((grad_gate, grad_up), partial)]
        partial_out = matmul(tie(hidden, partial), w_down).astype(BF16)
        [output] = boundary("sum", 7, partial_out, after_cross, nothing, gain_rows[0])
        sent = line("down", split_cotangent, hidden, hidden_far, False, (output,))
        incoming_down = line_out("down")
        grad_rows, grad_two, gain_three = boundary(
            "backward", 4, tie(partial, sent), cotangent[0], after_cross, gain_rows[2]
        )
        sent = line("gate", split_three, grad_gate, gate_far, True, (grad_two,))
        incoming_gate = line_out("gate")
        grad_two = tie(grad_two, sent)

        grad_mixed = product("sd,ed->se", grad_two, c_out).astype(BF16)
        grad_cq, grad_ckv = attend_back(
            cross_queries, cross_keys, cross_values, cross_rows, cross_cols, grad_mixed, False
        )
        cq_far, ckv_far = far_of(grad_cq), far_of(grad_ckv)
        partial = product("se,de->sd", grad_cq, c_query).astype(BF16)
        sent = line("up", split_three, grad_up, up_far, True, (partial,))
        incoming_up = line_out("up")
        line_merge("down", incoming_down, (partial,))
        grad_rows, grad_one, gain_two = boundary(
            "backward", 5, tie(partial, (sent, results["down"])), grad_rows, after_self, gain_rows[1]
        )
        line_across("down")

        width = model // (n_dp * n_mp)

        def projected_block(k):
            def rows_of(weight):
                cut = weight.reshape(n_dp, n_mp, width, weight.shape[1])
                return lax.dynamic_index_in_dim(cut, k, 1, keepdims=False).reshape(
                    n_dp * width, weight.shape[1]
                )

            return (
                cols_dot(grad_ckv_late[0], rows_of(c_key))
                + cols_dot(grad_ckv_late[1], rows_of(c_value))
            ).astype(
                BF16
            )

        grad_ckv_late = tie(grad_ckv, grad_one)
        block = [projected_block(k) for k in order]
        far_core = core(block[3])

        grad_mixed = product(
            "sd,ed->se", tie(grad_one, (block[1], block[3])), w_out
        ).astype(BF16)
        grad_sq, grad_sk, grad_sv = attend_back(
            queries, key_rows, value_rows, self_rows, self_cols, grad_mixed, True
        )
        far = (block[1].astype(F32) + far_core.astype(F32)).astype(BF16)
        grad_sq, grad_sk, grad_sv = tie((grad_sq, grad_sk, grad_sv), far)
        far_in = chip(far)
        near = (block[0].astype(F32) + core(block[2]).astype(F32)).astype(BF16)
        partial = (
            product("se,de->sd", grad_sq, w_query)
            + product("se,de->sd", grad_sk, w_key)
            + product("se,de->sd", grad_sv, w_value)
        ).astype(BF16)
        line_merge("gate", incoming_gate, (partial,))
        line("c_query", split_two, grad_cq, cq_far, True, (partial,))
        split_patch = (projected,)
        if paired:
            swapped = core_bit == 1
            split_patch = (
                projected,
                jnp.where(swapped, patch_high, patch_low),
                jnp.where(swapped, patch_low, patch_high),
            )
        sent = line("c_key", split_patch, grad_ckv, ckv_far, True, (partial,), 0)
        gains = jnp.pad(jnp.concatenate([gain_two, gain_three], axis=0), ((1, 5), (0, 0)))
        along = [results["c_query"][1], results["c_key"][1]] if paired else []
        grad_rows, gains_near, *halves = boundary(
            "last", 6, tie(partial, (sent, far, near, results["gate"], results["down"])), grad_rows,
            residual, gain_rows[0], exchange((grad_two,), (grad_one,)), gains, along,
        )
        if paired:
            line_merge("c_query", halves[2], ())
            line_merge("c_key", halves[3], ())
        mixed_far = far_of(tie(cross_mixed, grad_rows))
        line_across("gate")
        split_grad_two, split_grad_one = map(split, (grad_two, grad_one), halves[:2] or none)
        grad_projected = (near.astype(F32) + far_in.astype(F32)).astype(BF16)
        patch_partial = rows_dot(grad_projected, patch_own).astype(BF16)
        x, flip, unused = line_place()
        patch_parts = patch_partial.reshape(n_dp // 2, 2, width, patches.shape[2])
        patch_sent = lax.dynamic_index_in_dim(patch_parts, 1 - x, 1, keepdims=False)
        line("c_value", split_patch, grad_ckv, ckv_far, True, (grad_rows,), 1)
        line("c_out", split_grad_two, cross_mixed, mixed_far, False, (grad_rows,))
        line("w_out", split_grad_one, self_mixed, self_far, False, (grad_rows,))
        line_merge("up", incoming_up, (grad_rows,))
        if paired:
            patch_kept = lax.dynamic_index_in_dim(patch_parts, x, 1, keepdims=False)
            patch_kept, patch_sent = [
                jnp.where(flip == 1, v.astype(F32)[::-1], v.astype(F32)).astype(BF16)
                for v in (patch_kept, patch_sent)
            ]
            mine = lax.dynamic_index_in_dim(
                gains_near[:3].reshape(3, 4, 2, n_mp, width), x, 2, keepdims=False
            )
            mine = lax.dynamic_index_in_dim(mine, m, 2, keepdims=False).transpose(1, 0, 2)
            mine = jnp.where(flip == 1, mine[::-1], mine)
            mine = jnp.pad(mine, ((0, 0), (0, 29), (0, 128 - width))).astype(BF16)
            results["gains"] = mine[:1], mine[1:]
            early, late = ["down", "gate"], ["c_value", "w_out", "c_out"]
            merged = ["up", "c_query", "c_key"]
            late.append("gains")
            names = early + merged + late + ["w_query", "w_key", "w_value", "patch"]
            sums = line_sums(
                *[[results[n] for n in group] for group in (early, merged, late)],
                [grad_sq, grad_sk, grad_sv], *split_one, patch_kept, patch_sent,
            )
            results.update(zip(names, sums))
        else:
            results["patch"] = lax.psum_scatter(
                patch_partial, "dp", scatter_dimension=0, tiled=True
            ).astype(F32)
            line("w_query", split_one, grad_sq, grad_sq, True)
            line("w_key", split_one, grad_sk, grad_sk, True)
            line("w_value", split_one, grad_sv, grad_sv, True)
        turned["patch"] = True
        names = [n for n in results if n != "gains"]
        turns = tuple(bool(turned.get(n)) for n in names)
        results.update(zip(names, finish([results[n] for n in names], turns)))
        patch_total = results["patch"]
        if paired:
            gain_total = results["gains"][:3, :width]
        else:
            gain_total = lax.dynamic_index_in_dim(
                gains_near[:3].reshape(3, n_dp, n_mp, width), m, 2, keepdims=False
            )
            gain_total = lax.psum_scatter(
                gain_total.reshape(3, n_dp * width), "dp", scatter_dimension=1, tiled=True
            )
        sum_query, sum_key, sum_value = results["w_query"], results["w_key"], results["w_value"]
        sum_cquery, sum_ckey, sum_cvalue = results["c_query"], results["c_key"], results["c_value"]
        sum_out, sum_cout, sum_down = results["w_out"], results["c_out"], results["down"]
        sum_gate, sum_up = results["gate"], results["up"]
        return (
            output.astype(BF16)[None], grad_rows[None], gain_total,
            sum_query, sum_key, sum_value, sum_out,
            sum_cquery, sum_ckey, sum_cvalue, sum_cout,
            patch_total, sum_gate, sum_up, sum_down,
        )

    return shards


def solution(mesh):
    columns, rows = P(None, "mp"), P("mp", None)
    return jax.shard_map(
        layer(mesh.shape["dp"], mesh.shape["mp"]),
        mesh=mesh,
        in_specs=(
            P("dp", "mp", None), P(), columns, columns, columns, rows, columns, columns, columns,
            rows, P(), columns, columns, rows, P("dp", None, None), P("dp", None), P("dp", None),
            P("dp", "mp", None),
        ),
        out_specs=(
            P("dp", "mp", None), P("dp", "mp", None), P(None, ("dp", "mp")),
            P("dp", "mp"), P("dp", "mp"), P("dp", "mp"), P("mp", "dp"),
            P("dp", "mp"), P("dp", "mp"), P("dp", "mp"), P("mp", "dp"),
            P(None, ("dp", "mp")), P("dp", "mp"), P("dp", "mp"), P("mp", "dp"),
        ),
        check_vma=False,
    )
```

```python
import functools

import jax
import jax.numpy as jnp
from jax import lax
from jax.experimental import pallas as pl
from jax.experimental.pallas import tpu as pltpu
from jax.sharding import PartitionSpec as P

HEAD_DIM = 128
SEGS = 4
EPSILON = 1e-06
MASKED = -1000000000.0
F32 = jnp.float32
BF16 = jnp.bfloat16


def matmul(left, right):
    return jnp.dot(left, right, preferred_element_type=F32)


def product(spec, left, right):
    return jnp.einsum(spec, left, right, preferred_element_type=F32)


def rows_dot(left, right):
    return lax.dot_general(left, right, (((0,), (0,)), ((), ())), preferred_element_type=F32)


def cols_dot(left, right):
    return lax.dot_general(left, right, (((1,), (1,)), ((), ())), preferred_element_type=F32)


def tie(value, after):
    return lax.optimization_barrier((value, after))[0]


def inverse_rms(rows):
    return lax.rsqrt(jnp.mean(rows * rows, axis=-1, keepdims=True) + EPSILON)


def norm_rows(rows, gain):
    return (rows * inverse_rms(rows) * gain).astype(BF16)


def norm_back(rows, gain, grad):
    inv = inverse_rms(rows)
    weighted = gain * grad
    inner = jnp.mean(rows * weighted, axis=-1, keepdims=True)
    grad_rows = inv * weighted - rows * (inv * inv * inv) * inner
    return grad_rows, jnp.sum(grad * rows * inv, axis=0)


VMEM_LIMIT = 16 * 2**20
GELU_SCALE = 0.7978845608028654
GELU_CUBE = 0.044715
ANY = pl.BlockSpec(memory_space=pl.ANY)


def params(grid_rank):
    return pltpu.CompilerParams(
        dimension_semantics=("arbitrary",) * grid_rank, vmem_limit_bytes=VMEM_LIMIT
    )


def wide_params(grid_rank, size=24):
    return pltpu.CompilerParams(
        dimension_semantics=("arbitrary",) * grid_rank, vmem_limit_bytes=size * 2**20
    )


def cost(flops, size):
    return pl.CostEstimate(flops=flops, bytes_accessed=size, transcendentals=0)


def masked_scores(q_ref, k_ref, row_ref, col_ref, causal):
    scores = cols_dot(q_ref[...], k_ref[...]) * (HEAD_DIM ** (-0.5))
    allowed = row_ref[:, 0:1] == col_ref[0:1, :]
    if causal:
        allowed = allowed & (col_ref[1:2, :] <= row_ref[:, 1:2])
    return jnp.where(allowed, scores, MASKED)


def attend_kernel(causal, q_ref, k_ref, v_ref, row_ref, col_ref, out_ref):
    scores = masked_scores(q_ref, k_ref, row_ref, col_ref, causal)
    exponent = jnp.exp(scores - jnp.max(scores, axis=-1, keepdims=True))
    total = jnp.sum(exponent, axis=-1, keepdims=True)
    weights = (exponent * (1.0 / total)).astype(BF16)
    out_ref[...] = matmul(weights, v_ref[...]).astype(BF16)


def attend(queries, keys, values, rows, cols, causal):
    length, width = queries.shape
    spots = keys.shape[0]
    head = lambda size: pl.BlockSpec((size, HEAD_DIM), lambda h: (0, h))
    whole = lambda arr: pl.BlockSpec(arr.shape, lambda h: (0, 0))
    return pl.pallas_call(
        functools.partial(attend_kernel, causal),
        grid=(width // HEAD_DIM,),
        in_specs=[head(length), head(spots), head(spots), whole(rows), whole(cols)],
        out_specs=head(length),
        out_shape=jax.ShapeDtypeStruct((length, width), BF16),
        compiler_params=params(1),
        cost_estimate=pl.CostEstimate(
            flops=4 * length * spots * width,
            bytes_accessed=4 * (length + spots) * width,
            transcendentals=length * spots * width // HEAD_DIM,
        ),
    )(queries, keys, values, rows, cols)


def attend_back_kernel(causal, q_ref, k_ref, v_ref, row_ref, col_ref, do_ref, dq_ref, dk_ref, dv_ref):
    scale = HEAD_DIM ** (-0.5)
    scores = masked_scores(q_ref, k_ref, row_ref, col_ref, causal)
    exponent = jnp.exp(scores - jnp.max(scores, axis=-1, keepdims=True))
    weights = exponent * (1.0 / jnp.sum(exponent, axis=-1, keepdims=True))
    grad_weights = cols_dot(do_ref[...], v_ref[...])
    inner = jnp.sum(weights * grad_weights, axis=-1, keepdims=True)
    grad_scores = (weights * (grad_weights - inner)).astype(BF16)
    dq_ref[...] = (matmul(grad_scores, k_ref[...]) * scale).astype(BF16)
    dk_ref[...] = (rows_dot(grad_scores, q_ref[...]) * scale).astype(BF16)
    dv_ref[...] = rows_dot(weights.astype(BF16), do_ref[...]).astype(BF16)


def self_back_kernel(q_ref, k_ref, v_ref, row_ref, col_ref, do_ref, *outs):
    attend_back_kernel(
        True, q_ref, k_ref, v_ref, row_ref, col_ref, do_ref,
        *outs,
    )


def cross_back_kernel(q_ref, k_ref, v_ref, row_ref, col_ref, do_ref, dq_ref, out_ref):
    attend_back_kernel(
        False, q_ref, k_ref, v_ref, row_ref, col_ref, do_ref,
        dq_ref, out_ref.at[0], out_ref.at[1],
    )


def attend_back(queries, keys, values, rows, cols, grad_out, causal):
    length, width = queries.shape
    spots = keys.shape[0]
    head = lambda size: pl.BlockSpec((size, HEAD_DIM), lambda h: (0, h))
    whole = lambda arr: pl.BlockSpec(arr.shape, lambda h: (0, 0))
    shape = lambda *dims: jax.ShapeDtypeStruct(dims, BF16)
    if causal:
        out_specs, out_shape = (head(length),) * 3, (shape(length, width),) * 3
    else:
        out_specs = (head(length), pl.BlockSpec((2, spots, HEAD_DIM), lambda h: (0, 0, h)))
        out_shape = (shape(length, width), shape(2, spots, width))
    return pl.pallas_call(
        self_back_kernel if causal else cross_back_kernel,
        grid=(width // HEAD_DIM,),
        in_specs=[
            head(length), head(spots), head(spots), whole(rows), whole(cols), head(length),
        ],
        out_specs=out_specs,
        out_shape=out_shape,
        compiler_params=params(1),
        cost_estimate=pl.CostEstimate(
            flops=10 * length * spots * width,
            bytes_accessed=8 * (length + spots) * width,
            transcendentals=length * spots * width // HEAD_DIM,
        ),
    )(queries, keys, values, rows, cols, grad_out)


def assemble_kernel(*refs):
    *blocks, out_ref = refs
    step = blocks[0].shape[0]
    for k, block in enumerate(blocks):
        out_ref[k * step : (k + 1) * step] = block[...]


def assemble(blocks):
    step, width = blocks[0].shape
    columns = 512
    return pl.pallas_call(
        assemble_kernel,
        grid=(width // columns,),
        in_specs=[pl.BlockSpec((step, columns), lambda j: (0, j))] * len(blocks),
        out_specs=pl.BlockSpec((len(blocks) * step, columns), lambda j: (0, j)),
        out_shape=jax.ShapeDtypeStruct((len(blocks) * step, width), blocks[0].dtype),
        compiler_params=params(1),
        cost_estimate=cost(0, 4 * len(blocks) * step * width),
    )(*blocks)


def copy_kernel(at_ref, in_ref, out_ref):
    out_ref[...] = in_ref[...]


def pick_rows(at, arr, step):
    count, width = at.shape[0], arr.shape[1]
    return pl.pallas_call(
        copy_kernel,
        grid_spec=pltpu.PrefetchScalarGridSpec(
            num_scalar_prefetch=1,
            grid=(count,),
            in_specs=[pl.BlockSpec((step, width), lambda k, at: (at[k], 0))],
            out_specs=pl.BlockSpec((step, width), lambda k, at: (k, 0)),
        ),
        out_shape=jax.ShapeDtypeStruct((count * step, width), arr.dtype),
        compiler_params=params(1),
        cost_estimate=cost(0, 4 * count * step * width),
    )(at, arr)


def pick_columns(at, arr, rows, width):
    count = at.shape[0]
    return pl.pallas_call(
        copy_kernel,
        grid_spec=pltpu.PrefetchScalarGridSpec(
            num_scalar_prefetch=1,
            grid=(count,),
            in_specs=[pl.BlockSpec((rows, width), lambda k, at: (0, at[k]))],
            out_specs=pl.BlockSpec((rows, width), lambda k, at: (0, k)),
        ),
        out_shape=jax.ShapeDtypeStruct((rows, count * width), arr.dtype),
        compiler_params=params(1),
        cost_estimate=cost(0, 4 * count * rows * width),
    )(at, arr)


def pair_kernel(at_ref, a_ref, lo_ref, hi_ref, g_ref, far_ref, *rest):
    half = lo_ref.shape[0]
    if len(g_ref.shape) == 3:
        g_ref, far_ref = g_ref.at[0], far_ref.at[0]
    total = rows_dot(a_ref[...], g_ref[...])
    total += rows_dot(lo_ref[...], far_ref[:half])
    total += rows_dot(hi_ref[...], far_ref[half:])
    first_ref, rest_ref = rest[-2:]

    @pl.when(pl.program_id(0) == 0)
    def _():
        first_ref[0] = total.astype(BF16)

    @pl.when(pl.program_id(0) > 0)
    def _():
        rest_ref[0] = total.astype(BF16)


def pair_grad(at, own, low, high, grad, grad_far, after, pick=None):
    length, units = grad.shape[-2:]
    width = own.shape[1] // 8
    whole = pl.BlockSpec((length, units), lambda k, at: (0, 0))
    if pick is not None:
        whole = pl.BlockSpec((1, length, units), lambda k, at: (pick, 0, 0))
    side = pl.BlockSpec((length // 2, width), lambda k, at: (0, k))
    return pl.pallas_call(
        pair_kernel,
        grid_spec=pltpu.PrefetchScalarGridSpec(
            num_scalar_prefetch=1,
            grid=(4,),
            in_specs=[
                pl.BlockSpec((length, width), lambda k, at: (0, at[k])), side, side, whole, whole,
            ] + [ANY] * len(after),
            out_specs=(
                pl.BlockSpec((1, width, units), lambda k, at: (0, 0, 0)),
                pl.BlockSpec((1, width, units), lambda k, at: (jnp.maximum(k - 1, 0), 0, 0)),
            ),
        ),
        out_shape=tuple(jax.ShapeDtypeStruct((n, width, units), BF16) for n in (1, 3)),
        compiler_params=params(1),
        cost_estimate=cost(
            16 * length * width * units, 2 * units * (2 * length + 4 * width) + 16 * length * width
        ),
    )(at, own, low, high, grad, grad_far, *after)


def merge_kernel(left_ref, right_ref, *rest):
    rest[-1][...] = (left_ref[...].astype(F32) + right_ref[...].astype(F32)).astype(BF16)


def merge(left, right, after):
    spec = pl.BlockSpec((1,) + left.shape[1:], lambda k: (k, 0, 0))
    return pl.pallas_call(
        merge_kernel,
        grid=(left.shape[0],),
        in_specs=[spec, spec] + [ANY] * len(after),
        out_specs=spec,
        out_shape=jax.ShapeDtypeStruct(left.shape, BF16),
        compiler_params=params(1),
        cost_estimate=cost(left.size, 6 * left.size),
    )(left, right, *after)


def cross_kernel(at_ref, first_ref, rest_ref, in_ref, out_ref):
    part = jnp.where(pl.program_id(0) == 0, first_ref[...], rest_ref[...]).astype(F32)
    keep = jnp.where(at_ref[0] == 1, in_ref[...].astype(F32), 0.0)
    out_ref[...] = (part + keep).astype(BF16)


def cross_add(inner, first, rest, crossed):
    block = (1,) + rest.shape[1:]
    here = pl.BlockSpec(block, lambda k, at: (0, 0, 0))
    return pl.pallas_call(
        cross_kernel,
        grid_spec=pltpu.PrefetchScalarGridSpec(
            num_scalar_prefetch=1,
            grid=(2,),
            in_specs=[here, here, pl.BlockSpec(block, lambda k, at: (1 - k, 0, 0))],
            out_specs=pl.BlockSpec(block, lambda k, at: (k, 0, 0)),
        ),
        out_shape=jax.ShapeDtypeStruct((2,) + rest.shape[1:], BF16),
        compiler_params=params(1),
        cost_estimate=cost(crossed.size, 6 * crossed.size),
    )(inner, first, rest, crossed)


def add_rows(target, *sources):
    step = 32

    def body(i, carry):
        rows = pl.ds(pl.multiple_of(i * step, step), step)
        total = sources[0][rows].astype(F32)
        for source in sources[1:]:
            total = total + source[rows].astype(F32)
        target[rows] = total.astype(target.dtype)
        return carry

    lax.fori_loop(0, target.shape[0] // step, body, 0)


def line_kernel(ready, merged, count, pairs, *refs):
    refs = list(refs)
    take = lambda size: [refs.pop(0) for unused in range(size)]
    total = count + pairs + 1
    first = take(count)
    rest = dict(zip(range(ready, count), take(count - ready)))
    grads, [own, low, high, kept, sent] = take(pairs), take(5)
    outs = take(total)
    late = range(ready + merged, total)
    open_ends = range(ready, total)
    first += take(pairs + 1)
    rest.update(zip(range(count, total), take(pairs + 1)))
    far = take(pairs)
    [got] = take(1)
    from_outer = dict(zip(late, take(len(late))))
    from_inner = dict(zip(open_ends, take(len(open_ends))))
    last = take(total)
    send_out, got_out, send_in, got_in, send_last, got_last, send_x, got_x = refs
    dp, mp = lax.axis_index("dp"), lax.axis_index("mp")
    z, x = dp // 2, dp % 2
    beside = ((z + 1 - 2 * (z % 2)) * 2 + x, mp)
    across = ((3 - z) * 2 + x, mp)
    partner = (z * 2 + 1 - x, mp)
    flip = z // 2
    inner = (z == 1) | (z == 2)
    outer = (z == 0) | (z == 3)
    mesh_id = pl.DeviceIdType.MESH
    barrier = pltpu.get_barrier_semaphore()
    for device in (beside, partner):
        pl.semaphore_signal(barrier, inc=1, device_id=device, device_id_type=mesh_id)

    def copy(source, target, sent, got, device):
        return pltpu.make_async_remote_copy(
            src_ref=source, dst_ref=target, send_sem=sent, recv_sem=got,
            device_id=device, device_id_type=mesh_id,
        )

    def copy_out(g):
        return copy(rest[g], from_outer[g], send_out.at[g], got_out.at[g], beside)

    def copy_in(g):
        source = (from_outer if g in late else rest)[g].at[pl.ds(1, 2)]
        return copy(source, from_inner[g], send_in.at[g], got_in.at[g], across)

    def copy_last(g):
        source = first[g].at[0] if g < ready else from_inner[g].at[1]
        return copy(source, last[g], send_last.at[g], got_last.at[g], beside)

    def copy_grad(p):
        source, target = (grads[p], far[p]) if p < pairs else (sent, got)
        return copy(source, target, send_x.at[p], got_x.at[p], partner)

    def multiply(p):
        copy_grad(p).wait_recv()
        if p == pairs:
            add_rows(first[total - 1].at[0], kept.at[0], got.at[0])
            for k in range(3):
                add_rows(rest[total - 1].at[k], kept.at[k + 1], got.at[k + 1])
            return
        half, width = low.shape[0], first[count + p].shape[1]

        def body(k, carry):
            lane = k + flip * (3 - 2 * k)
            at = pl.ds(pl.multiple_of((2 * lane + x) * width, width), width)
            side = pl.ds(pl.multiple_of(k * width, width), width)
            value = rows_dot(own[:, at], grads[p][...])
            value += rows_dot(low[:, side], far[p][:half])
            value += rows_dot(high[:, side], far[p][half:])

            @pl.when(k == 0)
            def _():
                first[count + p][0] = value.astype(BF16)

            @pl.when(k > 0)
            def _():
                rest[count + p][jnp.maximum(k - 1, 0)] = value.astype(BF16)

            return carry

        lax.fori_loop(0, 4, body, 0)

    large = [g for g in late if g < count and first[g].shape[1] >= 256]
    small = [g for g in late if g < count and first[g].shape[1] < 256]
    sequence = large + list(range(count, total)) + small

    @pl.when(outer)
    def _():
        pl.semaphore_wait(barrier, 2)
        for p in range(pairs + 1):
            copy_grad(p).start()
        for g in sequence:
            if g >= count:
                multiply(g - count)
            copy_out(g).start()
        for g in list(range(ready + merged)) + sequence:
            copy_last(g).wait_recv()
            add_rows(outs[g], first[g].at[0], last[g])
        for g in late:
            copy_out(g).wait_send()

    @pl.when(inner)
    def _():
        pl.semaphore_signal(barrier, inc=1, device_id=across, device_id_type=mesh_id)
        pl.semaphore_wait(barrier, 3)
        for p in range(pairs + 1):
            copy_grad(p).start()
        for g in range(ready):
            copy_last(g).start()
        for g in range(ready, ready + merged):
            copy_in(g).start()

        def begin(g):
            copy_out(g).wait_recv()
            for k in (1, 2):
                add_rows(from_outer[g].at[k], rest[g].at[k], from_outer[g].at[k])
            copy_in(g).start()

        def finish(g):
            copy_in(g).wait_recv()
            add_rows(from_inner[g].at[1], first[g].at[0], from_inner[g].at[1])
            copy_last(g).start()
            near = [from_outer[g].at[0]] if g in late else []
            add_rows(outs[g], rest[g].at[0], from_inner[g].at[0], *near)

        for g in range(ready):
            add_rows(outs[g], first[g].at[1])
        waiting = list(range(ready, ready + merged))
        for g in sequence:
            if g >= count:
                multiply(g - count)
            begin(g)
            waiting.append(g)
            if len(waiting) > 2:
                finish(waiting.pop(0))
        for g in waiting:
            finish(g)
        for g in open_ends:
            copy_in(g).wait_send()
        for g in range(total):
            copy_last(g).wait_send()

    for p in range(pairs + 1):
        copy_grad(p).wait_send()


def line_sums(ready_parts, merged_parts, late_parts, grads, own, low, high, kept, sent):
    open_parts = list(merged_parts) + list(late_parts)
    parts = list(ready_parts) + [first for first, unused in open_parts]
    rests = [rest for unused, rest in open_parts]
    ready, merged, count, pairs = len(ready_parts), len(merged_parts), len(parts), len(grads)
    width = own.shape[1] // 8
    shapes = [p.shape[1:] for p in parts] + [(width, g.shape[1]) for g in grads] + [kept.shape[1:]]
    total, late = count + pairs + 1, shapes[ready + merged :]
    vmem = pl.BlockSpec(memory_space=pltpu.VMEM)
    sizes = [r * k for r, k in shapes]
    return pl.pallas_call(
        functools.partial(line_kernel, ready, merged, count, pairs),
        in_specs=[vmem] * (count + len(rests) + pairs + 5),
        out_specs=[vmem] * total,
        out_shape=[jax.ShapeDtypeStruct(shape, F32) for shape in shapes],
        scratch_shapes=[pltpu.VMEM((n,) + shape, BF16) for n in (1, 3) for shape in shapes[count:]]
        + [pltpu.VMEM(g.shape, BF16) for g in grads + [kept]]
        + [pltpu.VMEM((3,) + shape, BF16) for shape in late]
        + [pltpu.VMEM((2,) + shape, BF16) for shape in shapes[ready:]]
        + [pltpu.VMEM(shape, BF16) for shape in shapes]
        + [pltpu.SemaphoreType.DMA((total,))] * 6
        + [pltpu.SemaphoreType.DMA((pairs + 1,))] * 2,
        compiler_params=pltpu.CompilerParams(
            collective_id=0, has_side_effects=True, vmem_limit_bytes=53 * 2**20
        ),
        cost_estimate=cost(4 * sum(sizes), 40 * sum(sizes)),
    )(*parts, *rests, *grads, own, low, high, kept, sent)


def feed_kernel(n_ref, g_ref, u_ref, three_ref, down_ref, hid_ref, gate_ref, up_ref):
    gate = matmul(n_ref[...], g_ref[...])
    up = matmul(n_ref[...], u_ref[...])
    grad = cols_dot(three_ref[...], down_ref[...])
    square = gate * gate
    tanh = jnp.tanh(GELU_SCALE * (gate + GELU_CUBE * (gate * square)))
    half = 0.5 * (1.0 + tanh)
    gelu = gate * half
    slope = half + 0.5 * gate * (1.0 - tanh * tanh) * (
        GELU_SCALE * (1.0 + 3.0 * GELU_CUBE * square)
    )
    hid_ref[...] = (gelu * up).astype(BF16)
    gate_ref[...] = (grad * up * slope).astype(BF16)
    up_ref[...] = (grad * gelu).astype(BF16)


def feed(normed, w_gate, w_up, grad_three, w_down):
    length, model = normed.shape
    units = w_gate.shape[1]
    tile = 256
    column = lambda rows: pl.BlockSpec((rows, tile), lambda j: (0, j))
    whole = pl.BlockSpec((length, model), lambda j: (0, 0))
    return pl.pallas_call(
        feed_kernel,
        grid=(units // tile,),
        in_specs=[
            whole, column(model), column(model), whole,
            pl.BlockSpec((tile, model), lambda j: (j, 0)),
        ],
        out_specs=(column(length),) * 3,
        out_shape=(jax.ShapeDtypeStruct((length, units), BF16),) * 3,
        compiler_params=wide_params(1),
        cost_estimate=cost(6 * length * model * units, 6 * model * units + 6 * length * units),
    )(normed, w_gate, w_up, grad_three, w_down)


def feed_back_kernel(gate_ref, up_ref, g_ref, u_ref, out_ref):
    total = cols_dot(gate_ref[...], g_ref[...]) + cols_dot(up_ref[...], u_ref[...])
    out_ref[...] = total.astype(BF16)


def feed_back(grad_gate, grad_up, w_gate, w_up):
    length, units = grad_gate.shape
    model = w_gate.shape[0]
    tile = 512
    whole = pl.BlockSpec((length, units), lambda j: (0, 0))
    row = pl.BlockSpec((tile, units), lambda j: (j, 0))
    return pl.pallas_call(
        feed_back_kernel,
        grid=(model // tile,),
        in_specs=[whole, whole, row, row],
        out_specs=pl.BlockSpec((length, tile), lambda j: (0, j)),
        out_shape=jax.ShapeDtypeStruct((length, model), BF16),
        compiler_params=wide_params(1),
        cost_estimate=cost(4 * length * model * units, 4 * model * units + 4 * length * units),
    )(grad_gate, grad_up, w_gate, w_up)


def finish_kernel(turned, *refs):
    for turn, source, target in zip(turned, refs[: len(turned)], refs[len(turned) :]):
        target[...] = source[...].T if turn else source[...]


def finish(arrays, turned):
    steps = 2
    in_specs, out_specs, shapes = [], [], []
    for arr, turn in zip(arrays, turned):
        rows, width = arr.shape
        cut = rows // steps if rows // steps >= 128 else rows
        at = (lambda i: i) if cut < rows else (lambda i: 0)
        in_specs.append(pl.BlockSpec((cut, width), lambda i, at=at: (at(i), 0)))
        if turn:
            out_specs.append(pl.BlockSpec((width, cut), lambda i, at=at: (0, at(i))))
            shapes.append(jax.ShapeDtypeStruct((width, rows), F32))
        else:
            out_specs.append(pl.BlockSpec((cut, width), lambda i, at=at: (at(i), 0)))
            shapes.append(jax.ShapeDtypeStruct((rows, width), F32))
    return pl.pallas_call(
        functools.partial(finish_kernel, turned),
        grid=(steps,),
        in_specs=in_specs,
        out_specs=out_specs,
        out_shape=shapes,
        compiler_params=wide_params(1, 60),
        cost_estimate=cost(0, 8 * sum(a.size for a in arrays)),
    )(*arrays)


CHUNKS = 4


def boundary_kernel(mode, jobs, early, partial, rows, kept, gain, *refs):
    refs = list(refs)
    take = lambda size: [refs.pop(0) for unused in range(size)]
    [gains] = take(1) if mode == "last" else [None]
    wanted, along = take(jobs), take(early)
    [sums] = take(1) if mode != "first" else [None]
    [gathered] = take(1) if mode not in ("last", "sum") else [None]
    [gain_out] = take(1) if mode in ("backward", "last") else [None]
    low_out, high_out, along_out = take(jobs), take(jobs), take(early)
    from_core, far_sum, from_chip, whole = take(4)
    low, high, from_lane = take(jobs), take(jobs), take(early)
    sends, gots = take(2)
    if jobs:
        send_jobs, got_jobs = take(2)
    if early:
        send_along, got_along = take(2)
    if mode == "last":
        others, send_gains, got_gains = take(3)
    dp, mp = lax.axis_index("dp"), lax.axis_index("mp")
    core = (dp, mp + 1 - 2 * (mp % 2))
    chip = (dp, (mp + 2) % 4)
    mesh_id = pl.DeviceIdType.MESH
    step = rows.shape[0]
    size = step // CHUNKS
    barrier = pltpu.get_barrier_semaphore()
    beside = (dp + 1 - 2 * (dp % 2), mp)
    lane = dp // 2
    next_lane = ((lane + 1 - 2 * (lane % 2)) * 2 + dp % 2, mp)
    near = (core, chip, beside) if jobs else (core, chip)
    greeted = near + ((next_lane,) if early else ())
    for device in greeted:
        pl.semaphore_signal(barrier, inc=1, device_id=device, device_id_type=mesh_id)
    pl.semaphore_wait(barrier, len(greeted))

    def along_copy(k):
        return pltpu.make_async_remote_copy(
            src_ref=along[k], dst_ref=from_lane[k], send_sem=send_along.at[k],
            recv_sem=got_along.at[k], device_id=next_lane, device_id_type=mesh_id,
        )

    for k in range(early):
        along_copy(k).start()

    def job(hop, k):
        source, target = ((wanted, low), (low, high))[hop]
        return pltpu.make_async_remote_copy(
            src_ref=source[k], dst_ref=target[k], send_sem=send_jobs.at[hop, k],
            recv_sem=got_jobs.at[hop, k], device_id=(beside, core)[hop], device_id_type=mesh_id,
        )

    for k in range(jobs):
        job(0, k).start()

    def copy(kind, c, source, target, device):
        return pltpu.make_async_remote_copy(
            src_ref=source, dst_ref=target, send_sem=sends.at[kind, c], recv_sem=gots.at[kind, c],
            device_id=device, device_id_type=mesh_id,
        )

    def part(block, c):
        return pl.ds(block * step + c * size, size)

    def core_sum(block, c):
        return copy(
            block, c, partial.at[part(2 + block, c)], from_core.at[part(block, c)], core
        )

    def chip_sum(c):
        return copy(2, c, far_sum.at[part(0, c)], from_chip.at[part(0, c)], chip)

    def chip_row(c):
        return copy(3, c, whole.at[part(0, c)], whole.at[part(1, c)], chip)

    def core_row(block, c):
        return copy(
            4 + block, c, whole.at[part(block, c)], whole.at[part(2 + block, c)], core
        )

    every = range(CHUNKS)
    wide = lambda value: value.astype(F32)
    if mode != "first":
        for block in (1, 0):
            for c in every:
                core_sum(block, c).start()
        for c in every:
            core_sum(1, c).wait_recv()
            total = wide(partial[part(1, c)]) + wide(from_core[part(1, c)])
            far_sum[part(0, c)] = total.astype(BF16)
            chip_sum(c).start()
    if gain_out is not None:
        gain_out[...] = jnp.zeros_like(gain_out) if mode != "last" else gains[...]
    for c in every:
        here = part(0, c)
        if mode == "first":
            value = wide(rows[here])
        else:
            core_sum(0, c).wait_recv()
            chip_sum(c).wait_recv()
            total = wide(partial[here]) + wide(from_core[here]) + wide(from_chip[here])
            if mode in ("forward", "sum"):
                value = wide(rows[here]) + total
                sums[here] = value
            else:
                old = kept[here]
                inv = inverse_rms(old)
                weighted = gain[...] * total
                inner = jnp.mean(old * weighted, axis=-1, keepdims=True)
                value = wide(rows[here]) + inv * weighted - old * (inv * inv * inv) * inner
                gain_out[0:1] += jnp.sum(total * old * inv, axis=0, keepdims=True)
                sums[here] = value
        if gathered is not None:
            if mode != "backward":
                value = value * inverse_rms(value) * gain[...]
            whole[here] = value.astype(BF16)
            chip_row(c).start()
            core_row(0, c).start()
    if gathered is not None:
        for c in every:
            chip_row(c).wait_recv()
            core_row(1, c).start()
        for c in every:
            for block in range(2):
                core_row(block, c).wait_recv()
        gathered[...] = whole[...]
    if mode == "last":
        for k, device in enumerate(near):
            others[0] = gain_out[...]
            hop = pltpu.make_async_remote_copy(
                src_ref=others.at[0], dst_ref=others.at[k + 1], send_sem=send_gains.at[k],
                recv_sem=got_gains.at[k], device_id=device, device_id_type=mesh_id,
            )
            hop.start()
            hop.wait()
            gain_out[...] += others[k + 1]
    for k in range(jobs):
        job(0, k).wait_recv()
        job(1, k).start()
        low_out[k][...] = low[k][...]
    for k in range(jobs):
        job(0, k).wait_send()
        job(1, k).wait_recv()
        high_out[k][...] = high[k][...]
        job(1, k).wait_send()
    for k in range(early):
        along_copy(k).wait()
        along_out[k][...] = from_lane[k][...]
    for c in every:
        if mode != "first":
            core_sum(0, c).wait_send()
            core_sum(1, c).wait_send()
            chip_sum(c).wait_send()
        if gathered is not None:
            chip_row(c).wait_send()
            core_row(0, c).wait_send()
            core_row(1, c).wait_send()


def boundary(mode, number, partial, rows, kept, gain, wanted=(), gains=None, along=()):
    step, width = rows.shape
    vmem = pl.BlockSpec(memory_space=pltpu.VMEM)
    shapes = []
    if mode != "first":
        shapes.append(jax.ShapeDtypeStruct((step, width), F32))
    if mode not in ("last", "sum"):
        shapes.append(jax.ShapeDtypeStruct((4 * step, width), BF16))
    if mode in ("backward", "last"):
        shapes.append(jax.ShapeDtypeStruct((1 if mode == "backward" else 8, width), F32))
    given = [gains] if mode == "last" else []
    jobs, early = len(wanted), len(along)
    moved = list(wanted) * 2 + list(along)
    shapes += [jax.ShapeDtypeStruct(w.shape, BF16) for w in moved]
    scratch = [pltpu.VMEM(w.shape, BF16) for w in moved]
    outs = pl.pallas_call(
        functools.partial(boundary_kernel, mode, jobs, early),
        in_specs=[vmem] * (4 + len(given) + jobs + early),
        out_specs=[vmem] * len(shapes),
        out_shape=shapes,
        scratch_shapes=[
            pltpu.VMEM((2 * step, width), BF16),
            pltpu.VMEM((step, width), BF16),
            pltpu.VMEM((step, width), BF16),
            pltpu.VMEM((4 * step, width), BF16),
        ]
        + scratch
        + [pltpu.SemaphoreType.DMA((6, CHUNKS))] * 2
        + ([pltpu.SemaphoreType.DMA((2, jobs))] * 2 if jobs else [])
        + ([pltpu.SemaphoreType.DMA((early,))] * 2 if early else [])
        + (
            [pltpu.VMEM((4, 8, width), F32)] + [pltpu.SemaphoreType.DMA((3,))] * 2
            if mode == "last"
            else []
        ),
        compiler_params=pltpu.CompilerParams(
            collective_id=number, has_side_effects=True, vmem_limit_bytes=20 * 2**20
        ),
        cost_estimate=cost(10 * step * width, 60 * 2**20),
    )(partial, rows, kept, gain, *given, *wanted, *along)
    if not jobs:
        return outs
    outs = list(outs)
    plain = len(outs) - 2 * jobs - early
    halves = list(zip(outs[plain : plain + jobs], outs[plain + jobs :]))
    return outs[:plain] + halves + outs[plain + 2 * jobs :]


def layer(n_dp, n_mp):
    lanes = n_dp // 2
    paired = n_dp == 8

    def swap(value, axis, size, bit):
        return lax.ppermute(value, axis, [(i, i ^ bit) for i in range(size)])

    def core(value):
        return swap(value, "mp", n_mp, 1)

    def chip(value):
        return swap(value, "mp", n_mp, 2)

    def beside(value):
        return swap(value, "dp", n_dp, 1)

    def gather(mine):
        far = chip(mine)
        return assemble([mine, far, core(mine), core(far)])

    def gather_after(mine, after):
        return gather(tie(mine, after))

    def scatter_rows(partial):
        step = partial.shape[0] // 4
        block = [partial[k * step : (k + 1) * step] for k in range(4)]
        far = (block[1].astype(F32) + core(block[3]).astype(F32)).astype(BF16)
        far_in = chip(far)
        return block[0].astype(F32) + core(block[2]).astype(F32) + far_in.astype(F32)

    def line_place():
        z = lax.axis_index("dp") // 2
        number = lambda value: jnp.asarray(value).astype(jnp.int32)
        return lax.axis_index("dp") % 2, number(z >= 2), number((z == 1) | (z == 2))

    def outer_swap(value):
        return swap(value, "dp", n_dp, 2)

    def inner_swap(value):
        pairs = []
        for d in range(n_dp):
            for m in range(n_mp):
                inner = d // 2 in (1, 2)
                to = (d ^ 6) * n_mp + m if inner else d * n_mp + (m ^ 1)
                pairs.append((d * n_mp + m, to))
        return lax.ppermute(value, ("dp", "mp"), pairs)

    def lane_columns(parity):
        flip = line_place()[1]
        k = jnp.arange(4, dtype=jnp.int32)
        return 2 * (k + flip * (3 - 2 * k)) + parity

    def wanted_of(value, half=None):
        rows = value.shape[0] // 2
        if half is not None:
            value = pick_rows(jnp.stack([half]).astype(jnp.int32), value, rows)
        x = line_place()[0]
        return pick_columns(lane_columns(1 - x), value, rows, value.shape[1] // n_dp)

    def shards(
        tokens, norm_gains, w_query, w_key, w_value, w_out, c_query, c_key, c_value, c_out,
        patch_proj, w_gate, w_up, w_down, patches, segment_ids, image_index, cotangent,
    ):
        length = segment_ids.shape[1]
        model = tokens.shape[2]
        patch_rows = patches.shape[0] * patches.shape[1]
        m = lax.axis_index("mp")
        order = [m, m ^ 2, m ^ 1, m ^ 3]

        def blocks(arr, axis=0):
            step = arr.shape[axis] // 4
            return jnp.concatenate(
                [lax.dynamic_slice_in_dim(arr, k * step, step, axis) for k in order], axis=axis
            )

        places = blocks(jnp.arange(length, dtype=jnp.int32))
        segment_row = blocks(segment_ids[0])
        slots = jnp.arange(SEGS, dtype=jnp.int32)
        token_image = jnp.sum(
            jnp.where(segment_row[:, None] == slots, image_index[0][None, :], 0), axis=-1
        )
        patch_image = jnp.arange(patch_rows, dtype=jnp.int32) // patches.shape[1]

        far_of = beside if paired else (lambda value: value)
        core_bit = m % 2

        def exchange(*values):
            return [wanted_of(*value) for value in values] if paired else []

        def split(value, halves):
            return (value, *halves) if paired else (value,)

        def split_now(value):
            if not paired:
                return (value,)
            wanted = wanted_of(value)
            low = beside(wanted)
            return value, low, core(low)

        self_rows = jnp.stack([segment_row, places], axis=1)
        self_cols = self_rows.T
        cross_rows, cross_cols = token_image[:, None], patch_image[None, :]
        residual = tokens[0].astype(F32)
        gain_rows = [norm_gains[k : k + 1] for k in range(3)]
        nothing = jnp.zeros((16, 128), BF16)
        none = [None] * 4
        [normed_one] = boundary("first", 1, nothing, tokens[0], nothing, gain_rows[0])
        patch_own = patches.reshape(patch_rows, patches.shape[2])
        projected = matmul(patch_own, patch_proj).astype(BF16)
        queries = matmul(normed_one, w_query).astype(BF16)
        key_rows = matmul(normed_one, w_key).astype(BF16)
        value_rows = matmul(normed_one, w_value).astype(BF16)
        self_mixed = attend(queries, key_rows, value_rows, self_rows, self_cols, True)
        self_far = far_of(self_mixed)
        grad_three = gather_after(cotangent[0], normed_one)
        split_one = split_now(normed_one)
        self_mixed = tie(self_mixed, (grad_three, split_one))
        partial = matmul(self_mixed, w_out).astype(BF16)
        after_self, normed_two, *halves = boundary(
            "forward", 2, partial, tokens[0], nothing, gain_rows[1], exchange((projected, core_bit))
        )
        patch_low, patch_high = halves[0] if paired else (None, None)
        normed_two = tie(normed_two, self_far)
        cross_keys = matmul(projected, c_key).astype(BF16)
        cross_values = matmul(projected, c_value).astype(BF16)
        cross_queries = matmul(normed_two, c_query).astype(BF16)
        cross_mixed = attend(
            cross_queries, cross_keys, cross_values, cross_rows, cross_cols, False
        )
        partial = matmul(cross_mixed, c_out).astype(BF16)
        after_cross, normed_three, *halves = boundary(
            "forward", 3, partial, after_self, nothing, gain_rows[2],
            exchange((grad_three,), (normed_two,)),
        )
        split_cotangent, split_two = map(split, (grad_three, normed_two), halves or none)
        if paired:
            wanted = wanted_of(normed_three)
            low_three = beside(wanted)
            split_three = normed_three, low_three, core(low_three)
            normed_three = tie(normed_three, wanted)
        else:
            split_three, low_three = (normed_three,), normed_three
        hidden, grad_gate, grad_up = feed(normed_three, w_gate, w_up, grad_three, w_down)

        results, turned = {}, {}

        def line(name, split, grad, grad_far, rows_first, after=(), pick=None):
            turned[name] = not rows_first
            if not paired:
                grad = grad if pick is None else grad[pick]
                partial = product("td,te->de", split[0], grad).astype(BF16)
                total = lax.psum_scatter(partial, "dp", scatter_dimension=0, tiled=True)
                results[name] = total.astype(F32)
                return ()
            results[name] = pair_grad(
                lane_columns(line_place()[0]), *split, grad, grad_far, after, pick
            )
            return results[name]

        def line_out(name):
            return outer_swap(results[name][1]) if paired else None

        def line_merge(name, incoming, after):
            if paired:
                first, rest = results[name]
                results[name] = first, merge(rest, incoming, after)

        def line_across(name):
            if paired:
                inner = line_place()[2]
                first, rest = results[name]
                results[name] = cross_add(inner.reshape(1), first, rest, inner_swap(rest[1:]))

        hidden_far = far_of(tie(hidden, low_three))
        partial = feed_back(grad_gate, grad_up, w_gate, w_up)
        gate_far, up_far = [far_of(v) for v in tie((grad_gate, grad_up), partial)]
        partial_out = matmul(tie(hidden, partial), w_down).astype(BF16)
        [output] = boundary("sum", 7, partial_out, after_cross, nothing, gain_rows[0])
        sent = line("down", split_cotangent, hidden, hidden_far, False, (output,))
        incoming_down = line_out("down")
        grad_rows, grad_two, gain_three = boundary(
            "backward", 4, tie(partial, sent), cotangent[0], after_cross, gain_rows[2]
        )
        sent = line("gate", split_three, grad_gate, gate_far, True, (grad_two,))
        incoming_gate = line_out("gate")
        grad_two = tie(grad_two, sent)

        grad_mixed = product("sd,ed->se", grad_two, c_out).astype(BF16)
        grad_cq, grad_ckv = attend_back(
            cross_queries, cross_keys, cross_values, cross_rows, cross_cols, grad_mixed, False
        )
        cq_far, ckv_far = far_of(grad_cq), far_of(grad_ckv)
        partial = product("se,de->sd", grad_cq, c_query).astype(BF16)
        sent = line("up", split_three, grad_up, up_far, True, (partial,))
        incoming_up = line_out("up")
        line_merge("down", incoming_down, (partial,))
        grad_rows, grad_one, gain_two = boundary(
            "backward", 5, tie(partial, (sent, results["down"])), grad_rows, after_self, gain_rows[1]
        )
        line_across("down")

        width = model // (n_dp * n_mp)

        def projected_block(k):
            def rows_of(weight):
                cut = weight.reshape(n_dp, n_mp, width, weight.shape[1])
                return lax.dynamic_index_in_dim(cut, k, 1, keepdims=False).reshape(
                    n_dp * width, weight.shape[1]
                )

            return (
                cols_dot(grad_ckv_late[0], rows_of(c_key))
                + cols_dot(grad_ckv_late[1], rows_of(c_value))
            ).astype(
                BF16
            )

        grad_ckv_late = tie(grad_ckv, grad_one)
        block = [projected_block(k) for k in order]
        far_core = core(block[3])

        grad_mixed = product(
            "sd,ed->se", tie(grad_one, (block[1], block[3])), w_out
        ).astype(BF16)
        grad_sq, grad_sk, grad_sv = attend_back(
            queries, key_rows, value_rows, self_rows, self_cols, grad_mixed, True
        )
        far = (block[1].astype(F32) + far_core.astype(F32)).astype(BF16)
        grad_sq, grad_sk, grad_sv = tie((grad_sq, grad_sk, grad_sv), far)
        far_in = chip(far)
        near = (block[0].astype(F32) + core(block[2]).astype(F32)).astype(BF16)
        partial = (
            product("se,de->sd", grad_sq, w_query)
            + product("se,de->sd", grad_sk, w_key)
            + product("se,de->sd", grad_sv, w_value)
        ).astype(BF16)
        line_merge("gate", incoming_gate, (partial,))
        line("c_query", split_two, grad_cq, cq_far, True, (partial,))
        split_patch = (projected,)
        if paired:
            swapped = core_bit == 1
            split_patch = (
                projected,
                jnp.where(swapped, patch_high, patch_low),
                jnp.where(swapped, patch_low, patch_high),
            )
        sent = line("c_key", split_patch, grad_ckv, ckv_far, True, (partial,), 0)
        gains = jnp.pad(jnp.concatenate([gain_two, gain_three], axis=0), ((1, 5), (0, 0)))
        along = [results["c_query"][1], results["c_key"][1]] if paired else []
        grad_rows, gains_near, *halves = boundary(
            "last", 6, tie(partial, (sent, far, near, results["gate"], results["down"])), grad_rows,
            residual, gain_rows[0], exchange((grad_two,), (grad_one,)), gains, along,
        )
        if paired:
            line_merge("c_query", halves[2], ())
            line_merge("c_key", halves[3], ())
        mixed_far = far_of(tie(cross_mixed, grad_rows))
        line_across("gate")
        split_grad_two, split_grad_one = map(split, (grad_two, grad_one), halves[:2] or none)
        grad_projected = (near.astype(F32) + far_in.astype(F32)).astype(BF16)
        patch_partial = rows_dot(grad_projected, patch_own).astype(BF16)
        x, flip, unused = line_place()
        patch_parts = patch_partial.reshape(n_dp // 2, 2, width, patches.shape[2])
        patch_sent = lax.dynamic_index_in_dim(patch_parts, 1 - x, 1, keepdims=False)
        line("c_value", split_patch, grad_ckv, ckv_far, True, (grad_rows,), 1)
        line("c_out", split_grad_two, cross_mixed, mixed_far, False, (grad_rows,))
        line("w_out", split_grad_one, self_mixed, self_far, False, (grad_rows,))
        line_merge("up", incoming_up, (grad_rows,))
        if paired:
            patch_kept = lax.dynamic_index_in_dim(patch_parts, x, 1, keepdims=False)
            patch_kept, patch_sent = [
                jnp.where(flip == 1, v.astype(F32)[::-1], v.astype(F32)).astype(BF16)
                for v in (patch_kept, patch_sent)
            ]
            mine = lax.dynamic_index_in_dim(
                gains_near[:3].reshape(3, 4, 2, n_mp, width), x, 2, keepdims=False
            )
            mine = lax.dynamic_index_in_dim(mine, m, 2, keepdims=False).transpose(1, 0, 2)
            mine = jnp.where(flip == 1, mine[::-1], mine)
            mine = jnp.pad(mine, ((0, 0), (0, 29), (0, 128 - width))).astype(BF16)
            results["gains"] = mine[:1], mine[1:]
            early, late = ["down", "gate"], ["c_value", "w_out", "c_out"]
            merged = ["up", "c_query", "c_key"]
            late.append("gains")
            names = early + merged + late + ["w_query", "w_key", "w_value", "patch"]
            sums = line_sums(
                *[[results[n] for n in group] for group in (early, merged, late)],
                [grad_sq, grad_sk, grad_sv], *split_one, patch_kept, patch_sent,
            )
            results.update(zip(names, sums))
        else:
            results["patch"] = lax.psum_scatter(
                patch_partial, "dp", scatter_dimension=0, tiled=True
            ).astype(F32)
            line("w_query", split_one, grad_sq, grad_sq, True)
            line("w_key", split_one, grad_sk, grad_sk, True)
            line("w_value", split_one, grad_sv, grad_sv, True)
        turned["patch"] = True
        results["tokens"], turned["patch"] = grad_rows, False
        names = [n for n in results if n != "gains"]
        turns = tuple(bool(turned.get(n)) for n in names)
        results.update(zip(names, finish([results[n] for n in names], turns)))
        grad_rows = results["tokens"]
        patch_total = results["patch"].T
        if paired:
            gain_total = results["gains"][:3, :width]
        else:
            gain_total = lax.dynamic_index_in_dim(
                gains_near[:3].reshape(3, n_dp, n_mp, width), m, 2, keepdims=False
            )
            gain_total = lax.psum_scatter(
                gain_total.reshape(3, n_dp * width), "dp", scatter_dimension=1, tiled=True
            )
        sum_query, sum_key, sum_value = results["w_query"], results["w_key"], results["w_value"]
        sum_cquery, sum_ckey, sum_cvalue = results["c_query"], results["c_key"], results["c_value"]
        sum_out, sum_cout, sum_down = results["w_out"], results["c_out"], results["down"]
        sum_gate, sum_up = results["gate"], results["up"]
        return (
            output.astype(BF16)[None], grad_rows[None], gain_total,
            sum_query, sum_key, sum_value, sum_out,
            sum_cquery, sum_ckey, sum_cvalue, sum_cout,
            patch_total, sum_gate, sum_up, sum_down,
        )

    return shards


def solution(mesh):
    columns, rows = P(None, "mp"), P("mp", None)
    return jax.shard_map(
        layer(mesh.shape["dp"], mesh.shape["mp"]),
        mesh=mesh,
        in_specs=(
            P("dp", "mp", None), P(), columns, columns, columns, rows, columns, columns, columns,
            rows, P(), columns, columns, rows, P("dp", None, None), P("dp", None), P("dp", None),
            P("dp", "mp", None),
        ),
        out_specs=(
            P("dp", "mp", None), P("dp", "mp", None), P(None, ("dp", "mp")),
            P("dp", "mp"), P("dp", "mp"), P("dp", "mp"), P("mp", "dp"),
            P("dp", "mp"), P("dp", "mp"), P("dp", "mp"), P("mp", "dp"),
            P(None, ("dp", "mp")), P("dp", "mp"), P("dp", "mp"), P("mp", "dp"),
        ),
        check_vma=False,
    )
```
